32 devices in a mesh: groups: 2 (over x), fsdp: 4 (over y, core), tensor: 4 (over z).
Axes of the slice: x: 2, y: 2, z: 4, core: 2. Of those that a mesh axis runs over, the one named last changes fastest.
Arguments:
- tokens: bfloat16 [8192, 5120], P(('groups', 'fsdp', 'tensor')), parts along dimension 0, may hold values from -6 to 6
- w_qkv: bfloat16 [10240, 6144], P(('groups', 'fsdp', 'tensor')), parts along dimension 0, may hold values from -0.078125 to 0.078125
- norm_gain: float32 [5120], replicated, may hold values from 0.1 to 1.9
- q_gain: float32 [128], replicated, may hold values from 0.5 to 3
- k_gain: float32 [128], replicated, may hold values from 0.5 to 3
- lengths: int32 [8], P(('groups', 'fsdp')), parts along dimension 0, may hold values from 256 to 1024, as said below
Outputs:
- attended: bfloat16 [8192, 4096], P(('groups', 'fsdp'), 'tensor'), parts along dimension 0
The draws below stay inside these ranges and needn't reach their ends.
There are 2 independent parts, one for each index of `groups`. The reference program is written for one: setup_inputs(seed, part) draws one part's arguments, and reference() takes and returns one part's arrays. A program takes and returns all parts, laid end to end along the dimension named above; an argument that names none is the same for every part. Nothing has to cross between parts.
Inputs may be any that keep to these rules, and one draw needn't show every extreme that they name: `lengths`: one prompt has the full length 1024.
All inputs are finite; a program needn't handle non-finite values.
Results may differ from the reference program's by a relative error of at most 0.012.
The reference program's roundings to bfloat16 on the way (of `normed` and `probs`) count: a program that leaves them out, or rounds other values in their place, can miss the bound.
Values may be sent and summed in bfloat16 or wider, within the bound.
No kernel may reach another device: no remote copies, remote signals or barrier semaphores. Data moves between devices by JAX's collectives and lax.ppermute only.
A program may use at most 192 MiB of HBM per device.

```python
import math
import jax
import jax.numpy as jnp
from jax import lax

D = 5120
HEADS = 32
KV = 8
HD = 128
SEQ = 1024
GQ = 4
QKV_COLS = 6144
SEQS = 4
TOKENS = 4096


def draw_lengths(key, part):
    key = jax.random.fold_in(key, 11)
    values = jax.random.randint(key, (SEQS,), SEQ // 4, SEQ + 1)
    chosen = jax.random.randint(jax.random.fold_in(key, 2), (), 0, SEQS)
    return values.at[chosen].set(SEQ).astype(jnp.int32)


def steps_of(stream_key, extent, shards, least, high):
    def one(position, blocks):
        steps = jax.random.uniform(jax.random.fold_in(jax.random.fold_in(stream_key, 6), position), (blocks,), jnp.float32, least / len(shards), high / len(shards))
        return jnp.repeat(jnp.exp(steps), extent[position] // blocks).reshape((-1,) + (1,) * (len(extent) - position - 1))

    level = one(*shards[0])
    for cut in shards[1:]:
        level = level * one(*cut)
    return level


def scatter_about(stream_key, extent, width, limit, split=(), held_as=jnp.bfloat16):
    array = width * jax.random.normal(stream_key, extent, jnp.float32)
    if split:
        array = array * steps_of(stream_key, extent, split, -0.22, 0.18)
    return jnp.clip(array, -limit, limit).astype(held_as)


def setup_inputs(seed: int = 0, part: int = 0) -> dict:
    keys = jax.random.split(jax.random.key(seed), 7)
    part_splits = jax.random.split(jax.random.fold_in(keys[6], part), 7)
    return {
        "tokens": scatter_about(part_splits[0], (TOKENS, D), 1.0, 6.0, ((0, 16),)),
        "w_qkv": scatter_about(part_splits[1], (D, QKV_COLS), D ** -0.5, 0.078125, ((0, 16),)),
        "norm_gain": jnp.clip(1.0 + 0.18 * jax.random.normal(keys[2], (D,), jnp.float32), 0.1, 1.9),
        "q_gain": jnp.clip(jnp.exp(jax.random.uniform(keys[3], (HD,), jnp.float32, math.log(0.5), math.log(3.0))), 0.5, 3.0),
        "k_gain": jnp.clip(jnp.exp(jax.random.uniform(keys[4], (HD,), jnp.float32, math.log(0.5), math.log(3.0))), 0.5, 3.0),
        "lengths": draw_lengths(jax.random.fold_in(jax.random.fold_in(keys[6], part), 71), part),
    }


def head_norm(vec, gain):
    scale = lax.rsqrt(lax.optimization_barrier(jnp.mean(vec * vec, axis=-1, keepdims=True)) + 1e-06)
    return vec * scale * gain

def rotate(vec, positions):
    half = vec.shape[-1] // 2
    freqs = 1000000.0 ** (-2.0 * jnp.arange(half, dtype=jnp.float32) / vec.shape[-1])
    angle = positions.astype(jnp.float32)[:, None] * freqs[None, :]
    cosine = jnp.cos(angle)[:, None, None, :]
    sine = jnp.sin(angle)[:, None, None, :]
    first = vec[..., :half]
    second = vec[..., half:]
    return jnp.concatenate([first * cosine - second * sine, second * cosine + first * sine], axis=-1)

def attend(qkv, q_gain, k_gain, length):
    rows = qkv.shape[0]
    group = qkv.shape[2] - 2
    positions = jnp.arange(rows, dtype=jnp.int32)
    query = rotate(head_norm(qkv[:, :, :group], q_gain), positions).astype(jnp.bfloat16)
    keyed = rotate(head_norm(qkv[:, :, group:group + 1], k_gain), positions)[:, :, 0].astype(jnp.bfloat16)
    value = qkv[:, :, group + 1].astype(jnp.bfloat16)
    scores = jnp.einsum('ikgd,jkd->kgij', query.astype(jnp.float32), keyed.astype(jnp.float32)) / jnp.sqrt(jnp.float32(qkv.shape[3]))
    allowed = (positions[None, :] <= positions[:, None]) & (positions[None, :] < length)
    scores = jnp.where(allowed[None, None], scores, jnp.float32(-1e+30))
    top = lax.optimization_barrier(jnp.max(scores, axis=-1, keepdims=True))
    weights = jnp.exp(scores - top)
    probs = (weights / lax.optimization_barrier(jnp.sum(weights, axis=-1, keepdims=True))).astype(jnp.bfloat16)
    out = jnp.einsum('kgij,jkd->ikgd', probs.astype(jnp.float32), value.astype(jnp.float32))
    return out.reshape(rows, -1).astype(jnp.bfloat16)

def reference(tokens, w_qkv, norm_gain, q_gain, k_gain, lengths):

    def one(index):
        rows = lax.dynamic_slice_in_dim(tokens, index * SEQ, SEQ, 0).astype(jnp.float32)
        normed = head_norm(rows, norm_gain).astype(jnp.bfloat16)
        qkv = jnp.dot(normed, w_qkv, preferred_element_type=jnp.float32)
        qkv = qkv.reshape(SEQ, KV, GQ + 2, HD)
        return attend(qkv, q_gain, k_gain, lengths[index])
    outs = lax.map(one, jnp.arange(SEQS, dtype=jnp.int32))
    return outs.reshape(SEQS * SEQ, HEADS * HD)
```

```python
import jax
import jax.numpy as jnp
from jax import lax
from jax.sharding import PartitionSpec as P

KV = 8
HD = 128
GQ = 4


def head_norm(vec, gain):
    scale = lax.rsqrt(jnp.mean(vec * vec, axis=-1, keepdims=True) + 1e-06)
    return vec * scale * gain


def rotate(vec, positions):
    half = vec.shape[-1] // 2
    freqs = 1000000.0 ** (-2.0 * jnp.arange(half, dtype=jnp.float32) / vec.shape[-1])
    angle = positions.astype(jnp.float32)[:, None] * freqs[None, :]
    cosine = jnp.cos(angle)[:, None, None, :]
    sine = jnp.sin(angle)[:, None, None, :]
    first = vec[..., :half]
    second = vec[..., half:]
    return jnp.concatenate(
        [first * cosine - second * sine, second * cosine + first * sine], axis=-1
    )


def attend(qkv, q_gain, k_gain, length):
    rows = qkv.shape[0]
    group = qkv.shape[2] - 2
    positions = jnp.arange(rows, dtype=jnp.int32)
    query = rotate(head_norm(qkv[:, :, :group], q_gain), positions).astype(jnp.bfloat16)
    keyed = rotate(head_norm(qkv[:, :, group : group + 1], k_gain), positions)[:, :, 0].astype(
        jnp.bfloat16
    )
    value = qkv[:, :, group + 1].astype(jnp.bfloat16)
    scores = jnp.einsum(
        "ikgd,jkd->kgij", query, keyed, preferred_element_type=jnp.float32
    ) / jnp.sqrt(jnp.float32(qkv.shape[3]))
    allowed = (positions[None, :] <= positions[:, None]) & (positions[None, :] < length)
    scores = jnp.where(allowed[None, None], scores, jnp.float32(-1e30))
    top = jnp.max(scores, axis=-1, keepdims=True)
    weights = jnp.exp(scores - top)
    probs = (weights / jnp.sum(weights, axis=-1, keepdims=True)).astype(jnp.bfloat16)
    out = jnp.einsum("kgij,jkd->ikgd", probs, value, preferred_element_type=jnp.float32)
    return out.reshape(rows, -1).astype(jnp.bfloat16)


def gather_weights(w_qkv):
    tensor_count = lax.axis_size("tensor")
    fsdp_count = lax.axis_size("fsdp")
    t = lax.axis_index("tensor")
    f = lax.axis_index("fsdp")
    rows = w_qkv.shape[0]
    columns = w_qkv.shape[1] // tensor_count
    whole = jnp.zeros((fsdp_count, tensor_count, rows, columns), w_qkv.dtype)
    for shift in range(tensor_count):
        target = lax.rem(t + shift, tensor_count)
        piece = lax.dynamic_slice(w_qkv, (0, target * columns), (rows, columns))
        if shift:
            piece = lax.ppermute(
                piece,
                "tensor",
                [(i, (i + shift) % tensor_count) for i in range(tensor_count)],
            )
        source = lax.rem(t - shift + tensor_count, tensor_count)
        held = [(0, piece)]
        bit = fsdp_count // 2
        while bit:
            pairs = [(i, i ^ bit) for i in range(fsdp_count)]
            held = held + [(m ^ bit, lax.ppermute(p, "fsdp", pairs)) for m, p in held]
            bit //= 2
        for m, p in held:
            whole = lax.dynamic_update_slice(
                whole, p[None, None], (jnp.bitwise_xor(f, m), source, 0, 0)
            )
    return whole.reshape(fsdp_count * tensor_count * rows, columns)


def gather_rows(normed, chunks):
    count = lax.axis_size("tensor")
    t = lax.axis_index("tensor")
    rows, width = normed.shape
    part = rows // chunks
    right = [(i, i + 1) for i in range(count - 1)]
    left = [(i + 1, i) for i in range(count - 1)]
    whole = jnp.zeros((count, rows, width), normed.dtype)
    whole = lax.dynamic_update_slice(whole, normed[None], (t, 0, 0))
    for c in range(chunks):
        piece = normed[c * part : (c + 1) * part]
        from_left, from_right = [piece], [piece]
        for _ in range(count - 1):
            from_left.append(lax.ppermute(from_left[-1], "tensor", right))
            from_right.append(lax.ppermute(from_right[-1], "tensor", left))
        for k in range(1, count):
            block = jnp.where(t >= k, from_left[k], from_right[count - k])
            source = lax.rem(t - k + count, count)
            whole = lax.dynamic_update_slice(whole, block[None], (source, c * part, 0))
    return whole.reshape(count * rows, width)


def per_device(tokens, w_qkv, norm_gain, q_gain, k_gain, lengths):
    tensor_count = lax.axis_size("tensor")
    weight_cols = gather_weights(w_qkv)
    normed = head_norm(tokens.astype(jnp.float32), norm_gain).astype(jnp.bfloat16)
    qkv = jnp.dot(
        gather_rows(normed, 2),
        weight_cols,
        preferred_element_type=jnp.float32,
    )
    kv_local = KV // tensor_count
    qkv = qkv.reshape(qkv.shape[0], kv_local, GQ + 2, HD)
    return attend(qkv, q_gain, k_gain, lengths[0])


def solution(mesh):
    placed = (
        P(("groups", "fsdp", "tensor"), None),
        P(("groups", "fsdp", "tensor"), None),
        P(),
        P(),
        P(),
        P(("groups", "fsdp")),
    )
    return jax.shard_map(
        per_device,
        mesh=mesh,
        in_specs=placed,
        out_specs=P(("groups", "fsdp"), "tensor"),
        check_vma=False,
    )
```

```python
import jax
import jax.numpy as jnp
from jax import lax
from jax.sharding import PartitionSpec as P

KV = 8
HD = 128
GQ = 4


def head_norm(vec, gain):
    scale = lax.rsqrt(jnp.mean(vec * vec, axis=-1, keepdims=True) + 1e-06)
    return vec * scale * gain


def rotate(vec, positions):
    half = vec.shape[-1] // 2
    freqs = 1000000.0 ** (-2.0 * jnp.arange(half, dtype=jnp.float32) / vec.shape[-1])
    angle = positions.astype(jnp.float32)[:, None] * freqs[None, :]
    cosine = jnp.cos(angle)[:, None, None, :]
    sine = jnp.sin(angle)[:, None, None, :]
    first = vec[..., :half]
    second = vec[..., half:]
    return jnp.concatenate(
        [first * cosine - second * sine, second * cosine + first * sine], axis=-1
    )


def attend(qkv, q_gain, k_gain, length):
    rows = qkv.shape[0]
    group = qkv.shape[2] - 2
    positions = jnp.arange(rows, dtype=jnp.int32)
    query = rotate(head_norm(qkv[:, :, :group], q_gain), positions).astype(jnp.bfloat16)
    keyed = rotate(head_norm(qkv[:, :, group : group + 1], k_gain), positions)[:, :, 0].astype(
        jnp.bfloat16
    )
    value = qkv[:, :, group + 1].astype(jnp.bfloat16)
    scores = jnp.einsum(
        "ikgd,jkd->kgij", query, keyed, preferred_element_type=jnp.float32
    ) / jnp.sqrt(jnp.float32(qkv.shape[3]))
    allowed = (positions[None, :] <= positions[:, None]) & (positions[None, :] < length)
    scores = jnp.where(allowed[None, None], scores, jnp.float32(-1e30))
    top = jnp.max(scores, axis=-1, keepdims=True)
    weights = jnp.exp(scores - top)
    probs = (weights / jnp.sum(weights, axis=-1, keepdims=True)).astype(jnp.bfloat16)
    out = jnp.einsum("kgij,jkd->ikgd", probs, value, preferred_element_type=jnp.float32)
    return out.reshape(rows, -1).astype(jnp.bfloat16)


def gather_weights(w_qkv):
    tensor_count = lax.axis_size("tensor")
    fsdp_count = lax.axis_size("fsdp")
    local_rows = w_qkv.shape[0]
    columns = w_qkv.shape[1] // tensor_count
    moved = lax.all_to_all(w_qkv, "tensor", split_axis=1, concat_axis=0, tiled=True)
    whole = lax.all_gather(moved, "fsdp", axis=0, tiled=True)
    return whole.reshape(fsdp_count * tensor_count * local_rows, columns)


def per_device(tokens, w_qkv, norm_gain, q_gain, k_gain, lengths):
    tensor_count = lax.axis_size("tensor")
    weight_cols = gather_weights(w_qkv)
    normed = head_norm(tokens.astype(jnp.float32), norm_gain).astype(jnp.bfloat16)
    qkv = jnp.dot(
        lax.all_gather(normed, "tensor", axis=0, tiled=True),
        weight_cols,
        preferred_element_type=jnp.float32,
    )
    kv_local = KV // tensor_count
    qkv = qkv.reshape(qkv.shape[0], kv_local, GQ + 2, HD)
    return attend(qkv, q_gain, k_gain, lengths[0])


def solution(mesh):
    placed = (
        P(("groups", "fsdp", "tensor"), None),
        P(("groups", "fsdp", "tensor"), None),
        P(),
        P(),
        P(),
        P(("groups", "fsdp")),
    )
    return jax.shard_map(
        per_device,
        mesh=mesh,
        in_specs=placed,
        out_specs=P(("groups", "fsdp"), "tensor"),
        check_vma=False,
    )
```

```python
import functools
import jax
import jax.numpy as jnp
from jax import lax
from jax.experimental import pallas as pl
from jax.experimental.pallas import tpu as pltpu
from jax.sharding import PartitionSpec as P

KV = 8
HD = 128
GQ = 4
LOG2E = 1.4426950408889634
VMEM_BYTES = 52 * 1024 * 1024


def head_norm(vec, gain):
    scale = lax.rsqrt(jnp.mean(vec * vec, axis=-1, keepdims=True) + 1e-06)
    return vec * scale * gain


def angles(positions):
    half = HD // 2
    freqs = 1000000.0 ** (-2.0 * jnp.arange(half, dtype=jnp.float32) / HD)
    return positions.astype(jnp.float32)[:, None] * freqs[None, :]


def rotate(vec, positions):
    half = vec.shape[-1] // 2
    angle = angles(positions)
    cosine = jnp.cos(angle)[:, None, None, :]
    sine = jnp.sin(angle)[:, None, None, :]
    first = vec[..., :half]
    second = vec[..., half:]
    return jnp.concatenate(
        [first * cosine - second * sine, second * cosine + first * sine], axis=-1
    )


def attend(qkv, q_gain, k_gain, length):
    rows = qkv.shape[0]
    group = qkv.shape[2] - 2
    positions = jnp.arange(rows, dtype=jnp.int32)
    query = rotate(head_norm(qkv[:, :, :group], q_gain), positions).astype(jnp.bfloat16)
    keyed = rotate(head_norm(qkv[:, :, group : group + 1], k_gain), positions)[:, :, 0].astype(
        jnp.bfloat16
    )
    value = qkv[:, :, group + 1].astype(jnp.bfloat16)
    scores = jnp.einsum(
        "ikgd,jkd->kgij", query, keyed, preferred_element_type=jnp.float32
    ) / jnp.sqrt(jnp.float32(qkv.shape[3]))
    allowed = (positions[None, :] <= positions[:, None]) & (positions[None, :] < length)
    scores = jnp.where(allowed[None, None], scores, jnp.float32(-1e30))
    top = jnp.max(scores, axis=-1, keepdims=True)
    weights = jnp.exp(scores - top)
    probs = (weights / jnp.sum(weights, axis=-1, keepdims=True)).astype(jnp.bfloat16)
    out = jnp.einsum("kgij,jkd->ikgd", probs, value, preferred_element_type=jnp.float32)
    return out.reshape(rows, -1).astype(jnp.bfloat16)


def any_mesh(tokens, w_qkv, norm_gain, q_gain, k_gain, lengths):
    tensor_count = lax.axis_size("tensor")
    moved = lax.all_to_all(w_qkv, "tensor", split_axis=1, concat_axis=0, tiled=True)
    weight_cols = lax.all_gather(moved, "fsdp", axis=0, tiled=True)
    normed = head_norm(tokens.astype(jnp.float32), norm_gain).astype(jnp.bfloat16)
    qkv = jnp.dot(
        lax.all_gather(normed, "tensor", axis=0, tiled=True),
        weight_cols,
        preferred_element_type=jnp.float32,
    )
    qkv = qkv.reshape(qkv.shape[0], KV // tensor_count, GQ + 2, HD)
    return attend(qkv, q_gain, k_gain, lengths[0])


def project_kernel(blocks, tile, scal, *refs):
    rows_refs = refs[:blocks]
    pieces = refs[blocks : blocks + 16]
    cos_ref, sin_ref, gain_ref = refs[blocks + 16 : blocks + 19]
    outs = refs[blocks + 19 : 2 * blocks + 19]
    held, total, sems = refs[2 * blocks + 19 :]
    depth, columns = pieces[0].shape
    band = 4 * depth

    def copy(index):
        group, slot = divmod(index, 4)
        start = pl.multiple_of(scal[slot] * depth, 16)
        return pltpu.make_async_copy(
            pieces[index], held.at[group, pl.ds(start, depth), :], sems.at[index]
        )

    for index in range(16):
        copy(index).start()
    for group in range(4):
        for slot in range(4):
            copy(4 * group + slot).wait()
        offset = pl.multiple_of(scal[4 + group] * band, 128)
        first = 0
        for ref in rows_refs:
            rows = ref.shape[0]

            @pl.loop(0, columns // tile)
            def _(step, ref=ref, first=first, rows=rows):
                at = pl.ds(pl.multiple_of(step * tile, tile), tile)
                part = jnp.dot(
                    ref[:, pl.ds(offset, band)],
                    held[group, :, at],
                    preferred_element_type=jnp.float32,
                )
                if group:
                    part = part + total[first : first + rows, at]
                total[first : first + rows, at] = part

            first += rows
    first = 0
    for number, (ref, out) in enumerate(zip(rows_refs, outs)):
        rows = ref.shape[0]
        place = pl.ds(pl.multiple_of(scal[8 + number], 128), rows)
        cosine = cos_ref[place, :]
        sine = sin_ref[place, :]
        for head in range(columns // HD):
            kind = head % (GQ + 2)
            at = slice(head * HD, (head + 1) * HD)
            vec = total[first : first + rows, at]
            if kind <= GQ:
                scale = lax.rsqrt(jnp.mean(vec * vec, axis=-1, keepdims=True) + 1e-06)
                gain = gain_ref[0:1, :] if kind < GQ else gain_ref[1:2, :]
                vec = vec * scale * gain
                vec = vec * cosine + pltpu.roll(vec, HD // 2, 1) * sine
            out[:, at] = vec.astype(out.dtype)
        first += rows


def project(rows_list, places, pieces, scal, cos, sin, gains):
    blocks = len(rows_list)
    columns = pieces[0].shape[1]
    depth = pieces[0].shape[0]
    count = sum(r.shape[0] for r in rows_list)
    width = rows_list[0].shape[1]
    scal = jnp.concatenate([scal, jnp.stack(places)]).astype(jnp.int32)
    vmem = pl.BlockSpec(memory_space=pltpu.VMEM)
    return pl.pallas_call(
        functools.partial(project_kernel, blocks, 512),
        out_shape=[jax.ShapeDtypeStruct((r.shape[0], columns), jnp.bfloat16) for r in rows_list],
        in_specs=[pl.BlockSpec(memory_space=pltpu.SMEM)]
        + [vmem] * blocks
        + [pl.BlockSpec(memory_space=pl.ANY)] * 16
        + [vmem] * 3,
        out_specs=[vmem] * blocks,
        scratch_shapes=[
            pltpu.VMEM((4, 4 * depth, columns), jnp.bfloat16),
            pltpu.VMEM((count, columns), jnp.float32),
            pltpu.SemaphoreType.DMA((16,)),
        ],
        compiler_params=pltpu.CompilerParams(vmem_limit_bytes=VMEM_BYTES),
        cost_estimate=pl.CostEstimate(
            flops=2 * count * width * columns,
            bytes_accessed=2 * (width * columns + count * (width + columns)),
            transcendentals=0,
        ),
        name="project",
    )(scal, *rows_list, *pieces, cos, sin, gains)


def attend_kernel(parts, block, scal, *refs):
    near = refs[:parts]
    far = refs[parts : 2 * parts]
    out = refs[2 * parts]
    held, sems = refs[2 * parts + 1 :]
    middle = scal[0]
    length = scal[1]
    copies = []
    for number in range(parts):
        rows = near[number].shape[0]
        place = pl.ds(pl.multiple_of(scal[2 + number], 128), rows)
        copies.append(
            [
                pltpu.make_async_copy(ref, held.at[place, :], sems.at[number])
                for ref in (near[number], far[number])
            ]
        )
        pl.when(middle == 1)(copies[-1][0].start)
        pl.when(middle == 0)(copies[-1][1].start)
    for pair in copies:
        pair[0].wait()
    total = held.shape[0]
    heads = held.shape[1] // ((GQ + 2) * HD)
    factor = LOG2E / float(HD) ** 0.5
    row = lax.broadcasted_iota(jnp.int32, (block, block), 0)
    col = lax.broadcasted_iota(jnp.int32, (block, block), 1)
    contract = (((1,), (1,)), ((), ()))
    for group in range(heads):
        base = group * (GQ + 2) * HD
        key_at = slice(base + GQ * HD, base + (GQ + 1) * HD)
        value_at = slice(base + (GQ + 1) * HD, base + (GQ + 2) * HD)

        @pl.loop(0, GQ)
        def _(j, base=base, key_at=key_at, value_at=value_at, group=group):
            query_at = pl.ds(pl.multiple_of(base + j * HD, HD), HD)
            out_at = pl.ds(pl.multiple_of((group * GQ + j) * HD, HD), HD)
            for step in range(total // block):
                low = step * block
                high = low + block
                query = held[low:high, query_at]
                last = lax.dot_general(
                    query, held[low:high, key_at], contract, preferred_element_type=jnp.float32
                )
                last = jnp.where((col <= row) & (col + low < length), last, -1e30)
                top = jnp.max(last, axis=-1, keepdims=True)
                if step:
                    rest = lax.dot_general(
                        query, held[:low, key_at], contract, preferred_element_type=jnp.float32
                    )
                    keys = lax.broadcasted_iota(jnp.int32, (1, low), 1)
                    rest = rest + jnp.where(keys < length, 0.0, -1e30)
                    top = jnp.maximum(top, jnp.max(rest, axis=-1, keepdims=True))
                shift = top * factor
                probs = jnp.exp2(last * factor - shift)
                norm = jnp.sum(probs, axis=-1, keepdims=True)
                value = jnp.dot(
                    probs.astype(jnp.bfloat16),
                    held[low:high, value_at],
                    preferred_element_type=jnp.float32,
                )
                if step:
                    probs = jnp.exp2(rest * factor - shift)
                    norm = norm + jnp.sum(probs, axis=-1, keepdims=True)
                    value = value + jnp.dot(
                        probs.astype(jnp.bfloat16),
                        held[:low, value_at],
                        preferred_element_type=jnp.float32,
                    )
                out[low:high, out_at] = (value / norm).astype(out.dtype)


def attend_blocks(near, far, places, middle, length):
    parts = len(near)
    rows = sum(n.shape[0] for n in near)
    columns = near[0].shape[1]
    wide = columns // (GQ + 2) * GQ
    scal = jnp.stack([middle, length] + list(places)).astype(jnp.int32)
    return pl.pallas_call(
        functools.partial(attend_kernel, parts, 256),
        out_shape=jax.ShapeDtypeStruct((rows, wide), jnp.bfloat16),
        in_specs=[pl.BlockSpec(memory_space=pltpu.SMEM)]
        + [pl.BlockSpec(memory_space=pl.ANY)] * (2 * parts),
        out_specs=pl.BlockSpec(memory_space=pltpu.VMEM),
        scratch_shapes=[
            pltpu.VMEM((rows, columns), jnp.bfloat16),
            pltpu.SemaphoreType.DMA((parts,)),
        ],
        compiler_params=pltpu.CompilerParams(vmem_limit_bytes=VMEM_BYTES),
        cost_estimate=pl.CostEstimate(
            flops=4 * rows * rows * wide,
            bytes_accessed=2 * rows * (columns + wide),
            transcendentals=rows * rows * wide // HD // 2,
        ),
        name="attend",
    )(scal, *near, *far)


def four_planes(tokens, w_qkv, norm_gain, q_gain, k_gain, lengths):
    t = lax.axis_index("tensor")
    f = lax.axis_index("fsdp")
    rows = tokens.shape[0]
    columns = w_qkv.shape[1] // 4
    side = t // 2
    end = 3 * side
    mid = 1 + side
    far_end = 3 * (1 - side)
    far_mid = 2 - side

    def slab(block):
        return lax.dynamic_slice(w_qkv, (0, block * columns), (w_qkv.shape[0], columns))

    def across(x, pairs):
        return lax.ppermute(x, "tensor", pairs)

    def beside(x, bit):
        return lax.ppermute(x, "fsdp", [(i, i ^ bit) for i in range(4)])

    inward = [(0, 1), (3, 2)]
    swap = [(1, 2), (2, 1)]
    far = [(0, 2), (3, 1)]
    outward = [(1, 0), (2, 3)]

    def collect(same, other):
        mine = [same, across(same, inward), across(other, swap), across(other, far)]
        over = [beside(x, 2) for x in mine]
        return mine + over + [beside(x, 1) for x in mine] + [beside(x, 1) for x in over]

    end_pieces = collect(slab(end), slab(far_end))
    mid_pieces = collect(slab(mid), slab(far_mid))
    scal = jnp.stack([mid, end, far_mid, far_end] + [jnp.bitwise_xor(f, m) for m in (0, 2, 1, 3)])

    normed = head_norm(tokens.astype(jnp.float32), norm_gain).astype(jnp.bfloat16)
    half = rows // 2
    near_rows = [across(normed[:half], inward), across(normed[half:], inward)]
    swap_rows = across(normed, swap)
    far_rows = [across(x, swap) for x in near_rows]

    positions = jnp.arange(4 * rows, dtype=jnp.int32)
    angle = angles(positions)
    cos = jnp.concatenate([jnp.cos(angle)] * 2, axis=1)
    sin = jnp.concatenate([-jnp.sin(angle), jnp.sin(angle)], axis=1)
    gains = jnp.stack([q_gain, k_gain])

    blocks = [normed, swap_rows, near_rows[0], near_rows[1], far_rows[0], far_rows[1]]
    places = [
        mid * rows,
        far_mid * rows,
        end * rows,
        end * rows + half,
        far_end * rows,
        far_end * rows + half,
    ]

    def run(picked, pieces):
        return project(
            [blocks[i] for i in picked], [places[i] for i in picked], pieces, scal, cos, sin, gains
        )

    sent = []
    for picked in ([0], [1], [2, 3], [4], [5]):
        sent += [across(x, outward) for x in run(picked, end_pieces)]
    near = []
    for picked in ([0, 1, 2, 3], [4], [5]):
        near += run(picked, mid_pieces)
    middle = jnp.where((t == 1) | (t == 2), 1, 0)
    return attend_blocks(near, sent, places, middle, lengths[0])


def solution(mesh):
    placed = (
        P(("groups", "fsdp", "tensor"), None),
        P(("groups", "fsdp", "tensor"), None),
        P(),
        P(),
        P(),
        P(("groups", "fsdp")),
    )
    sizes = dict(mesh.shape)
    body = four_planes if sizes["tensor"] == 4 and sizes["fsdp"] == 4 else any_mesh
    return jax.shard_map(
        body,
        mesh=mesh,
        in_specs=placed,
        out_specs=P(("groups", "fsdp"), "tensor"),
        check_vma=False,
    )
```

```python
import functools
import jax
import jax.numpy as jnp
from jax import lax
from jax.experimental import pallas as pl
from jax.experimental.pallas import tpu as pltpu
from jax.sharding import PartitionSpec as P

KV = 8
HD = 128
GQ = 4
LOG2E = 1.4426950408889634
VMEM_BYTES = 52 * 1024 * 1024


def head_norm(vec, gain):
    scale = lax.rsqrt(jnp.mean(vec * vec, axis=-1, keepdims=True) + 1e-06)
    return vec * scale * gain


def angles(positions):
    half = HD // 2
    freqs = 1000000.0 ** (-2.0 * jnp.arange(half, dtype=jnp.float32) / HD)
    return positions.astype(jnp.float32)[:, None] * freqs[None, :]


def rotate(vec, positions):
    half = vec.shape[-1] // 2
    angle = angles(positions)
    cosine = jnp.cos(angle)[:, None, None, :]
    sine = jnp.sin(angle)[:, None, None, :]
    first = vec[..., :half]
    second = vec[..., half:]
    return jnp.concatenate(
        [first * cosine - second * sine, second * cosine + first * sine], axis=-1
    )


def attend(qkv, q_gain, k_gain, length):
    rows = qkv.shape[0]
    group = qkv.shape[2] - 2
    positions = jnp.arange(rows, dtype=jnp.int32)
    query = rotate(head_norm(qkv[:, :, :group], q_gain), positions).astype(jnp.bfloat16)
    keyed = rotate(head_norm(qkv[:, :, group : group + 1], k_gain), positions)[:, :, 0].astype(
        jnp.bfloat16
    )
    value = qkv[:, :, group + 1].astype(jnp.bfloat16)
    scores = jnp.einsum(
        "ikgd,jkd->kgij", query, keyed, preferred_element_type=jnp.float32
    ) / jnp.sqrt(jnp.float32(qkv.shape[3]))
    allowed = (positions[None, :] <= positions[:, None]) & (positions[None, :] < length)
    scores = jnp.where(allowed[None, None], scores, jnp.float32(-1e30))
    top = jnp.max(scores, axis=-1, keepdims=True)
    weights = jnp.exp(scores - top)
    probs = (weights / jnp.sum(weights, axis=-1, keepdims=True)).astype(jnp.bfloat16)
    out = jnp.einsum("kgij,jkd->ikgd", probs, value, preferred_element_type=jnp.float32)
    return out.reshape(rows, -1).astype(jnp.bfloat16)


def any_mesh(tokens, w_qkv, norm_gain, q_gain, k_gain, lengths):
    tensor_count = lax.axis_size("tensor")
    moved = lax.all_to_all(w_qkv, "tensor", split_axis=1, concat_axis=0, tiled=True)
    weight_cols = lax.all_gather(moved, "fsdp", axis=0, tiled=True)
    normed = head_norm(tokens.astype(jnp.float32), norm_gain).astype(jnp.bfloat16)
    qkv = jnp.dot(
        lax.all_gather(normed, "tensor", axis=0, tiled=True),
        weight_cols,
        preferred_element_type=jnp.float32,
    )
    qkv = qkv.reshape(qkv.shape[0], KV // tensor_count, GQ + 2, HD)
    return attend(qkv, q_gain, k_gain, lengths[0])


def project_kernel(blocks, bases, tile, scal, *refs):
    rows_refs = refs[:blocks]
    pieces = refs[blocks : blocks + 16]
    cos_ref, sin_ref, gain_ref = refs[blocks + 16 : blocks + 19]
    outs = refs[blocks + 19 : 2 * blocks + 19]
    taken, held, row_sems, sems = refs[2 * blocks + 19 :]
    depth = pieces[0].shape[0]
    columns = outs[0].shape[1]
    steps = columns // tile

    def copies(step):
        made = []
        for index in range(16):
            start = pl.multiple_of((scal[4 + index // 4] * 4 + scal[index % 4]) * depth, 16)
            low = bases[index] + step * tile
            made.append(
                pltpu.make_async_copy(
                    pieces[index].at[:, low : low + tile],
                    held.at[step % 2, pl.ds(start, depth), :],
                    sems.at[step % 2, index],
                )
            )
        return made

    row_copies = []
    first = 0
    for number, ref in enumerate(rows_refs):
        rows = ref.shape[0]
        row_copies.append(
            pltpu.make_async_copy(ref, taken.at[first : first + rows, :], row_sems.at[number])
        )
        first += rows
    for copy in copies(0) + row_copies:
        copy.start()
    for step in range(steps):
        if step + 1 < steps:
            for copy in copies(step + 1):
                copy.start()
        if step == 0:
            for copy in row_copies:
                copy.wait()
        for copy in copies(step):
            copy.wait()
        total = jnp.dot(taken[...], held[step % 2], preferred_element_type=jnp.float32)
        first = 0
        for number, out in enumerate(outs):
            rows = out.shape[0]
            place = pl.ds(pl.multiple_of(scal[8 + number], 128), rows)
            cosine = cos_ref[place, :]
            sine = sin_ref[place, :]
            for head in range(tile // HD):
                kind = (step * (tile // HD) + head) % (GQ + 2)
                vec = total[first : first + rows, head * HD : (head + 1) * HD]
                if kind <= GQ:
                    scale = lax.rsqrt(jnp.mean(vec * vec, axis=-1, keepdims=True) + 1e-06)
                    gain = gain_ref[0:1, :] if kind < GQ else gain_ref[1:2, :]
                    vec = vec * scale * gain
                    vec = vec * cosine + pltpu.roll(vec, HD // 2, 1) * sine
                at = step * tile + head * HD
                out[:, at : at + HD] = vec.astype(out.dtype)
            first += rows


def project(rows_list, places, pieces, scal, cos, sin, gains):
    blocks = len(rows_list)
    arrays = [p for p, _ in pieces]
    bases = [base for _, base in pieces]
    columns = min(p.shape[1] for p in arrays)
    depth = arrays[0].shape[0]
    tile = columns // 3
    count = sum(r.shape[0] for r in rows_list)
    width = rows_list[0].shape[1]
    scal = jnp.concatenate([scal, jnp.stack(places)]).astype(jnp.int32)
    vmem = pl.BlockSpec(memory_space=pltpu.VMEM)
    hbm = pl.BlockSpec(memory_space=pl.ANY)
    return pl.pallas_call(
        functools.partial(project_kernel, blocks, bases, tile),
        out_shape=[jax.ShapeDtypeStruct((r.shape[0], columns), jnp.bfloat16) for r in rows_list],
        in_specs=[pl.BlockSpec(memory_space=pltpu.SMEM)]
        + [hbm] * blocks
        + [hbm] * 16
        + [vmem] * 3,
        out_specs=[vmem] * blocks,
        scratch_shapes=[
            pltpu.VMEM((count, width), jnp.bfloat16),
            pltpu.VMEM((2, width, tile), jnp.bfloat16),
            pltpu.SemaphoreType.DMA((blocks,)),
            pltpu.SemaphoreType.DMA((2, 16)),
        ],
        compiler_params=pltpu.CompilerParams(vmem_limit_bytes=VMEM_BYTES),
        cost_estimate=pl.CostEstimate(
            flops=2 * count * width * columns,
            bytes_accessed=2 * (width * columns + count * (width + columns)),
            transcendentals=0,
        ),
        name="project",
    )(scal, *rows_list, *arrays, cos, sin, gains)


def attend_kernel(parts, block, scal, *refs):
    near = refs[:parts]
    far = refs[parts : 2 * parts]
    out = refs[2 * parts]
    held, sems = refs[2 * parts + 1 :]
    middle = scal[0]
    length = scal[1]
    copies = []
    for number in range(parts):
        rows = near[number].shape[0]
        place = pl.ds(pl.multiple_of(scal[2 + number], 128), rows)
        copies.append(
            [
                pltpu.make_async_copy(ref, held.at[place, :], sems.at[number])
                for ref in (near[number], far[number])
            ]
        )
        pl.when(middle == 1)(copies[-1][0].start)
        pl.when(middle == 0)(copies[-1][1].start)
    for pair in copies:
        pair[0].wait()
    total = held.shape[0]
    heads = held.shape[1] // ((GQ + 2) * HD)
    factor = LOG2E / float(HD) ** 0.5
    row = lax.broadcasted_iota(jnp.int32, (block, block), 0)
    col = lax.broadcasted_iota(jnp.int32, (block, block), 1)
    contract = (((1,), (1,)), ((), ()))
    for group in range(heads):
        base = group * (GQ + 2) * HD
        key_at = slice(base + GQ * HD, base + (GQ + 1) * HD)
        value_at = slice(base + (GQ + 1) * HD, base + (GQ + 2) * HD)

        @pl.loop(0, GQ)
        def _(j, base=base, key_at=key_at, value_at=value_at, group=group):
            query_at = pl.ds(pl.multiple_of(base + j * HD, HD), HD)
            out_at = pl.ds(pl.multiple_of((group * GQ + j) * HD, HD), HD)
            for step in range(total // block):
                low = step * block
                high = low + block
                query = held[low:high, query_at]
                last = lax.dot_general(
                    query, held[low:high, key_at], contract, preferred_element_type=jnp.float32
                )
                last = jnp.where((col <= row) & (col + low < length), last, -1e30)
                top = jnp.max(last, axis=-1, keepdims=True)
                if step:
                    rest = lax.dot_general(
                        query, held[:low, key_at], contract, preferred_element_type=jnp.float32
                    )
                    keys = lax.broadcasted_iota(jnp.int32, (1, low), 1)
                    rest = rest + jnp.where(keys < length, 0.0, -1e30)
                    top = jnp.maximum(top, jnp.max(rest, axis=-1, keepdims=True))
                shift = top * factor
                probs = jnp.exp2(last * factor - shift)
                norm = jnp.sum(probs, axis=-1, keepdims=True)
                value = jnp.dot(
                    probs.astype(jnp.bfloat16),
                    held[low:high, value_at],
                    preferred_element_type=jnp.float32,
                )
                if step:
                    probs = jnp.exp2(rest * factor - shift)
                    norm = norm + jnp.sum(probs, axis=-1, keepdims=True)
                    value = value + jnp.dot(
                        probs.astype(jnp.bfloat16),
                        held[:low, value_at],
                        preferred_element_type=jnp.float32,
                    )
                out[low:high, out_at] = (value / norm).astype(out.dtype)


def attend_blocks(near, far, places, middle, length):
    parts = len(near)
    rows = sum(n.shape[0] for n in near)
    columns = near[0].shape[1]
    wide = columns // (GQ + 2) * GQ
    scal = jnp.stack([middle, length] + list(places)).astype(jnp.int32)
    return pl.pallas_call(
        functools.partial(attend_kernel, parts, 256),
        out_shape=jax.ShapeDtypeStruct((rows, wide), jnp.bfloat16),
        in_specs=[pl.BlockSpec(memory_space=pltpu.SMEM)]
        + [pl.BlockSpec(memory_space=pl.ANY)] * (2 * parts),
        out_specs=pl.BlockSpec(memory_space=pltpu.VMEM),
        scratch_shapes=[
            pltpu.VMEM((rows, columns), jnp.bfloat16),
            pltpu.SemaphoreType.DMA((parts,)),
        ],
        compiler_params=pltpu.CompilerParams(vmem_limit_bytes=VMEM_BYTES),
        cost_estimate=pl.CostEstimate(
            flops=4 * rows * rows * wide,
            bytes_accessed=2 * rows * (columns + wide),
            transcendentals=rows * rows * wide // HD // 2,
        ),
        name="attend",
    )(scal, *near, *far)


def after(x, *earlier):
    return lax.optimization_barrier((x,) + earlier)[0]


def four_planes(tokens, w_qkv, norm_gain, q_gain, k_gain, lengths):
    t = lax.axis_index("tensor")
    f = lax.axis_index("fsdp")
    rows = tokens.shape[0]
    columns = w_qkv.shape[1] // 4
    side = t // 2
    end = 3 * side
    mid = 1 + side
    far_end = 3 * (1 - side)
    far_mid = 2 - side

    def slab(block):
        return lax.dynamic_slice(w_qkv, (0, block * columns), (w_qkv.shape[0], columns))

    def across(x, pairs):
        return lax.ppermute(x, "tensor", pairs)

    def beside(x, bit):
        return lax.ppermute(x, "fsdp", [(i, i ^ bit) for i in range(4)])

    inward = [(0, 1), (3, 2)]
    swap = [(1, 2), (2, 1)]
    far = [(0, 2), (3, 1)]
    outward = [(1, 0), (2, 3)]

    same = jnp.concatenate([slab(end), slab(mid)], axis=1)
    other = jnp.concatenate([slab(far_end), slab(far_mid)], axis=1)
    normed = head_norm(tokens.astype(jnp.float32), norm_gain).astype(jnp.bfloat16)
    half = rows // 2

    from_swap = across(other, swap)
    from_end = across(same, inward)
    over_mine = beside(same, 2)
    core_mine = beside(same, 1)
    from_far_e = across(after(other[:, :columns], from_swap), far)
    rows_a1 = across(after(normed[:half], from_end), inward)
    over_swap_e = beside(after(from_swap[:, :columns], over_mine), 2)
    over_end_e = beside(after(from_end[:, :columns], over_mine), 2)
    core_swap = beside(from_swap, 1)
    core_end = beside(from_end, 1)
    core_over = beside(over_mine, 1)
    from_far_o = across(after(other[:, columns:], from_far_e), far)
    rows_b = across(after(normed, from_far_e), swap)
    rows_a2 = across(after(normed[half:], rows_a1), inward)
    over_far_e = beside(after(from_far_e, over_swap_e, over_end_e), 2)
    core_far_e = beside(from_far_e, 1)
    core_over_swap_e = beside(over_swap_e, 1)
    core_over_end_e = beside(over_end_e, 1)
    rows_c1 = across(after(rows_a1, from_far_o), swap)
    over_swap_o = beside(after(from_swap[:, columns:], over_far_e), 2)
    over_end_o = beside(after(from_end[:, columns:], over_far_e), 2)
    core_over_far_e = beside(over_far_e, 1)
    core_far_o = beside(from_far_o, 1)
    rows_c2 = across(after(rows_a2, rows_b), swap)
    over_far_o = beside(after(from_far_o, over_swap_o), 2)
    core_over_swap_o = beside(over_swap_o, 1)
    core_over_end_o = beside(over_end_o, 1)
    core_over_far_o = beside(over_far_o, 1)

    end_pieces = [
        (same, 0), (from_end, 0), (from_swap, 0), (from_far_e, 0),
        (over_mine, 0), (over_end_e, 0), (over_swap_e, 0), (over_far_e, 0),
        (core_mine, 0), (core_end, 0), (core_swap, 0), (core_far_e, 0),
        (core_over, 0), (core_over_end_e, 0), (core_over_swap_e, 0), (core_over_far_e, 0),
    ]
    mid_pieces = [
        (same, columns), (from_end, columns), (from_swap, columns), (from_far_o, 0),
        (over_mine, columns), (over_end_o, 0), (over_swap_o, 0), (over_far_o, 0),
        (core_mine, columns), (core_end, columns), (core_swap, columns), (core_far_o, 0),
        (core_over, columns), (core_over_end_o, 0), (core_over_swap_o, 0), (core_over_far_o, 0),
    ]
    scal = jnp.stack([mid, end, far_mid, far_end] + [jnp.bitwise_xor(f, m) for m in (0, 2, 1, 3)])

    positions = jnp.arange(4 * rows, dtype=jnp.int32)
    angle = angles(positions)
    cos = jnp.concatenate([jnp.cos(angle)] * 2, axis=1)
    sin = jnp.concatenate([-jnp.sin(angle), jnp.sin(angle)], axis=1)
    gains = jnp.stack([q_gain, k_gain])

    blocks = [normed, rows_b, rows_a1, rows_a2, rows_c1, rows_c2]
    places = [
        mid * rows,
        far_mid * rows,
        end * rows,
        end * rows + half,
        far_end * rows,
        far_end * rows + half,
    ]

    def run(picked, pieces):
        return project(
            [blocks[i] for i in picked], [places[i] for i in picked], pieces, scal, cos, sin, gains
        )

    sent = []
    for picked in ([0], [1, 2, 3], [4], [5]):
        sent += [across(x, outward) for x in run(picked, end_pieces)]
    near = []
    for picked in ([0, 1, 2, 3], [4, 5]):
        near += run(picked, mid_pieces)
    middle = jnp.where((t == 1) | (t == 2), 1, 0)
    return attend_blocks(near, sent, places, middle, lengths[0])


def solution(mesh):
    placed = (
        P(("groups", "fsdp", "tensor"), None),
        P(("groups", "fsdp", "tensor"), None),
        P(),
        P(),
        P(),
        P(("groups", "fsdp")),
    )
    sizes = dict(mesh.shape)
    body = four_planes if sizes["tensor"] == 4 and sizes["fsdp"] == 4 else any_mesh
    return jax.shard_map(
        body,
        mesh=mesh,
        in_specs=placed,
        out_specs=P(("groups", "fsdp"), "tensor"),
        check_vma=False,
    )
```

```python
import functools
import jax
import jax.numpy as jnp
from jax import lax
from jax.experimental import pallas as pl
from jax.experimental.pallas import tpu as pltpu
from jax.sharding import PartitionSpec as P

KV = 8
HD = 128
GQ = 4
LOG2E = 1.4426950408889634
VMEM_BYTES = 48 * 1024 * 1024


def head_norm(vec, gain):
    scale = lax.rsqrt(jnp.mean(vec * vec, axis=-1, keepdims=True) + 1e-06)
    return vec * scale * gain


def angles(positions):
    half = HD // 2
    freqs = 1000000.0 ** (-2.0 * jnp.arange(half, dtype=jnp.float32) / HD)
    return positions.astype(jnp.float32)[:, None] * freqs[None, :]


def rotate(vec, positions):
    half = vec.shape[-1] // 2
    angle = angles(positions)
    cosine = jnp.cos(angle)[:, None, None, :]
    sine = jnp.sin(angle)[:, None, None, :]
    first = vec[..., :half]
    second = vec[..., half:]
    return jnp.concatenate(
        [first * cosine - second * sine, second * cosine + first * sine], axis=-1
    )


def attend(qkv, q_gain, k_gain, length):
    rows = qkv.shape[0]
    group = qkv.shape[2] - 2
    positions = jnp.arange(rows, dtype=jnp.int32)
    query = rotate(head_norm(qkv[:, :, :group], q_gain), positions).astype(jnp.bfloat16)
    keyed = rotate(head_norm(qkv[:, :, group : group + 1], k_gain), positions)[:, :, 0].astype(
        jnp.bfloat16
    )
    value = qkv[:, :, group + 1].astype(jnp.bfloat16)
    scores = jnp.einsum(
        "ikgd,jkd->kgij", query, keyed, preferred_element_type=jnp.float32
    ) / jnp.sqrt(jnp.float32(qkv.shape[3]))
    allowed = (positions[None, :] <= positions[:, None]) & (positions[None, :] < length)
    scores = jnp.where(allowed[None, None], scores, jnp.float32(-1e30))
    top = jnp.max(scores, axis=-1, keepdims=True)
    weights = jnp.exp(scores - top)
    probs = (weights / jnp.sum(weights, axis=-1, keepdims=True)).astype(jnp.bfloat16)
    out = jnp.einsum("kgij,jkd->ikgd", probs, value, preferred_element_type=jnp.float32)
    return out.reshape(rows, -1).astype(jnp.bfloat16)


def any_mesh(tokens, w_qkv, norm_gain, q_gain, k_gain, lengths):
    tensor_count = lax.axis_size("tensor")
    moved = lax.all_to_all(w_qkv, "tensor", split_axis=1, concat_axis=0, tiled=True)
    weight_cols = lax.all_gather(moved, "fsdp", axis=0, tiled=True)
    normed = head_norm(tokens.astype(jnp.float32), norm_gain).astype(jnp.bfloat16)
    qkv = jnp.dot(
        lax.all_gather(normed, "tensor", axis=0, tiled=True),
        weight_cols,
        preferred_element_type=jnp.float32,
    )
    qkv = qkv.reshape(qkv.shape[0], KV // tensor_count, GQ + 2, HD)
    return attend(qkv, q_gain, k_gain, lengths[0])


def project_kernel(blocks, tile, scal, *refs):
    rows_refs = refs[:blocks]
    pieces = refs[blocks : blocks + 4]
    cos_ref, sin_ref, gain_ref = refs[blocks + 4 : blocks + 7]
    outs = refs[blocks + 7 : 2 * blocks + 7]
    taken, held, made, row_sems, sems, out_sems = refs[2 * blocks + 7 :]
    depth = pieces[0].shape[0] // 4
    columns = made.shape[1]
    steps = columns // tile

    def copies(step):
        listed = []
        for index in range(16):
            slot, group = divmod(index, 4)
            start = pl.multiple_of((group * 4 + scal[slot]) * depth, 16)
            low = step * tile
            listed.append(
                pltpu.make_async_copy(
                    pieces[slot].at[group * depth : (group + 1) * depth, low : low + tile],
                    held.at[step % 2, pl.ds(start, depth), :],
                    sems.at[step % 2, index],
                )
            )
        return listed

    starts = [sum(r.shape[0] for r in rows_refs[:n]) for n in range(blocks)]
    row_copies = [
        pltpu.make_async_copy(
            ref, taken.at[first : first + ref.shape[0], :], row_sems.at[number]
        )
        for number, (ref, first) in enumerate(zip(rows_refs, starts))
    ]
    out_copies = []
    for copy in copies(0) + row_copies:
        copy.start()
    for step in range(steps):
        if step + 1 < steps:
            for copy in copies(step + 1):
                copy.start()
        if step == 0:
            for copy in row_copies:
                copy.wait()
        for copy in copies(step):
            copy.wait()
        total = jnp.dot(taken[...], held[step % 2], preferred_element_type=jnp.float32)
        for number, (out, first) in enumerate(zip(outs, starts)):
            rows = out.shape[0]
            place = pl.ds(pl.multiple_of(scal[4 + number], 128), rows)
            cosine = cos_ref[place, :]
            sine = sin_ref[place, :]
            for head in range(tile // HD):
                kind = (step * (tile // HD) + head) % (GQ + 2)
                vec = total[first : first + rows, head * HD : (head + 1) * HD]
                if kind <= GQ:
                    scale = lax.rsqrt(jnp.mean(vec * vec, axis=-1, keepdims=True) + 1e-06)
                    gain = gain_ref[0:1, :] if kind < GQ else gain_ref[1:2, :]
                    vec = vec * scale * gain
                    vec = vec * cosine + pltpu.roll(vec, HD // 2, 1) * sine
                at = step * tile + head * HD
                made[first : first + rows, at : at + HD] = vec.astype(made.dtype)
            out_copies.append(
                pltpu.make_async_copy(
                    made.at[first : first + rows, step * tile : (step + 1) * tile],
                    out.at[:, step * tile : (step + 1) * tile],
                    out_sems.at[step, number],
                )
            )
            out_copies[-1].start()
    for copy in out_copies:
        copy.wait()


def project(rows_list, places, pieces, scal, cos, sin, gains):
    blocks = len(rows_list)
    columns = pieces[0].shape[1]
    steps = 3
    tile = columns // steps
    count = sum(r.shape[0] for r in rows_list)
    width = rows_list[0].shape[1]
    scal = jnp.concatenate([scal, jnp.stack(places)]).astype(jnp.int32)
    vmem = pl.BlockSpec(memory_space=pltpu.VMEM)
    hbm = pl.BlockSpec(memory_space=pltpu.HBM)
    return pl.pallas_call(
        functools.partial(project_kernel, blocks, tile),
        out_shape=[pltpu.HBM((r.shape[0], columns), jnp.bfloat16) for r in rows_list],
        in_specs=[pl.BlockSpec(memory_space=pltpu.SMEM)] + [hbm] * (blocks + 4) + [vmem] * 3,
        out_specs=[hbm] * blocks,
        scratch_shapes=[
            pltpu.VMEM((count, width), jnp.bfloat16),
            pltpu.VMEM((2, width, tile), jnp.bfloat16),
            pltpu.VMEM((count, columns), jnp.bfloat16),
            pltpu.SemaphoreType.DMA((blocks,)),
            pltpu.SemaphoreType.DMA((2, 16)),
            pltpu.SemaphoreType.DMA((steps, blocks)),
        ],
        compiler_params=pltpu.CompilerParams(vmem_limit_bytes=VMEM_BYTES),
        cost_estimate=pl.CostEstimate(
            flops=2 * count * width * columns,
            bytes_accessed=2 * (width * columns + count * (width + columns)),
            transcendentals=0,
        ),
        name="project",
    )(scal, *rows_list, *pieces, cos, sin, gains)


def attend_kernel(parts, block, scal, *refs):
    near = refs[:parts]
    far = refs[parts : 2 * parts]
    out = refs[2 * parts]
    held, sems = refs[2 * parts + 1 :]
    middle = scal[0]
    length = scal[1]
    copies = []
    for number in range(parts):
        rows = near[number].shape[0]
        place = pl.ds(pl.multiple_of(scal[2 + number], 128), rows)
        copies.append(
            [
                pltpu.make_async_copy(ref, held.at[place, :], sems.at[number])
                for ref in (near[number], far[number])
            ]
        )
        pl.when(middle == 1)(copies[-1][0].start)
        pl.when(middle == 0)(copies[-1][1].start)
    for pair in copies:
        pair[0].wait()
    total = held.shape[0]
    heads = held.shape[1] // ((GQ + 2) * HD)
    factor = LOG2E / float(HD) ** 0.5
    row = lax.broadcasted_iota(jnp.int32, (block, block), 0)
    col = lax.broadcasted_iota(jnp.int32, (block, block), 1)
    contract = (((1,), (1,)), ((), ()))
    for group in range(heads):
        base = group * (GQ + 2) * HD
        key_at = slice(base + GQ * HD, base + (GQ + 1) * HD)
        value_at = slice(base + (GQ + 1) * HD, base + (GQ + 2) * HD)

        @pl.loop(0, GQ)
        def _(j, base=base, key_at=key_at, value_at=value_at, group=group):
            query_at = pl.ds(pl.multiple_of(base + j * HD, HD), HD)
            out_at = pl.ds(pl.multiple_of((group * GQ + j) * HD, HD), HD)
            for step in range(total // block):
                low = step * block
                high = low + block
                query = held[low:high, query_at]
                last = lax.dot_general(
                    query, held[low:high, key_at], contract, preferred_element_type=jnp.float32
                )
                last = jnp.where((col <= row) & (col + low < length), last, -1e30)
                top = jnp.max(last, axis=-1, keepdims=True)
                if step:
                    rest = lax.dot_general(
                        query, held[:low, key_at], contract, preferred_element_type=jnp.float32
                    )
                    keys = lax.broadcasted_iota(jnp.int32, (1, low), 1)
                    rest = rest + jnp.where(keys < length, 0.0, -1e30)
                    top = jnp.maximum(top, jnp.max(rest, axis=-1, keepdims=True))
                shift = top * factor
                probs = jnp.exp2(last * factor - shift)
                norm = jnp.sum(probs, axis=-1, keepdims=True)
                value = jnp.dot(
                    probs.astype(jnp.bfloat16),
                    held[low:high, value_at],
                    preferred_element_type=jnp.float32,
                )
                if step:
                    probs = jnp.exp2(rest * factor - shift)
                    norm = norm + jnp.sum(probs, axis=-1, keepdims=True)
                    value = value + jnp.dot(
                        probs.astype(jnp.bfloat16),
                        held[:low, value_at],
                        preferred_element_type=jnp.float32,
                    )
                out[low:high, out_at] = (value / norm).astype(out.dtype)


def attend_blocks(near, far, places, middle, length):
    parts = len(near)
    rows = sum(n.shape[0] for n in near)
    columns = near[0].shape[1]
    wide = columns // (GQ + 2) * GQ
    scal = jnp.stack([middle, length] + list(places)).astype(jnp.int32)
    return pl.pallas_call(
        functools.partial(attend_kernel, parts, 256),
        out_shape=jax.ShapeDtypeStruct((rows, wide), jnp.bfloat16),
        in_specs=[pl.BlockSpec(memory_space=pltpu.SMEM)]
        + [pl.BlockSpec(memory_space=pl.ANY)] * (2 * parts),
        out_specs=pl.BlockSpec(memory_space=pltpu.VMEM),
        scratch_shapes=[
            pltpu.VMEM((rows, columns), jnp.bfloat16),
            pltpu.SemaphoreType.DMA((parts,)),
        ],
        compiler_params=pltpu.CompilerParams(vmem_limit_bytes=VMEM_BYTES),
        cost_estimate=pl.CostEstimate(
            flops=4 * rows * rows * wide,
            bytes_accessed=2 * rows * (columns + wide),
            transcendentals=rows * rows * wide // HD // 2,
        ),
        name="attend",
    )(scal, *near, *far)


def after(x, *earlier):
    return lax.optimization_barrier((x,) + earlier)[0]


def four_planes(tokens, w_qkv, norm_gain, q_gain, k_gain, lengths):
    t = lax.axis_index("tensor")
    rows = tokens.shape[0]
    columns = w_qkv.shape[1] // 4
    side = t // 2
    end = 3 * side
    mid = 1 + side
    far_end = 3 * (1 - side)
    far_mid = 2 - side

    def slab(block):
        return lax.dynamic_slice(w_qkv, (0, block * columns), (w_qkv.shape[0], columns))

    def across(x, pairs):
        return lax.ppermute(x, "tensor", pairs)

    def spread(x):
        return lax.all_gather(x, "fsdp", axis=0, tiled=True)

    inward = [(0, 1), (3, 2)]
    swap = [(1, 2), (2, 1)]
    far = [(0, 2), (3, 1)]
    outward = [(1, 0), (2, 3)]

    same_e, same_o, other_e, other_o = slab(end), slab(mid), slab(far_end), slab(far_mid)
    normed = head_norm(tokens.astype(jnp.float32), norm_gain).astype(jnp.bfloat16)
    half = rows // 2

    swap_e = across(other_e, swap)
    far_e = across(other_e, far)
    end_e = across(same_e, inward)
    swap_e, far_e, end_e = lax.optimization_barrier((swap_e, far_e, end_e))
    swap_o = across(after(other_o, swap_e), swap)
    far_o = across(after(other_o, swap_e), far)
    end_o = across(after(same_o, swap_e), inward)
    rows_a = across(after(normed, swap_e), inward)
    rows_b = across(after(normed, swap_e), swap)
    swap_o, far_o, end_o = lax.optimization_barrier((swap_o, far_o, end_o))
    rows_a, rows_b = lax.optimization_barrier((rows_a, rows_b))
    rows_c1 = across(rows_a[:half], swap)
    rows_c2 = across(rows_a[half:], swap)

    scal = jnp.stack([mid, end, far_mid, far_end]).astype(jnp.int32)
    end_pieces = [spread(x) for x in (same_e, end_e, swap_e, far_e)]
    mid_pieces = [spread(x) for x in (same_o, end_o, swap_o, far_o)]

    positions = jnp.arange(4 * rows, dtype=jnp.int32)
    angle = angles(positions)
    cos = jnp.concatenate([jnp.cos(angle)] * 2, axis=1)
    sin = jnp.concatenate([-jnp.sin(angle), jnp.sin(angle)], axis=1)
    gains = jnp.stack([q_gain, k_gain])

    blocks = [normed, rows_b, rows_a, rows_c1, rows_c2]
    places = [mid * rows, far_mid * rows, end * rows, far_end * rows, far_end * rows + half]

    def run(picked, pieces):
        return project(
            [blocks[i] for i in picked], [places[i] for i in picked], pieces, scal, cos, sin, gains
        )

    sent = []
    for picked in ([0], [1], [2], [3], [4]):
        sent += [across(x, outward) for x in run(picked, end_pieces)]
    near = []
    for picked in ([0, 1, 2], [3], [4]):
        near += run(picked, mid_pieces)
    middle = jnp.where((t == 1) | (t == 2), 1, 0)
    return attend_blocks(near, sent, places, middle, lengths[0])


def solution(mesh):
    placed = (
        P(("groups", "fsdp", "tensor"), None),
        P(("groups", "fsdp", "tensor"), None),
        P(),
        P(),
        P(),
        P(("groups", "fsdp")),
    )
    sizes = dict(mesh.shape)
    body = four_planes if sizes["tensor"] == 4 and sizes["fsdp"] == 4 else any_mesh
    return jax.shard_map(
        body,
        mesh=mesh,
        in_specs=placed,
        out_specs=P(("groups", "fsdp"), "tensor"),
        check_vma=False,
    )
```

```python
import functools
import jax
import jax.numpy as jnp
from jax import lax
from jax.experimental import pallas as pl
from jax.experimental.pallas import tpu as pltpu
from jax.sharding import PartitionSpec as P

KV = 8
HD = 128
GQ = 4
LOG2E = 1.4426950408889634
VMEM_BYTES = 48 * 1024 * 1024


def head_norm(vec, gain):
    scale = lax.rsqrt(jnp.mean(vec * vec, axis=-1, keepdims=True) + 1e-06)
    return vec * scale * gain


def angles(positions):
    half = HD // 2
    freqs = 1000000.0 ** (-2.0 * jnp.arange(half, dtype=jnp.float32) / HD)
    return positions.astype(jnp.float32)[:, None] * freqs[None, :]


def rotate(vec, positions):
    half = vec.shape[-1] // 2
    angle = angles(positions)
    cosine = jnp.cos(angle)[:, None, None, :]
    sine = jnp.sin(angle)[:, None, None, :]
    first = vec[..., :half]
    second = vec[..., half:]
    return jnp.concatenate(
        [first * cosine - second * sine, second * cosine + first * sine], axis=-1
    )


def attend(qkv, q_gain, k_gain, length):
    rows = qkv.shape[0]
    group = qkv.shape[2] - 2
    positions = jnp.arange(rows, dtype=jnp.int32)
    query = rotate(head_norm(qkv[:, :, :group], q_gain), positions).astype(jnp.bfloat16)
    keyed = rotate(head_norm(qkv[:, :, group : group + 1], k_gain), positions)[:, :, 0].astype(
        jnp.bfloat16
    )
    value = qkv[:, :, group + 1].astype(jnp.bfloat16)
    scores = jnp.einsum(
        "ikgd,jkd->kgij", query, keyed, preferred_element_type=jnp.float32
    ) / jnp.sqrt(jnp.float32(qkv.shape[3]))
    allowed = (positions[None, :] <= positions[:, None]) & (positions[None, :] < length)
    scores = jnp.where(allowed[None, None], scores, jnp.float32(-1e30))
    top = jnp.max(scores, axis=-1, keepdims=True)
    weights = jnp.exp(scores - top)
    probs = (weights / jnp.sum(weights, axis=-1, keepdims=True)).astype(jnp.bfloat16)
    out = jnp.einsum("kgij,jkd->ikgd", probs, value, preferred_element_type=jnp.float32)
    return out.reshape(rows, -1).astype(jnp.bfloat16)


def any_mesh(tokens, w_qkv, norm_gain, q_gain, k_gain, lengths):
    tensor_count = lax.axis_size("tensor")
    moved = lax.all_to_all(w_qkv, "tensor", split_axis=1, concat_axis=0, tiled=True)
    weight_cols = lax.all_gather(moved, "fsdp", axis=0, tiled=True)
    normed = head_norm(tokens.astype(jnp.float32), norm_gain).astype(jnp.bfloat16)
    qkv = jnp.dot(
        lax.all_gather(normed, "tensor", axis=0, tiled=True),
        weight_cols,
        preferred_element_type=jnp.float32,
    )
    qkv = qkv.reshape(qkv.shape[0], KV // tensor_count, GQ + 2, HD)
    return attend(qkv, q_gain, k_gain, lengths[0])


def project_kernel(counts, tile, scal, *refs):
    blocks = len(counts)
    rows_refs = refs[:blocks]
    pieces = refs[blocks : blocks + 16]
    cos_ref, sin_ref, gain_ref, out = refs[blocks + 16 : blocks + 20]
    taken, held, made, row_sems, sems, out_sems = refs[blocks + 20 :]
    depth = pieces[0].shape[0]
    columns = made.shape[1]
    steps = columns // tile

    def copies(step):
        listed = []
        for index in range(16):
            start = pl.multiple_of((scal[4 + index // 4] * 4 + scal[index % 4]) * depth, 16)
            listed.append(
                pltpu.make_async_copy(
                    pieces[index].at[:, step * tile : (step + 1) * tile],
                    held.at[step % 2, pl.ds(start, depth), :],
                    sems.at[step % 2, index],
                )
            )
        return listed

    starts = [sum(counts[:n]) for n in range(blocks)]
    row_copies = [
        pltpu.make_async_copy(ref, taken.at[first : first + rows, :], row_sems.at[number])
        for number, (ref, first, rows) in enumerate(zip(rows_refs, starts, counts))
    ]
    out_copies = []
    for copy in copies(0) + row_copies:
        copy.start()
    for step in range(steps):
        if step + 1 < steps:
            for copy in copies(step + 1):
                copy.start()
        if step == 0:
            for copy in row_copies:
                copy.wait()
        for copy in copies(step):
            copy.wait()
        total = jnp.dot(taken[...], held[step % 2], preferred_element_type=jnp.float32)
        for number, (first, rows) in enumerate(zip(starts, counts)):
            place = pl.ds(pl.multiple_of(scal[8 + number], 128), rows)
            cosine = cos_ref[place, :]
            sine = sin_ref[place, :]
            for head in range(tile // HD):
                kind = (step * (tile // HD) + head) % (GQ + 2)
                vec = total[first : first + rows, head * HD : (head + 1) * HD]
                if kind <= GQ:
                    scale = lax.rsqrt(jnp.mean(vec * vec, axis=-1, keepdims=True) + 1e-06)
                    gain = gain_ref[0:1, :] if kind < GQ else gain_ref[1:2, :]
                    vec = vec * scale * gain
                    vec = vec * cosine + pltpu.roll(vec, HD // 2, 1) * sine
                at = step * tile + head * HD
                made[first : first + rows, at : at + HD] = vec.astype(made.dtype)
        at = slice(step * tile, (step + 1) * tile)
        out_copies.append(pltpu.make_async_copy(made.at[:, at], out.at[:, at], out_sems.at[step]))
        out_copies[-1].start()
    for copy in out_copies:
        copy.wait()


def project(rows_list, places, pieces, scal, cos, sin, gains):
    counts = [r.shape[0] for r in rows_list]
    columns = pieces[0].shape[1]
    steps = 3
    tile = columns // steps
    count = sum(counts)
    width = rows_list[0].shape[1]
    scal = jnp.concatenate([scal, jnp.stack(places)]).astype(jnp.int32)
    vmem = pl.BlockSpec(memory_space=pltpu.VMEM)
    hbm = pl.BlockSpec(memory_space=pltpu.HBM)
    return pl.pallas_call(
        functools.partial(project_kernel, counts, tile),
        out_shape=pltpu.HBM((count, columns), jnp.bfloat16),
        in_specs=[pl.BlockSpec(memory_space=pltpu.SMEM)]
        + [hbm] * (len(counts) + 16)
        + [vmem] * 3,
        out_specs=hbm,
        scratch_shapes=[
            pltpu.VMEM((count, width), jnp.bfloat16),
            pltpu.VMEM((2, width, tile), jnp.bfloat16),
            pltpu.VMEM((count, columns), jnp.bfloat16),
            pltpu.SemaphoreType.DMA((len(counts),)),
            pltpu.SemaphoreType.DMA((2, 16)),
            pltpu.SemaphoreType.DMA((steps,)),
        ],
        compiler_params=pltpu.CompilerParams(vmem_limit_bytes=VMEM_BYTES),
        cost_estimate=pl.CostEstimate(
            flops=2 * count * width * columns,
            bytes_accessed=2 * (width * columns + count * (width + columns)),
            transcendentals=0,
        ),
        name="project",
    )(scal, *rows_list, *pieces, cos, sin, gains)


def attend_kernel(near_parts, far_parts, block, scal, *refs):
    near = refs[: len(near_parts)]
    far = refs[len(near_parts) : len(near_parts) + len(far_parts)]
    out, held, sems = refs[len(near_parts) + len(far_parts) :]
    middle = scal[0]
    length = scal[1]

    def fetch(sources, parts):
        copies = []
        for ref, blocks in zip(sources, parts):
            for first, rows, number in blocks:
                place = pl.ds(pl.multiple_of(scal[2 + number], 128), rows)
                copies.append(
                    pltpu.make_async_copy(
                        ref.at[first : first + rows, :], held.at[place, :], sems.at[number]
                    )
                )
        for copy in copies:
            copy.start()
        for copy in copies:
            copy.wait()

    @pl.when(middle == 1)
    def _():
        fetch(near, near_parts)

    @pl.when(middle == 0)
    def _():
        fetch(far, far_parts)

    total = held.shape[0]
    heads = held.shape[1] // ((GQ + 2) * HD)
    factor = LOG2E / float(HD) ** 0.5
    row = lax.broadcasted_iota(jnp.int32, (block, block), 0)
    col = lax.broadcasted_iota(jnp.int32, (block, block), 1)
    contract = (((1,), (1,)), ((), ()))
    for group in range(heads):
        base = group * (GQ + 2) * HD
        key_at = slice(base + GQ * HD, base + (GQ + 1) * HD)
        value_at = slice(base + (GQ + 1) * HD, base + (GQ + 2) * HD)

        @pl.loop(0, GQ)
        def _(j, base=base, key_at=key_at, value_at=value_at, group=group):
            query_at = pl.ds(pl.multiple_of(base + j * HD, HD), HD)
            out_at = pl.ds(pl.multiple_of((group * GQ + j) * HD, HD), HD)
            for step in range(total // block):
                low = step * block
                high = low + block
                query = held[low:high, query_at]
                last = lax.dot_general(
                    query, held[low:high, key_at], contract, preferred_element_type=jnp.float32
                )
                last = jnp.where((col <= row) & (col + low < length), last, -1e30)
                top = jnp.max(last, axis=-1, keepdims=True)
                if step:
                    rest = lax.dot_general(
                        query, held[:low, key_at], contract, preferred_element_type=jnp.float32
                    )
                    keys = lax.broadcasted_iota(jnp.int32, (1, low), 1)
                    rest = rest + jnp.where(keys < length, 0.0, -1e30)
                    top = jnp.maximum(top, jnp.max(rest, axis=-1, keepdims=True))
                shift = top * factor
                probs = jnp.exp2(last * factor - shift)
                norm = jnp.sum(probs, axis=-1, keepdims=True)
                value = jnp.dot(
                    probs.astype(jnp.bfloat16),
                    held[low:high, value_at],
                    preferred_element_type=jnp.float32,
                )
                if step:
                    probs = jnp.exp2(rest * factor - shift)
                    norm = norm + jnp.sum(probs, axis=-1, keepdims=True)
                    value = value + jnp.dot(
                        probs.astype(jnp.bfloat16),
                        held[:low, value_at],
                        preferred_element_type=jnp.float32,
                    )
                out[low:high, out_at] = (value / norm).astype(out.dtype)


def attend_blocks(near, far, near_parts, far_parts, places, middle, length):
    rows = sum(n.shape[0] for n in near)
    columns = near[0].shape[1]
    wide = columns // (GQ + 2) * GQ
    scal = jnp.stack([middle, length] + list(places)).astype(jnp.int32)
    hbm = pl.BlockSpec(memory_space=pltpu.HBM)
    return pl.pallas_call(
        functools.partial(attend_kernel, near_parts, far_parts, 256),
        out_shape=jax.ShapeDtypeStruct((rows, wide), jnp.bfloat16),
        in_specs=[pl.BlockSpec(memory_space=pltpu.SMEM)] + [hbm] * (len(near) + len(far)),
        out_specs=pl.BlockSpec(memory_space=pltpu.VMEM),
        scratch_shapes=[
            pltpu.VMEM((rows, columns), jnp.bfloat16),
            pltpu.SemaphoreType.DMA((len(places),)),
        ],
        compiler_params=pltpu.CompilerParams(vmem_limit_bytes=VMEM_BYTES),
        cost_estimate=pl.CostEstimate(
            flops=4 * rows * rows * wide,
            bytes_accessed=2 * rows * (columns + wide),
            transcendentals=rows * rows * wide // HD // 2,
        ),
        name="attend",
    )(scal, *near, *far)


def after(x, *earlier):
    return lax.optimization_barrier((x,) + earlier)[0]


def four_planes(tokens, w_qkv, norm_gain, q_gain, k_gain, lengths):
    t = lax.axis_index("tensor")
    f = lax.axis_index("fsdp")
    rows = tokens.shape[0]
    columns = w_qkv.shape[1] // 4
    side = t // 2
    end = 3 * side
    mid = 1 + side
    far_end = 3 * (1 - side)
    far_mid = 2 - side

    def slab(block):
        return lax.dynamic_slice(w_qkv, (0, block * columns), (w_qkv.shape[0], columns))

    def across(x, pairs):
        return lax.ppermute(x, "tensor", pairs)

    def beside(x, bit):
        return lax.ppermute(x, "fsdp", [(i, i ^ bit) for i in range(4)])

    inward = [(0, 1), (3, 2)]
    swap = [(1, 2), (2, 1)]
    far = [(0, 2), (3, 1)]
    outward = [(1, 0), (2, 3)]

    same_e, same_o, other_e, other_o = slab(end), slab(mid), slab(far_end), slab(far_mid)
    normed = head_norm(tokens.astype(jnp.float32), norm_gain).astype(jnp.bfloat16)

    swap_e = across(other_e, swap)
    far_e = across(other_e, far)
    end_e = across(same_e, inward)
    swap_o = across(after(other_o, swap_e), swap)
    rows_b = across(after(normed, swap_o), swap)
    rows_a = across(after(normed, far_e, end_e), inward)
    far_o = across(after(other_o, far_e, end_e), far)
    end_o = across(after(same_o, far_o), inward)
    rows_c = across(rows_a, swap)

    over = []
    for piece in (same_e, swap_e, far_e, end_e, same_o, swap_o, far_o, end_o):
        over.append(beside(after(piece, *over[-2:-1]), 2))

    def all_pieces(mine, theirs):
        return mine + theirs + [beside(x, 1) for x in mine] + [beside(x, 1) for x in theirs]

    end_pieces = all_pieces([same_e, swap_e, far_e, end_e], over[:4])
    mid_pieces = all_pieces([same_o, swap_o, far_o, end_o], over[4:])
    scal = jnp.stack([mid, far_mid, far_end, end] + [jnp.bitwise_xor(f, m) for m in (0, 2, 1, 3)])

    positions = jnp.arange(4 * rows, dtype=jnp.int32)
    angle = angles(positions)
    cos = jnp.concatenate([jnp.cos(angle)] * 2, axis=1)
    sin = jnp.concatenate([-jnp.sin(angle), jnp.sin(angle)], axis=1)
    gains = jnp.stack([q_gain, k_gain])

    blocks = [normed, rows_b, rows_a, rows_c]
    places = [mid * rows, far_mid * rows, end * rows, far_end * rows]

    def run(picked, pieces):
        return project(
            [blocks[i] for i in picked], [places[i] for i in picked], pieces, scal, cos, sin, gains
        )

    sent = [across(run(picked, end_pieces), outward) for picked in ([0, 1], [2, 3])]
    near = [run([0, 1, 2, 3], mid_pieces)]
    near_parts = [[(i * rows, rows, i) for i in range(4)]]
    far_parts = [[(i * rows, rows, 2 * n + i) for i in range(2)] for n in range(2)]
    middle = jnp.where((t == 1) | (t == 2), 1, 0)
    return attend_blocks(near, sent, near_parts, far_parts, places, middle, lengths[0])


def solution(mesh):
    placed = (
        P(("groups", "fsdp", "tensor"), None),
        P(("groups", "fsdp", "tensor"), None),
        P(),
        P(),
        P(),
        P(("groups", "fsdp")),
    )
    sizes = dict(mesh.shape)
    body = four_planes if sizes["tensor"] == 4 and sizes["fsdp"] == 4 else any_mesh
    return jax.shard_map(
        body,
        mesh=mesh,
        in_specs=placed,
        out_specs=P(("groups", "fsdp"), "tensor"),
        check_vma=False,
    )
```

```python
import functools
import jax
import jax.numpy as jnp
from jax import lax
from jax.experimental import pallas as pl
from jax.experimental.pallas import tpu as pltpu
from jax.sharding import PartitionSpec as P

KV = 8
HD = 128
GQ = 4
LOG2E = 1.4426950408889634
VMEM_BYTES = 48 * 1024 * 1024


def head_norm(vec, gain):
    scale = lax.rsqrt(jnp.mean(vec * vec, axis=-1, keepdims=True) + 1e-06)
    return vec * scale * gain


def angles(positions):
    half = HD // 2
    freqs = 1000000.0 ** (-2.0 * jnp.arange(half, dtype=jnp.float32) / HD)
    return positions.astype(jnp.float32)[:, None] * freqs[None, :]


def rotate(vec, positions):
    half = vec.shape[-1] // 2
    angle = angles(positions)
    cosine = jnp.cos(angle)[:, None, None, :]
    sine = jnp.sin(angle)[:, None, None, :]
    first = vec[..., :half]
    second = vec[..., half:]
    return jnp.concatenate(
        [first * cosine - second * sine, second * cosine + first * sine], axis=-1
    )


def attend(qkv, q_gain, k_gain, length):
    rows = qkv.shape[0]
    group = qkv.shape[2] - 2
    positions = jnp.arange(rows, dtype=jnp.int32)
    query = rotate(head_norm(qkv[:, :, :group], q_gain), positions).astype(jnp.bfloat16)
    keyed = rotate(head_norm(qkv[:, :, group : group + 1], k_gain), positions)[:, :, 0].astype(
        jnp.bfloat16
    )
    value = qkv[:, :, group + 1].astype(jnp.bfloat16)
    scores = jnp.einsum(
        "ikgd,jkd->kgij", query, keyed, preferred_element_type=jnp.float32
    ) / jnp.sqrt(jnp.float32(qkv.shape[3]))
    allowed = (positions[None, :] <= positions[:, None]) & (positions[None, :] < length)
    scores = jnp.where(allowed[None, None], scores, jnp.float32(-1e30))
    top = jnp.max(scores, axis=-1, keepdims=True)
    weights = jnp.exp(scores - top)
    probs = (weights / jnp.sum(weights, axis=-1, keepdims=True)).astype(jnp.bfloat16)
    out = jnp.einsum("kgij,jkd->ikgd", probs, value, preferred_element_type=jnp.float32)
    return out.reshape(rows, -1).astype(jnp.bfloat16)


def any_mesh(tokens, w_qkv, norm_gain, q_gain, k_gain, lengths):
    tensor_count = lax.axis_size("tensor")
    moved = lax.all_to_all(w_qkv, "tensor", split_axis=1, concat_axis=0, tiled=True)
    weight_cols = lax.all_gather(moved, "fsdp", axis=0, tiled=True)
    normed = head_norm(tokens.astype(jnp.float32), norm_gain).astype(jnp.bfloat16)
    qkv = jnp.dot(
        lax.all_gather(normed, "tensor", axis=0, tiled=True),
        weight_cols,
        preferred_element_type=jnp.float32,
    )
    qkv = qkv.reshape(qkv.shape[0], KV // tensor_count, GQ + 2, HD)
    return attend(qkv, q_gain, k_gain, lengths[0])


def project_kernel(counts, sources, tile, scal, *refs):
    blocks = len(counts)
    arrays = max(source[0] for source in sources) + 1
    rows_refs = refs[:blocks]
    pieces = refs[blocks : blocks + arrays]
    cos_ref, sin_ref, gain_ref, out = refs[blocks + arrays : blocks + arrays + 4]
    taken, held, made, row_sems, sems, out_sems = refs[blocks + arrays + 4 :]
    depth = taken.shape[1] // 16
    columns = made.shape[1]
    steps = columns // tile

    def copies(step):
        listed = []
        for index, (array, first, group, slot) in enumerate(sources):
            start = pl.multiple_of((scal[group] * 4 + scal[slot]) * depth, 16)
            listed.append(
                pltpu.make_async_copy(
                    pieces[array].at[first : first + depth, step * tile : (step + 1) * tile],
                    held.at[step % 2, pl.ds(start, depth), :],
                    sems.at[step % 2, index],
                )
            )
        return listed

    starts = [sum(counts[:n]) for n in range(blocks)]
    row_copies = [
        pltpu.make_async_copy(ref, taken.at[first : first + rows, :], row_sems.at[number])
        for number, (ref, first, rows) in enumerate(zip(rows_refs, starts, counts))
    ]
    out_copies = []
    for copy in copies(0) + row_copies:
        copy.start()
    for step in range(steps):
        if step + 1 < steps:
            for copy in copies(step + 1):
                copy.start()
        if step == 0:
            for copy in row_copies:
                copy.wait()
        for copy in copies(step):
            copy.wait()
        total = jnp.dot(taken[...], held[step % 2], preferred_element_type=jnp.float32)
        for number, (first, rows) in enumerate(zip(starts, counts)):
            place = pl.ds(pl.multiple_of(scal[12 + number], 128), rows)
            cosine = cos_ref[place, :]
            sine = sin_ref[place, :]
            for head in range(tile // HD):
                kind = (step * (tile // HD) + head) % (GQ + 2)
                vec = total[first : first + rows, head * HD : (head + 1) * HD]
                if kind <= GQ:
                    scale = lax.rsqrt(jnp.mean(vec * vec, axis=-1, keepdims=True) + 1e-06)
                    gain = gain_ref[0:1, :] if kind < GQ else gain_ref[1:2, :]
                    vec = vec * scale * gain
                    vec = vec * cosine + pltpu.roll(vec, HD // 2, 1) * sine
                at = step * tile + head * HD
                made[first : first + rows, at : at + HD] = vec.astype(made.dtype)
        at = slice(step * tile, (step + 1) * tile)
        out_copies.append(pltpu.make_async_copy(made.at[:, at], out.at[:, at], out_sems.at[step]))
        out_copies[-1].start()
    for copy in out_copies:
        copy.wait()


def project(rows_list, places, spread_pieces, own_pieces, scal, cos, sin, gains):
    pieces, sources = [], []
    depth = rows_list[0].shape[1] // 16
    for slot, array in spread_pieces:
        sources += [(len(pieces), m * depth, 8 + m, slot) for m in range(4)]
        pieces.append(array)
    for slot, four in own_pieces:
        sources += [(len(pieces) + m, 0, 4 + m, slot) for m in range(4)]
        pieces += four
    counts = [r.shape[0] for r in rows_list]
    columns = pieces[0].shape[1]
    steps = 3
    tile = columns // steps
    count = sum(counts)
    width = rows_list[0].shape[1]
    scal = jnp.concatenate([scal, jnp.stack(places)]).astype(jnp.int32)
    vmem = pl.BlockSpec(memory_space=pltpu.VMEM)
    hbm = pl.BlockSpec(memory_space=pltpu.HBM)
    return pl.pallas_call(
        functools.partial(project_kernel, counts, sources, tile),
        out_shape=pltpu.HBM((count, columns), jnp.bfloat16),
        in_specs=[pl.BlockSpec(memory_space=pltpu.SMEM)]
        + [hbm] * (len(counts) + len(pieces))
        + [vmem] * 3,
        out_specs=hbm,
        scratch_shapes=[
            pltpu.VMEM((count, width), jnp.bfloat16),
            pltpu.VMEM((2, width, tile), jnp.bfloat16),
            pltpu.VMEM((count, columns), jnp.bfloat16),
            pltpu.SemaphoreType.DMA((len(counts),)),
            pltpu.SemaphoreType.DMA((2, 16)),
            pltpu.SemaphoreType.DMA((steps,)),
        ],
        compiler_params=pltpu.CompilerParams(vmem_limit_bytes=VMEM_BYTES),
        cost_estimate=pl.CostEstimate(
            flops=2 * count * width * columns,
            bytes_accessed=2 * (width * columns + count * (width + columns)),
            transcendentals=0,
        ),
        name="project",
    )(scal, *rows_list, *pieces, cos, sin, gains)


def attend_kernel(near_parts, far_parts, block, scal, *refs):
    near = refs[: len(near_parts)]
    far = refs[len(near_parts) : len(near_parts) + len(far_parts)]
    out, held, sems = refs[len(near_parts) + len(far_parts) :]
    middle = scal[0]
    length = scal[1]

    def fetch(sources, parts):
        copies = []
        for ref, blocks in zip(sources, parts):
            for first, rows, number in blocks:
                place = pl.ds(pl.multiple_of(scal[2 + number], 128), rows)
                copies.append(
                    pltpu.make_async_copy(
                        ref.at[first : first + rows, :], held.at[place, :], sems.at[number]
                    )
                )
        for copy in copies:
            copy.start()
        for copy in copies:
            copy.wait()

    @pl.when(middle == 1)
    def _():
        fetch(near, near_parts)

    @pl.when(middle == 0)
    def _():
        fetch(far, far_parts)

    total = held.shape[0]
    heads = held.shape[1] // ((GQ + 2) * HD)
    factor = LOG2E / float(HD) ** 0.5
    row = lax.broadcasted_iota(jnp.int32, (block, block), 0)
    col = lax.broadcasted_iota(jnp.int32, (block, block), 1)
    contract = (((1,), (1,)), ((), ()))
    for group in range(heads):
        base = group * (GQ + 2) * HD
        key_at = slice(base + GQ * HD, base + (GQ + 1) * HD)
        value_at = slice(base + (GQ + 1) * HD, base + (GQ + 2) * HD)

        @pl.loop(0, GQ)
        def _(j, base=base, key_at=key_at, value_at=value_at, group=group):
            query_at = pl.ds(pl.multiple_of(base + j * HD, HD), HD)
            out_at = pl.ds(pl.multiple_of((group * GQ + j) * HD, HD), HD)
            for step in range(total // block):
                low = step * block
                high = low + block
                query = held[low:high, query_at]
                last = lax.dot_general(
                    query, held[low:high, key_at], contract, preferred_element_type=jnp.float32
                )
                last = jnp.where((col <= row) & (col + low < length), last, -1e30)
                top = jnp.max(last, axis=-1, keepdims=True)
                if step:
                    rest = lax.dot_general(
                        query, held[:low, key_at], contract, preferred_element_type=jnp.float32
                    )
                    keys = lax.broadcasted_iota(jnp.int32, (1, low), 1)
                    rest = rest + jnp.where(keys < length, 0.0, -1e30)
                    top = jnp.maximum(top, jnp.max(rest, axis=-1, keepdims=True))
                shift = top * factor
                probs = jnp.exp2(last * factor - shift)
                norm = jnp.sum(probs, axis=-1, keepdims=True)
                value = jnp.dot(
                    probs.astype(jnp.bfloat16),
                    held[low:high, value_at],
                    preferred_element_type=jnp.float32,
                )
                if step:
                    probs = jnp.exp2(rest * factor - shift)
                    norm = norm + jnp.sum(probs, axis=-1, keepdims=True)
                    value = value + jnp.dot(
                        probs.astype(jnp.bfloat16),
                        held[:low, value_at],
                        preferred_element_type=jnp.float32,
                    )
                out[low:high, out_at] = (value / norm).astype(out.dtype)


def attend_blocks(near, far, near_parts, far_parts, places, middle, length):
    rows = sum(n.shape[0] for n in near)
    columns = near[0].shape[1]
    wide = columns // (GQ + 2) * GQ
    scal = jnp.stack([middle, length] + list(places)).astype(jnp.int32)
    hbm = pl.BlockSpec(memory_space=pltpu.HBM)
    return pl.pallas_call(
        functools.partial(attend_kernel, near_parts, far_parts, 256),
        out_shape=jax.ShapeDtypeStruct((rows, wide), jnp.bfloat16),
        in_specs=[pl.BlockSpec(memory_space=pltpu.SMEM)] + [hbm] * (len(near) + len(far)),
        out_specs=pl.BlockSpec(memory_space=pltpu.VMEM),
        scratch_shapes=[
            pltpu.VMEM((rows, columns), jnp.bfloat16),
            pltpu.SemaphoreType.DMA((len(places),)),
        ],
        compiler_params=pltpu.CompilerParams(vmem_limit_bytes=VMEM_BYTES),
        cost_estimate=pl.CostEstimate(
            flops=4 * rows * rows * wide,
            bytes_accessed=2 * rows * (columns + wide),
            transcendentals=rows * rows * wide // HD // 2,
        ),
        name="attend",
    )(scal, *near, *far)


def after(x, *earlier):
    return lax.optimization_barrier((x,) + earlier)[0]


def four_planes(tokens, w_qkv, norm_gain, q_gain, k_gain, lengths):
    t = lax.axis_index("tensor")
    f = lax.axis_index("fsdp")
    rows = tokens.shape[0]
    columns = w_qkv.shape[1] // 4
    side = t // 2
    end = 3 * side
    mid = 1 + side
    far_end = 3 * (1 - side)
    far_mid = 2 - side

    def slab(block):
        return lax.dynamic_slice(w_qkv, (0, block * columns), (w_qkv.shape[0], columns))

    def across(x, pairs):
        return lax.ppermute(x, "tensor", pairs)

    def beside(x, bit):
        return lax.ppermute(x, "fsdp", [(i, i ^ bit) for i in range(4)])

    def spread(x):
        return lax.all_gather(x, "fsdp", axis=0, tiled=True)

    inward = [(0, 1), (3, 2)]
    swap = [(1, 2), (2, 1)]
    far = [(0, 2), (3, 1)]
    outward = [(1, 0), (2, 3)]

    same_e, same_o, other_e, other_o = slab(end), slab(mid), slab(far_end), slab(far_mid)
    normed = head_norm(tokens.astype(jnp.float32), norm_gain).astype(jnp.bfloat16)

    def core_pair(piece, over):
        return [piece, over, beside(piece, 1), beside(over, 1)]

    own_e, own_o = spread(same_e), spread(same_o)
    swap_e = across(other_e, swap)
    far_e = across(other_e, far)
    end_e = across(same_e, inward)
    swap_o = across(other_o, swap)
    swap_e, far_e, end_e, swap_o = lax.optimization_barrier((swap_e, far_e, end_e, swap_o))
    far_o = across(after(other_o, swap_e), far)
    end_o = across(after(same_o, swap_e), inward)
    over_swap_e = beside(swap_e, 2)
    over_far_e = beside(far_e, 2)
    far_o, end_o, over_swap_e, over_far_e = lax.optimization_barrier(
        (far_o, end_o, over_swap_e, over_far_e)
    )
    rows_a = across(after(normed, far_o), inward)
    rows_b = across(after(normed, far_o), swap)
    over_end_e = beside(after(end_e, far_o), 2)
    over_swap_o = beside(after(swap_o, over_end_e), 2)
    rows_c = across(after(rows_a, over_swap_o), swap)

    end_pieces = (
        [(0, own_e)],
        [
            (1, core_pair(swap_e, over_swap_e)),
            (2, core_pair(far_e, over_far_e)),
            (3, core_pair(end_e, over_end_e)),
        ],
    )
    mid_pieces = (
        [(0, own_o), (2, spread(far_o)), (3, spread(end_o))],
        [(1, core_pair(swap_o, over_swap_o))],
    )
    scal = jnp.stack(
        [mid, far_mid, far_end, end]
        + [jnp.bitwise_xor(f, m) for m in (0, 2, 1, 3)]
        + [jnp.int32(m) for m in range(4)]
    )

    positions = jnp.arange(4 * rows, dtype=jnp.int32)
    angle = angles(positions)
    cos = jnp.concatenate([jnp.cos(angle)] * 2, axis=1)
    sin = jnp.concatenate([-jnp.sin(angle), jnp.sin(angle)], axis=1)
    gains = jnp.stack([q_gain, k_gain])

    blocks = [normed, rows_b, rows_a, rows_c]
    places = [mid * rows, far_mid * rows, end * rows, far_end * rows]

    def run(picked, pieces):
        return project(
            [blocks[i] for i in picked], [places[i] for i in picked], *pieces, scal, cos, sin, gains
        )

    sent = [across(run(picked, end_pieces), outward) for picked in ([0, 1], [2, 3])]
    near = [run([0, 1, 2, 3], mid_pieces)]
    near_parts = [[(i * rows, rows, i) for i in range(4)]]
    far_parts = [[(i * rows, rows, 2 * n + i) for i in range(2)] for n in range(2)]
    middle = jnp.where((t == 1) | (t == 2), 1, 0)
    return attend_blocks(near, sent, near_parts, far_parts, places, middle, lengths[0])


def solution(mesh):
    placed = (
        P(("groups", "fsdp", "tensor"), None),
        P(("groups", "fsdp", "tensor"), None),
        P(),
        P(),
        P(),
        P(("groups", "fsdp")),
    )
    sizes = dict(mesh.shape)
    body = four_planes if sizes["tensor"] == 4 and sizes["fsdp"] == 4 else any_mesh
    return jax.shard_map(
        body,
        mesh=mesh,
        in_specs=placed,
        out_specs=P(("groups", "fsdp"), "tensor"),
        check_vma=False,
    )
```

```python
import functools
import jax
import jax.numpy as jnp
from jax import lax
from jax.experimental import pallas as pl
from jax.experimental.pallas import tpu as pltpu
from jax.sharding import PartitionSpec as P

KV = 8
HD = 128
GQ = 4
LOG2E = 1.4426950408889634
VMEM_BYTES = 48 * 1024 * 1024


def head_norm(vec, gain):
    scale = lax.rsqrt(jnp.mean(vec * vec, axis=-1, keepdims=True) + 1e-06)
    return vec * scale * gain


def angles(positions):
    half = HD // 2
    freqs = 1000000.0 ** (-2.0 * jnp.arange(half, dtype=jnp.float32) / HD)
    return positions.astype(jnp.float32)[:, None] * freqs[None, :]


def rotate(vec, positions):
    half = vec.shape[-1] // 2
    angle = angles(positions)
    cosine = jnp.cos(angle)[:, None, None, :]
    sine = jnp.sin(angle)[:, None, None, :]
    first = vec[..., :half]
    second = vec[..., half:]
    return jnp.concatenate(
        [first * cosine - second * sine, second * cosine + first * sine], axis=-1
    )


def attend(qkv, q_gain, k_gain, length):
    rows = qkv.shape[0]
    group = qkv.shape[2] - 2
    positions = jnp.arange(rows, dtype=jnp.int32)
    query = rotate(head_norm(qkv[:, :, :group], q_gain), positions).astype(jnp.bfloat16)
    keyed = rotate(head_norm(qkv[:, :, group : group + 1], k_gain), positions)[:, :, 0].astype(
        jnp.bfloat16
    )
    value = qkv[:, :, group + 1].astype(jnp.bfloat16)
    scores = jnp.einsum(
        "ikgd,jkd->kgij", query, keyed, preferred_element_type=jnp.float32
    ) / jnp.sqrt(jnp.float32(qkv.shape[3]))
    allowed = (positions[None, :] <= positions[:, None]) & (positions[None, :] < length)
    scores = jnp.where(allowed[None, None], scores, jnp.float32(-1e30))
    top = jnp.max(scores, axis=-1, keepdims=True)
    weights = jnp.exp(scores - top)
    probs = (weights / jnp.sum(weights, axis=-1, keepdims=True)).astype(jnp.bfloat16)
    out = jnp.einsum("kgij,jkd->ikgd", probs, value, preferred_element_type=jnp.float32)
    return out.reshape(rows, -1).astype(jnp.bfloat16)


def any_mesh(tokens, w_qkv, norm_gain, q_gain, k_gain, lengths):
    tensor_count = lax.axis_size("tensor")
    moved = lax.all_to_all(w_qkv, "tensor", split_axis=1, concat_axis=0, tiled=True)
    weight_cols = lax.all_gather(moved, "fsdp", axis=0, tiled=True)
    normed = head_norm(tokens.astype(jnp.float32), norm_gain).astype(jnp.bfloat16)
    qkv = jnp.dot(
        lax.all_gather(normed, "tensor", axis=0, tiled=True),
        weight_cols,
        preferred_element_type=jnp.float32,
    )
    qkv = qkv.reshape(qkv.shape[0], KV // tensor_count, GQ + 2, HD)
    return attend(qkv, q_gain, k_gain, lengths[0])


def project_kernel(counts, sources, tile, scal, *refs):
    blocks = len(counts)
    arrays = max(source[0] for source in sources) + 1
    rows_refs = refs[:blocks]
    pieces = refs[blocks : blocks + arrays]
    cos_ref, sin_ref, gain_ref, out = refs[blocks + arrays : blocks + arrays + 4]
    taken, held, made, row_sems, sems, out_sems = refs[blocks + arrays + 4 :]
    depth = taken.shape[1] // 16
    columns = made.shape[1]
    steps = columns // tile

    def copies(step):
        listed = []
        for index, (array, first, base, group, slot) in enumerate(sources):
            start = pl.multiple_of((scal[group] * 4 + scal[slot]) * depth, 16)
            low = base + step * tile
            listed.append(
                pltpu.make_async_copy(
                    pieces[array].at[first : first + depth, low : low + tile],
                    held.at[step % 2, pl.ds(start, depth), :],
                    sems.at[step % 2, index],
                )
            )
        return listed

    starts = [sum(counts[:n]) for n in range(blocks)]
    row_copies = [
        pltpu.make_async_copy(ref, taken.at[first : first + rows, :], row_sems.at[number])
        for number, (ref, first, rows) in enumerate(zip(rows_refs, starts, counts))
    ]
    out_copies = []
    for copy in copies(0) + row_copies:
        copy.start()
    for step in range(steps):
        if step + 1 < steps:
            for copy in copies(step + 1):
                copy.start()
        if step == 0:
            for copy in row_copies:
                copy.wait()
        for copy in copies(step):
            copy.wait()
        total = jnp.dot(taken[...], held[step % 2], preferred_element_type=jnp.float32)
        for number, (first, rows) in enumerate(zip(starts, counts)):
            place = pl.ds(pl.multiple_of(scal[12 + number], 128), rows)
            cosine = cos_ref[place, :]
            sine = sin_ref[place, :]
            for head in range(tile // HD):
                kind = (step * (tile // HD) + head) % (GQ + 2)
                vec = total[first : first + rows, head * HD : (head + 1) * HD]
                if kind <= GQ:
                    scale = lax.rsqrt(jnp.mean(vec * vec, axis=-1, keepdims=True) + 1e-06)
                    gain = gain_ref[0:1, :] if kind < GQ else gain_ref[1:2, :]
                    vec = vec * scale * gain
                    vec = vec * cosine + pltpu.roll(vec, HD // 2, 1) * sine
                at = step * tile + head * HD
                made[first : first + rows, at : at + HD] = vec.astype(made.dtype)
        at = slice(step * tile, (step + 1) * tile)
        out_copies.append(pltpu.make_async_copy(made.at[:, at], out.at[:, at], out_sems.at[step]))
        out_copies[-1].start()
    for copy in out_copies:
        copy.wait()


def project(rows_list, places, columns, spread_pieces, own_pieces, scal, cos, sin, gains):
    pieces, sources = [], []
    depth = rows_list[0].shape[1] // 16
    for slot, base, array in spread_pieces:
        sources += [(len(pieces), m * depth, base, 8 + m, slot) for m in range(4)]
        pieces.append(array)
    for slot, base, four in own_pieces:
        sources += [(len(pieces) + m, 0, base, 4 + m, slot) for m in range(4)]
        pieces += four
    counts = [r.shape[0] for r in rows_list]
    steps = 3
    tile = columns // steps
    count = sum(counts)
    width = rows_list[0].shape[1]
    scal = jnp.concatenate([scal, jnp.stack(places)]).astype(jnp.int32)
    vmem = pl.BlockSpec(memory_space=pltpu.VMEM)
    hbm = pl.BlockSpec(memory_space=pltpu.HBM)
    return pl.pallas_call(
        functools.partial(project_kernel, counts, sources, tile),
        out_shape=pltpu.HBM((count, columns), jnp.bfloat16),
        in_specs=[pl.BlockSpec(memory_space=pltpu.SMEM)]
        + [hbm] * (len(counts) + len(pieces))
        + [vmem] * 3,
        out_specs=hbm,
        scratch_shapes=[
            pltpu.VMEM((count, width), jnp.bfloat16),
            pltpu.VMEM((2, width, tile), jnp.bfloat16),
            pltpu.VMEM((count, columns), jnp.bfloat16),
            pltpu.SemaphoreType.DMA((len(counts),)),
            pltpu.SemaphoreType.DMA((2, 16)),
            pltpu.SemaphoreType.DMA((steps,)),
        ],
        compiler_params=pltpu.CompilerParams(vmem_limit_bytes=VMEM_BYTES),
        cost_estimate=pl.CostEstimate(
            flops=2 * count * width * columns,
            bytes_accessed=2 * (width * columns + count * (width + columns)),
            transcendentals=0,
        ),
        name="project",
    )(scal, *rows_list, *pieces, cos, sin, gains)


def attend_kernel(near_parts, far_parts, block, scal, *refs):
    near = refs[: len(near_parts)]
    far = refs[len(near_parts) : len(near_parts) + len(far_parts)]
    out, held, sems = refs[len(near_parts) + len(far_parts) :]
    middle = scal[0]
    length = scal[1]

    def fetch(sources, parts):
        copies = []
        for ref, blocks in zip(sources, parts):
            for first, rows, number in blocks:
                place = pl.ds(pl.multiple_of(scal[2 + number], 128), rows)
                copies.append(
                    pltpu.make_async_copy(
                        ref.at[first : first + rows, :], held.at[place, :], sems.at[number]
                    )
                )
        for copy in copies:
            copy.start()
        for copy in copies:
            copy.wait()

    @pl.when(middle == 1)
    def _():
        fetch(near, near_parts)

    @pl.when(middle == 0)
    def _():
        fetch(far, far_parts)

    total = held.shape[0]
    heads = held.shape[1] // ((GQ + 2) * HD)
    factor = LOG2E / float(HD) ** 0.5
    row = lax.broadcasted_iota(jnp.int32, (block, block), 0)
    col = lax.broadcasted_iota(jnp.int32, (block, block), 1)
    contract = (((1,), (1,)), ((), ()))
    for group in range(heads):
        base = group * (GQ + 2) * HD
        key_at = slice(base + GQ * HD, base + (GQ + 1) * HD)
        value_at = slice(base + (GQ + 1) * HD, base + (GQ + 2) * HD)

        @pl.loop(0, GQ)
        def _(j, base=base, key_at=key_at, value_at=value_at, group=group):
            query_at = pl.ds(pl.multiple_of(base + j * HD, HD), HD)
            out_at = pl.ds(pl.multiple_of((group * GQ + j) * HD, HD), HD)
            for step in range(total // block):
                low = step * block
                high = low + block
                query = held[low:high, query_at]
                last = lax.dot_general(
                    query, held[low:high, key_at], contract, preferred_element_type=jnp.float32
                )
                last = jnp.where((col <= row) & (col + low < length), last, -1e30)
                top = jnp.max(last, axis=-1, keepdims=True)
                if step:
                    rest = lax.dot_general(
                        query, held[:low, key_at], contract, preferred_element_type=jnp.float32
                    )
                    keys = lax.broadcasted_iota(jnp.int32, (1, low), 1)
                    rest = rest + jnp.where(keys < length, 0.0, -1e30)
                    top = jnp.maximum(top, jnp.max(rest, axis=-1, keepdims=True))
                shift = top * factor
                probs = jnp.exp2(last * factor - shift)
                norm = jnp.sum(probs, axis=-1, keepdims=True)
                value = jnp.dot(
                    probs.astype(jnp.bfloat16),
                    held[low:high, value_at],
                    preferred_element_type=jnp.float32,
                )
                if step:
                    probs = jnp.exp2(rest * factor - shift)
                    norm = norm + jnp.sum(probs, axis=-1, keepdims=True)
                    value = value + jnp.dot(
                        probs.astype(jnp.bfloat16),
                        held[:low, value_at],
                        preferred_element_type=jnp.float32,
                    )
                out[low:high, out_at] = (value / norm).astype(out.dtype)


def attend_blocks(near, far, near_parts, far_parts, places, middle, length):
    rows = sum(n.shape[0] for n in near)
    columns = near[0].shape[1]
    wide = columns // (GQ + 2) * GQ
    scal = jnp.stack([middle, length] + list(places)).astype(jnp.int32)
    hbm = pl.BlockSpec(memory_space=pltpu.HBM)
    return pl.pallas_call(
        functools.partial(attend_kernel, near_parts, far_parts, 256),
        out_shape=jax.ShapeDtypeStruct((rows, wide), jnp.bfloat16),
        in_specs=[pl.BlockSpec(memory_space=pltpu.SMEM)] + [hbm] * (len(near) + len(far)),
        out_specs=pl.BlockSpec(memory_space=pltpu.VMEM),
        scratch_shapes=[
            pltpu.VMEM((rows, columns), jnp.bfloat16),
            pltpu.SemaphoreType.DMA((len(places),)),
        ],
        compiler_params=pltpu.CompilerParams(vmem_limit_bytes=VMEM_BYTES),
        cost_estimate=pl.CostEstimate(
            flops=4 * rows * rows * wide,
            bytes_accessed=2 * rows * (columns + wide),
            transcendentals=rows * rows * wide // HD // 2,
        ),
        name="attend",
    )(scal, *near, *far)


def after(x, *earlier):
    return lax.optimization_barrier((x,) + earlier)[0]


def four_planes(tokens, w_qkv, norm_gain, q_gain, k_gain, lengths):
    t = lax.axis_index("tensor")
    f = lax.axis_index("fsdp")
    rows = tokens.shape[0]
    columns = w_qkv.shape[1] // 4
    side = t // 2
    end = 3 * side
    mid = 1 + side
    far_end = 3 * (1 - side)
    far_mid = 2 - side

    def slab(block):
        return lax.dynamic_slice(w_qkv, (0, block * columns), (w_qkv.shape[0], columns))

    def across(x, pairs):
        return lax.ppermute(x, "tensor", pairs)

    def beside(x, bit):
        return lax.ppermute(x, "fsdp", [(i, i ^ bit) for i in range(4)])

    def spread(x):
        return lax.all_gather(x, "fsdp", axis=0, tiled=True)

    inward = [(0, 1), (3, 2)]
    swap = [(1, 2), (2, 1)]
    far = [(0, 2), (3, 1)]
    outward = [(1, 0), (2, 3)]

    same = jnp.concatenate([slab(end), slab(mid)], axis=1)
    other = jnp.concatenate([slab(far_end), slab(far_mid)], axis=1)
    normed = head_norm(tokens.astype(jnp.float32), norm_gain).astype(jnp.bfloat16)

    def core_pair(piece, over):
        return [piece, over, beside(piece, 1), beside(over, 1)]

    own = spread(same)
    swap_w = across(other, swap)
    far_w = across(other, far)
    end_w = across(same, inward)
    rows_b = across(after(normed, swap_w), swap)
    rows_a = across(after(normed, swap_w), inward)
    over_swap = beside(after(swap_w, rows_b), 2)
    far_e, end_e = far_w[:, :columns], end_w[:, :columns]
    over_far_e = beside(far_e, 2)
    over_end_e = beside(after(end_e, over_swap), 2)
    rows_c = across(after(rows_a, over_end_e), swap)

    swap_pieces = core_pair(swap_w, over_swap)
    end_pieces = (
        [(0, 0, own)],
        [
            (1, 0, swap_pieces),
            (2, 0, core_pair(far_e, over_far_e)),
            (3, 0, core_pair(end_e, over_end_e)),
        ],
    )
    mid_pieces = (
        [
            (0, columns, own),
            (2, 0, spread(far_w[:, columns:])),
            (3, 0, spread(end_w[:, columns:])),
        ],
        [(1, columns, swap_pieces)],
    )
    scal = jnp.stack(
        [mid, far_mid, far_end, end]
        + [jnp.bitwise_xor(f, m) for m in (0, 2, 1, 3)]
        + [jnp.int32(m) for m in range(4)]
    )

    positions = jnp.arange(4 * rows, dtype=jnp.int32)
    angle = angles(positions)
    cos = jnp.concatenate([jnp.cos(angle)] * 2, axis=1)
    sin = jnp.concatenate([-jnp.sin(angle), jnp.sin(angle)], axis=1)
    gains = jnp.stack([q_gain, k_gain])

    blocks = [normed, rows_b, rows_a, rows_c]
    places = [mid * rows, far_mid * rows, end * rows, far_end * rows]

    def run(picked, pieces):
        return project(
            [blocks[i] for i in picked],
            [places[i] for i in picked],
            columns,
            *pieces,
            scal,
            cos,
            sin,
            gains,
        )

    sent = [across(run(picked, end_pieces), outward) for picked in ([0, 1], [2, 3])]
    near = [run([0, 1, 2, 3], mid_pieces)]
    near_parts = [[(i * rows, rows, i) for i in range(4)]]
    far_parts = [[(i * rows, rows, 2 * n + i) for i in range(2)] for n in range(2)]
    middle = jnp.where((t == 1) | (t == 2), 1, 0)
    return attend_blocks(near, sent, near_parts, far_parts, places, middle, lengths[0])


def solution(mesh):
    placed = (
        P(("groups", "fsdp", "tensor"), None),
        P(("groups", "fsdp", "tensor"), None),
        P(),
        P(),
        P(),
        P(("groups", "fsdp")),
    )
    sizes = dict(mesh.shape)
    body = four_planes if sizes["tensor"] == 4 and sizes["fsdp"] == 4 else any_mesh
    return jax.shard_map(
        body,
        mesh=mesh,
        in_specs=placed,
        out_specs=P(("groups", "fsdp"), "tensor"),
        check_vma=False,
    )
```

```python
import functools
import jax
import jax.numpy as jnp
from jax import lax
from jax.experimental import pallas as pl
from jax.experimental.pallas import tpu as pltpu
from jax.sharding import PartitionSpec as P

KV = 8
HD = 128
GQ = 4
LOG2E = 1.4426950408889634
VMEM_BYTES = 48 * 1024 * 1024


def head_norm(vec, gain):
    scale = lax.rsqrt(jnp.mean(vec * vec, axis=-1, keepdims=True) + 1e-06)
    return vec * scale * gain


def angles(positions):
    half = HD // 2
    freqs = 1000000.0 ** (-2.0 * jnp.arange(half, dtype=jnp.float32) / HD)
    return positions.astype(jnp.float32)[:, None] * freqs[None, :]


def rotate(vec, positions):
    half = vec.shape[-1] // 2
    angle = angles(positions)
    cosine = jnp.cos(angle)[:, None, None, :]
    sine = jnp.sin(angle)[:, None, None, :]
    first = vec[..., :half]
    second = vec[..., half:]
    return jnp.concatenate(
        [first * cosine - second * sine, second * cosine + first * sine], axis=-1
    )


def attend(qkv, q_gain, k_gain, length):
    rows = qkv.shape[0]
    group = qkv.shape[2] - 2
    positions = jnp.arange(rows, dtype=jnp.int32)
    query = rotate(head_norm(qkv[:, :, :group], q_gain), positions).astype(jnp.bfloat16)
    keyed = rotate(head_norm(qkv[:, :, group : group + 1], k_gain), positions)[:, :, 0].astype(
        jnp.bfloat16
    )
    value = qkv[:, :, group + 1].astype(jnp.bfloat16)
    scores = jnp.einsum(
        "ikgd,jkd->kgij", query, keyed, preferred_element_type=jnp.float32
    ) / jnp.sqrt(jnp.float32(qkv.shape[3]))
    allowed = (positions[None, :] <= positions[:, None]) & (positions[None, :] < length)
    scores = jnp.where(allowed[None, None], scores, jnp.float32(-1e30))
    top = jnp.max(scores, axis=-1, keepdims=True)
    weights = jnp.exp(scores - top)
    probs = (weights / jnp.sum(weights, axis=-1, keepdims=True)).astype(jnp.bfloat16)
    out = jnp.einsum("kgij,jkd->ikgd", probs, value, preferred_element_type=jnp.float32)
    return out.reshape(rows, -1).astype(jnp.bfloat16)


def any_mesh(tokens, w_qkv, norm_gain, q_gain, k_gain, lengths):
    tensor_count = lax.axis_size("tensor")
    moved = lax.all_to_all(w_qkv, "tensor", split_axis=1, concat_axis=0, tiled=True)
    weight_cols = lax.all_gather(moved, "fsdp", axis=0, tiled=True)
    normed = head_norm(tokens.astype(jnp.float32), norm_gain).astype(jnp.bfloat16)
    qkv = jnp.dot(
        lax.all_gather(normed, "tensor", axis=0, tiled=True),
        weight_cols,
        preferred_element_type=jnp.float32,
    )
    qkv = qkv.reshape(qkv.shape[0], KV // tensor_count, GQ + 2, HD)
    return attend(qkv, q_gain, k_gain, lengths[0])


def project_kernel(counts, sources, tile, scal, *refs):
    blocks = len(counts)
    arrays = max(source[0] for source in sources) + 1
    middle_rows, end_rows = refs[:blocks], refs[blocks : 2 * blocks]
    refs = refs[2 * blocks :]
    pieces = refs[:arrays]
    cos_ref, sin_ref, gain_ref, out = refs[arrays : arrays + 4]
    taken, held, made, row_sems, sems, out_sems = refs[arrays + 4 :]
    depth = taken.shape[1] // 16
    columns = made.shape[1]
    steps = columns // tile

    def copies(step):
        listed = []
        for index, (array, first, group, slot) in enumerate(sources):
            start = pl.multiple_of((scal[group] * 4 + scal[slot]) * depth, 16)
            low = step * tile
            listed.append(
                pltpu.make_async_copy(
                    pieces[array].at[first : first + depth, low : low + tile],
                    held.at[step % 2, pl.ds(start, depth), :],
                    sems.at[step % 2, index],
                )
            )
        return listed

    starts = [sum(counts[:n]) for n in range(blocks)]
    row_copies = [
        [
            pltpu.make_async_copy(ref, taken.at[first : first + rows, :], row_sems.at[number])
            for ref in (middle_rows[number], end_rows[number])
        ]
        for number, (first, rows) in enumerate(zip(starts, counts))
    ]
    out_copies = []
    for copy in copies(0):
        copy.start()
    for in_middle, in_end in row_copies:
        pl.when(scal[8] == 1)(in_middle.start)
        pl.when(scal[8] == 0)(in_end.start)
    for step in range(steps):
        if step + 1 < steps:
            for copy in copies(step + 1):
                copy.start()
        if step == 0:
            for in_middle, _ in row_copies:
                in_middle.wait()
        for copy in copies(step):
            copy.wait()
        total = jnp.dot(taken[...], held[step % 2], preferred_element_type=jnp.float32)
        for number, (first, rows) in enumerate(zip(starts, counts)):
            place = pl.ds(pl.multiple_of(scal[9 + number], 128), rows)
            cosine = cos_ref[place, :]
            sine = sin_ref[place, :]
            for head in range(tile // HD):
                kind = (step * (tile // HD) + head) % (GQ + 2)
                vec = total[first : first + rows, head * HD : (head + 1) * HD]
                if kind <= GQ:
                    scale = lax.rsqrt(jnp.mean(vec * vec, axis=-1, keepdims=True) + 1e-06)
                    gain = gain_ref[0:1, :] if kind < GQ else gain_ref[1:2, :]
                    vec = vec * scale * gain
                    vec = vec * cosine + pltpu.roll(vec, HD // 2, 1) * sine
                at = step * tile + head * HD
                made[first : first + rows, at : at + HD] = vec.astype(made.dtype)
        at = slice(step * tile, (step + 1) * tile)
        out_copies.append(pltpu.make_async_copy(made.at[:, at], out.at[:, at], out_sems.at[step]))
        out_copies[-1].start()
    for copy in out_copies:
        copy.wait()


def project(rows_list, places, pieces, scal, cos, sin, gains):
    depth = rows_list[0][0].shape[1] // 16
    columns = pieces[0].shape[1]
    sources = [(n, m * depth, 4 + m, n) for n in range(4) for m in range(4)]
    counts = [r.shape[0] for r, _ in rows_list]
    steps = 3
    tile = columns // steps
    count = sum(counts)
    width = rows_list[0][0].shape[1]
    scal = jnp.concatenate([scal, jnp.stack(places)]).astype(jnp.int32)
    vmem = pl.BlockSpec(memory_space=pltpu.VMEM)
    hbm = pl.BlockSpec(memory_space=pltpu.HBM)
    return pl.pallas_call(
        functools.partial(project_kernel, counts, sources, tile),
        out_shape=pltpu.HBM((count, columns), jnp.bfloat16),
        in_specs=[pl.BlockSpec(memory_space=pltpu.SMEM)]
        + [hbm] * (2 * len(counts) + len(pieces))
        + [vmem] * 3,
        out_specs=hbm,
        scratch_shapes=[
            pltpu.VMEM((count, width), jnp.bfloat16),
            pltpu.VMEM((2, width, tile), jnp.bfloat16),
            pltpu.VMEM((count, columns), jnp.bfloat16),
            pltpu.SemaphoreType.DMA((len(counts),)),
            pltpu.SemaphoreType.DMA((2, 16)),
            pltpu.SemaphoreType.DMA((steps,)),
        ],
        compiler_params=pltpu.CompilerParams(vmem_limit_bytes=VMEM_BYTES),
        cost_estimate=pl.CostEstimate(
            flops=2 * count * width * columns,
            bytes_accessed=2 * (width * columns + count * (width + columns)),
            transcendentals=0,
        ),
        name="project",
    )(scal, *[r for r, _ in rows_list], *[r for _, r in rows_list], *pieces, cos, sin, gains)


def attend_kernel(parts, block, scal, *refs):
    out, held, sems = refs[len(parts) :]
    length = scal[0]

    copies = []
    for ref, blocks in zip(refs, parts):
        for first, rows, number in blocks:
            place = pl.ds(pl.multiple_of(scal[1 + number], 128), rows)
            copies.append(
                pltpu.make_async_copy(
                    ref.at[first : first + rows, :], held.at[place, :], sems.at[number]
                )
            )
    for copy in copies:
        copy.start()
    for copy in copies:
        copy.wait()

    total = held.shape[0]
    heads = held.shape[1] // ((GQ + 2) * HD)
    factor = LOG2E / float(HD) ** 0.5
    row = lax.broadcasted_iota(jnp.int32, (block, block), 0)
    col = lax.broadcasted_iota(jnp.int32, (block, block), 1)
    contract = (((1,), (1,)), ((), ()))
    for group in range(heads):
        base = group * (GQ + 2) * HD
        key_at = slice(base + GQ * HD, base + (GQ + 1) * HD)
        value_at = slice(base + (GQ + 1) * HD, base + (GQ + 2) * HD)

        @pl.loop(0, GQ)
        def _(j, base=base, key_at=key_at, value_at=value_at, group=group):
            query_at = pl.ds(pl.multiple_of(base + j * HD, HD), HD)
            out_at = pl.ds(pl.multiple_of((group * GQ + j) * HD, HD), HD)
            for step in range(total // block):
                low = step * block
                high = low + block
                query = held[low:high, query_at]
                last = lax.dot_general(
                    query, held[low:high, key_at], contract, preferred_element_type=jnp.float32
                )
                last = jnp.where((col <= row) & (col + low < length), last, -1e30)
                top = jnp.max(last, axis=-1, keepdims=True)
                if step:
                    rest = lax.dot_general(
                        query, held[:low, key_at], contract, preferred_element_type=jnp.float32
                    )
                    keys = lax.broadcasted_iota(jnp.int32, (1, low), 1)
                    rest = rest + jnp.where(keys < length, 0.0, -1e30)
                    top = jnp.maximum(top, jnp.max(rest, axis=-1, keepdims=True))
                shift = top * factor
                probs = jnp.exp2(last * factor - shift)
                norm = jnp.sum(probs, axis=-1, keepdims=True)
                value = jnp.dot(
                    probs.astype(jnp.bfloat16),
                    held[low:high, value_at],
                    preferred_element_type=jnp.float32,
                )
                if step:
                    probs = jnp.exp2(rest * factor - shift)
                    norm = norm + jnp.sum(probs, axis=-1, keepdims=True)
                    value = value + jnp.dot(
                        probs.astype(jnp.bfloat16),
                        held[:low, value_at],
                        preferred_element_type=jnp.float32,
                    )
                out[low:high, out_at] = (value / norm).astype(out.dtype)


def attend_blocks(arrays, parts, places, length):
    rows = sum(a.shape[0] for a in arrays)
    columns = arrays[0].shape[1]
    wide = columns // (GQ + 2) * GQ
    scal = jnp.stack([length] + list(places)).astype(jnp.int32)
    hbm = pl.BlockSpec(memory_space=pltpu.HBM)
    return pl.pallas_call(
        functools.partial(attend_kernel, parts, 256),
        out_shape=jax.ShapeDtypeStruct((rows, wide), jnp.bfloat16),
        in_specs=[pl.BlockSpec(memory_space=pltpu.SMEM)] + [hbm] * len(arrays),
        out_specs=pl.BlockSpec(memory_space=pltpu.VMEM),
        scratch_shapes=[
            pltpu.VMEM((rows, columns), jnp.bfloat16),
            pltpu.SemaphoreType.DMA((len(places),)),
        ],
        compiler_params=pltpu.CompilerParams(vmem_limit_bytes=VMEM_BYTES),
        cost_estimate=pl.CostEstimate(
            flops=4 * rows * rows * wide,
            bytes_accessed=2 * rows * (columns + wide),
            transcendentals=rows * rows * wide // HD // 2,
        ),
        name="attend",
    )(scal, *arrays)


def after(x, *earlier):
    return lax.optimization_barrier((x,) + earlier)[0]


def four_planes(tokens, w_qkv, norm_gain, q_gain, k_gain, lengths):
    t = lax.axis_index("tensor")
    rows = tokens.shape[0]
    half = rows // 2
    columns = w_qkv.shape[1] // 4
    side = t // 2
    far_end = 3 * (1 - side)
    far_mid = 2 - side

    def slab(block):
        return lax.dynamic_slice(w_qkv, (0, block * columns), (w_qkv.shape[0], columns))

    def across(x, pairs):
        return lax.ppermute(x, "tensor", pairs)

    def exchange(x, bits):
        return across(x, [(i, i ^ bits) for i in range(4)])

    def spread(x):
        return lax.all_gather(x, "fsdp", axis=0, tiled=True)

    swap = [(1, 2), (2, 1)]
    far = [(0, 2), (3, 1)]
    outward = [(1, 0), (2, 3)]

    planes = [t] + [jnp.bitwise_xor(t, m) for m in (1, 2, 3)]
    own, out1, out2, out3 = [slab(p) for p in planes]
    normed = head_norm(tokens.astype(jnp.float32), norm_gain).astype(jnp.bfloat16)
    first, second = normed[:half], normed[half:]

    in2, in3, in1 = exchange(out2, 2), exchange(out3, 3), exchange(out1, 1)
    in1, in2, in3 = lax.optimization_barrier((in1, in2, in3))
    paired = exchange(normed, 1)
    swap1 = across(first, swap)
    swap2 = across(after(second, in1), swap)
    far1 = across(after(first, in2), far)
    far2 = across(after(second, in3), far)
    on1, on2 = across(swap1, outward), across(swap2, outward)
    on3, on4 = across(far1, outward), across(far2, outward)

    pieces = [spread(x) for x in (own, in1, in2, in3)]
    middle = jnp.where((t == 1) | (t == 2), 1, 0)
    scal = jnp.stack(planes + [jnp.int32(m) for m in range(4)] + [middle])

    positions = jnp.arange(4 * rows, dtype=jnp.int32)
    angle = angles(positions)
    cos = jnp.concatenate([jnp.cos(angle)] * 2, axis=1)
    sin = jnp.concatenate([-jnp.sin(angle), jnp.sin(angle)], axis=1)
    gains = jnp.stack([q_gain, k_gain])

    calls = [
        [((normed, normed), t * rows), ((paired, paired), planes[1] * rows)],
        [((swap1, on1), far_mid * rows), ((swap2, on2), far_mid * rows + half)],
        [((far1, on3), far_end * rows), ((far2, on4), far_end * rows + half)],
    ]
    made, parts, places = [], [], []
    for call in calls:
        listed, first_row = [], 0
        for (block, _), place in call:
            listed.append((first_row, block.shape[0], len(places)))
            first_row += block.shape[0]
            places.append(place)
        parts.append(listed)
        made.append(
            project([b for b, _ in call], [p for _, p in call], pieces, scal, cos, sin, gains)
        )
    return attend_blocks(made, parts, places, lengths[0])


def solution(mesh):
    placed = (
        P(("groups", "fsdp", "tensor"), None),
        P(("groups", "fsdp", "tensor"), None),
        P(),
        P(),
        P(),
        P(("groups", "fsdp")),
    )
    sizes = dict(mesh.shape)
    body = four_planes if sizes["tensor"] == 4 and sizes["fsdp"] == 4 else any_mesh
    return jax.shard_map(
        body,
        mesh=mesh,
        in_specs=placed,
        out_specs=P(("groups", "fsdp"), "tensor"),
        check_vma=False,
    )
```

```python
import functools
import jax
import jax.numpy as jnp
from jax import lax
from jax.experimental import pallas as pl
from jax.experimental.pallas import tpu as pltpu
from jax.sharding import PartitionSpec as P

KV = 8
HD = 128
GQ = 4
LOG2E = 1.4426950408889634
VMEM_BYTES = 48 * 1024 * 1024


def head_norm(vec, gain):
    scale = lax.rsqrt(jnp.mean(vec * vec, axis=-1, keepdims=True) + 1e-06)
    return vec * scale * gain


def angles(positions):
    half = HD // 2
    freqs = 1000000.0 ** (-2.0 * jnp.arange(half, dtype=jnp.float32) / HD)
    return positions.astype(jnp.float32)[:, None] * freqs[None, :]


def rotate(vec, positions):
    half = vec.shape[-1] // 2
    angle = angles(positions)
    cosine = jnp.cos(angle)[:, None, None, :]
    sine = jnp.sin(angle)[:, None, None, :]
    first = vec[..., :half]
    second = vec[..., half:]
    return jnp.concatenate(
        [first * cosine - second * sine, second * cosine + first * sine], axis=-1
    )


def attend(qkv, q_gain, k_gain, length):
    rows = qkv.shape[0]
    group = qkv.shape[2] - 2
    positions = jnp.arange(rows, dtype=jnp.int32)
    query = rotate(head_norm(qkv[:, :, :group], q_gain), positions).astype(jnp.bfloat16)
    keyed = rotate(head_norm(qkv[:, :, group : group + 1], k_gain), positions)[:, :, 0].astype(
        jnp.bfloat16
    )
    value = qkv[:, :, group + 1].astype(jnp.bfloat16)
    scores = jnp.einsum(
        "ikgd,jkd->kgij", query, keyed, preferred_element_type=jnp.float32
    ) / jnp.sqrt(jnp.float32(qkv.shape[3]))
    allowed = (positions[None, :] <= positions[:, None]) & (positions[None, :] < length)
    scores = jnp.where(allowed[None, None], scores, jnp.float32(-1e30))
    top = jnp.max(scores, axis=-1, keepdims=True)
    weights = jnp.exp(scores - top)
    probs = (weights / jnp.sum(weights, axis=-1, keepdims=True)).astype(jnp.bfloat16)
    out = jnp.einsum("kgij,jkd->ikgd", probs, value, preferred_element_type=jnp.float32)
    return out.reshape(rows, -1).astype(jnp.bfloat16)


def any_mesh(tokens, w_qkv, norm_gain, q_gain, k_gain, lengths):
    tensor_count = lax.axis_size("tensor")
    moved = lax.all_to_all(w_qkv, "tensor", split_axis=1, concat_axis=0, tiled=True)
    weight_cols = lax.all_gather(moved, "fsdp", axis=0, tiled=True)
    normed = head_norm(tokens.astype(jnp.float32), norm_gain).astype(jnp.bfloat16)
    qkv = jnp.dot(
        lax.all_gather(normed, "tensor", axis=0, tiled=True),
        weight_cols,
        preferred_element_type=jnp.float32,
    )
    qkv = qkv.reshape(qkv.shape[0], KV // tensor_count, GQ + 2, HD)
    return attend(qkv, q_gain, k_gain, lengths[0])


def project_kernel(counts, sources, tile, scal, *refs):
    blocks = len(counts)
    arrays = max(source[0] for source in sources) + 1
    middle_rows, end_rows = refs[:blocks], refs[blocks : 2 * blocks]
    refs = refs[2 * blocks :]
    pieces = refs[:arrays]
    cos_ref, sin_ref, gain_ref, out = refs[arrays : arrays + 4]
    taken, held, made, row_sems, sems, out_sems = refs[arrays + 4 :]
    depth = taken.shape[1] // 16
    columns = made.shape[1]
    steps = columns // tile

    def copies(step):
        listed = []
        for index, (array, first, group, slot) in enumerate(sources):
            start = pl.multiple_of((scal[group] * 4 + scal[slot]) * depth, 16)
            low = step * tile
            listed.append(
                pltpu.make_async_copy(
                    pieces[array].at[first : first + depth, low : low + tile],
                    held.at[step % 2, pl.ds(start, depth), :],
                    sems.at[step % 2, index],
                )
            )
        return listed

    starts = [sum(counts[:n]) for n in range(blocks)]
    row_copies = [
        [
            pltpu.make_async_copy(ref, taken.at[first : first + rows, :], row_sems.at[number])
            for ref in (middle_rows[number], end_rows[number])
        ]
        for number, (first, rows) in enumerate(zip(starts, counts))
    ]
    out_copies = []
    for copy in copies(0):
        copy.start()
    for in_middle, in_end in row_copies:
        pl.when(scal[8] == 1)(in_middle.start)
        pl.when(scal[8] == 0)(in_end.start)
    for step in range(steps):
        if step + 1 < steps:
            for copy in copies(step + 1):
                copy.start()
        if step == 0:
            for in_middle, _ in row_copies:
                in_middle.wait()
        for copy in copies(step):
            copy.wait()
        total = jnp.dot(taken[...], held[step % 2], preferred_element_type=jnp.float32)
        for number, (first, rows) in enumerate(zip(starts, counts)):
            place = pl.ds(pl.multiple_of(scal[9 + number], 128), rows)
            cosine = cos_ref[place, :]
            sine = sin_ref[place, :]
            for head in range(tile // HD):
                kind = (step * (tile // HD) + head) % (GQ + 2)
                vec = total[first : first + rows, head * HD : (head + 1) * HD]
                if kind <= GQ:
                    scale = lax.rsqrt(jnp.mean(vec * vec, axis=-1, keepdims=True) + 1e-06)
                    gain = gain_ref[0:1, :] if kind < GQ else gain_ref[1:2, :]
                    vec = vec * scale * gain
                    vec = vec * cosine + pltpu.roll(vec, HD // 2, 1) * sine
                at = step * tile + head * HD
                made[first : first + rows, at : at + HD] = vec.astype(made.dtype)
        at = slice(step * tile, (step + 1) * tile)
        out_copies.append(pltpu.make_async_copy(made.at[:, at], out.at[:, at], out_sems.at[step]))
        out_copies[-1].start()
    for copy in out_copies:
        copy.wait()


def project(rows_list, places, pieces, scal, cos, sin, gains):
    depth = rows_list[0][0].shape[1] // 16
    columns = pieces[0].shape[1]
    sources = [(n, m * depth, 4 + m, n) for n in range(4) for m in range(4)]
    counts = [r.shape[0] for r, _ in rows_list]
    steps = 3
    tile = columns // steps
    count = sum(counts)
    width = rows_list[0][0].shape[1]
    scal = jnp.concatenate([scal, jnp.stack(places)]).astype(jnp.int32)
    vmem = pl.BlockSpec(memory_space=pltpu.VMEM)
    hbm = pl.BlockSpec(memory_space=pltpu.HBM)
    return pl.pallas_call(
        functools.partial(project_kernel, counts, sources, tile),
        out_shape=pltpu.HBM((count, columns), jnp.bfloat16),
        in_specs=[pl.BlockSpec(memory_space=pltpu.SMEM)]
        + [hbm] * (2 * len(counts) + len(pieces))
        + [vmem] * 3,
        out_specs=hbm,
        scratch_shapes=[
            pltpu.VMEM((count, width), jnp.bfloat16),
            pltpu.VMEM((2, width, tile), jnp.bfloat16),
            pltpu.VMEM((count, columns), jnp.bfloat16),
            pltpu.SemaphoreType.DMA((len(counts),)),
            pltpu.SemaphoreType.DMA((2, 16)),
            pltpu.SemaphoreType.DMA((steps,)),
        ],
        compiler_params=pltpu.CompilerParams(vmem_limit_bytes=VMEM_BYTES),
        cost_estimate=pl.CostEstimate(
            flops=2 * count * width * columns,
            bytes_accessed=2 * (width * columns + count * (width + columns)),
            transcendentals=0,
        ),
        name="project",
    )(scal, *[r for r, _ in rows_list], *[r for _, r in rows_list], *pieces, cos, sin, gains)


def attend_kernel(parts, block, scal, *refs):
    out, held, sems = refs[len(parts) :]
    length = scal[0]

    copies = []
    for ref, blocks in zip(refs, parts):
        for first, rows, number in blocks:
            place = pl.ds(pl.multiple_of(scal[1 + number], 128), rows)
            copies.append(
                pltpu.make_async_copy(
                    ref.at[first : first + rows, :], held.at[place, :], sems.at[number]
                )
            )
    for copy in copies:
        copy.start()
    for copy in copies:
        copy.wait()

    total = held.shape[0]
    heads = held.shape[1] // ((GQ + 2) * HD)
    factor = LOG2E / float(HD) ** 0.5
    row = lax.broadcasted_iota(jnp.int32, (block, block), 0)
    col = lax.broadcasted_iota(jnp.int32, (block, block), 1)
    contract = (((1,), (1,)), ((), ()))
    for group in range(heads):
        base = group * (GQ + 2) * HD
        key_at = slice(base + GQ * HD, base + (GQ + 1) * HD)
        value_at = slice(base + (GQ + 1) * HD, base + (GQ + 2) * HD)

        @pl.loop(0, GQ)
        def _(j, base=base, key_at=key_at, value_at=value_at, group=group):
            query_at = pl.ds(pl.multiple_of(base + j * HD, HD), HD)
            out_at = pl.ds(pl.multiple_of((group * GQ + j) * HD, HD), HD)
            for step in range(total // block):
                low = step * block
                high = low + block
                query = held[low:high, query_at]
                last = lax.dot_general(
                    query, held[low:high, key_at], contract, preferred_element_type=jnp.float32
                )
                last = jnp.where((col <= row) & (col + low < length), last, -1e30)
                top = jnp.max(last, axis=-1, keepdims=True)
                if step:
                    rest = lax.dot_general(
                        query, held[:low, key_at], contract, preferred_element_type=jnp.float32
                    )
                    keys = lax.broadcasted_iota(jnp.int32, (1, low), 1)
                    rest = rest + jnp.where(keys < length, 0.0, -1e30)
                    top = jnp.maximum(top, jnp.max(rest, axis=-1, keepdims=True))
                shift = top * factor
                probs = jnp.exp2(last * factor - shift)
                norm = jnp.sum(probs, axis=-1, keepdims=True)
                value = jnp.dot(
                    probs.astype(jnp.bfloat16),
                    held[low:high, value_at],
                    preferred_element_type=jnp.float32,
                )
                if step:
                    probs = jnp.exp2(rest * factor - shift)
                    norm = norm + jnp.sum(probs, axis=-1, keepdims=True)
                    value = value + jnp.dot(
                        probs.astype(jnp.bfloat16),
                        held[:low, value_at],
                        preferred_element_type=jnp.float32,
                    )
                out[low:high, out_at] = (value / norm).astype(out.dtype)


def attend_blocks(arrays, parts, places, length):
    rows = sum(a.shape[0] for a in arrays)
    columns = arrays[0].shape[1]
    wide = columns // (GQ + 2) * GQ
    scal = jnp.stack([length] + list(places)).astype(jnp.int32)
    hbm = pl.BlockSpec(memory_space=pltpu.HBM)
    return pl.pallas_call(
        functools.partial(attend_kernel, parts, 256),
        out_shape=jax.ShapeDtypeStruct((rows, wide), jnp.bfloat16),
        in_specs=[pl.BlockSpec(memory_space=pltpu.SMEM)] + [hbm] * len(arrays),
        out_specs=pl.BlockSpec(memory_space=pltpu.VMEM),
        scratch_shapes=[
            pltpu.VMEM((rows, columns), jnp.bfloat16),
            pltpu.SemaphoreType.DMA((len(places),)),
        ],
        compiler_params=pltpu.CompilerParams(vmem_limit_bytes=VMEM_BYTES),
        cost_estimate=pl.CostEstimate(
            flops=4 * rows * rows * wide,
            bytes_accessed=2 * rows * (columns + wide),
            transcendentals=rows * rows * wide // HD // 2,
        ),
        name="attend",
    )(scal, *arrays)


def after(x, *earlier):
    return lax.optimization_barrier((x,) + earlier)[0]


def four_planes(tokens, w_qkv, norm_gain, q_gain, k_gain, lengths):
    t = lax.axis_index("tensor")
    rows = tokens.shape[0]
    half = rows // 2
    columns = w_qkv.shape[1] // 4
    side = t // 2
    far_end = 3 * (1 - side)
    far_mid = 2 - side

    def slab(block):
        return lax.dynamic_slice(w_qkv, (0, block * columns), (w_qkv.shape[0], columns))

    def across(x, pairs):
        return lax.ppermute(x, "tensor", pairs)

    def exchange(x, bits):
        return across(x, [(i, i ^ bits) for i in range(4)])

    def spread(x):
        return lax.all_gather(x, "fsdp", axis=0, tiled=True)

    swap = [(1, 2), (2, 1)]
    far = [(0, 2), (3, 1)]
    outward = [(1, 0), (2, 3)]

    planes = [t] + [jnp.bitwise_xor(t, m) for m in (1, 2, 3)]
    own, out1, out2, out3 = [slab(p) for p in planes]
    normed = head_norm(tokens.astype(jnp.float32), norm_gain).astype(jnp.bfloat16)
    first, second = normed[:half], normed[half:]

    in2, in3, in1 = exchange(out2, 2), exchange(out3, 3), exchange(out1, 1)
    pair1 = exchange(first, 1)
    in1, in2, in3, pair1 = lax.optimization_barrier((in1, in2, in3, pair1))
    pair2 = exchange(after(second, in1), 1)
    swap1 = across(after(first, in1), swap)
    swap2 = across(after(second, in1), swap)
    far1 = across(after(first, swap1, pair2), far)
    on1, on2 = across(swap1, outward), across(swap2, outward)
    far2 = across(after(second, swap2, on1), far)
    on3, on4 = across(far1, outward), across(far2, outward)

    pieces = [spread(x) for x in (own, in1, in2, in3)]
    middle = jnp.where((t == 1) | (t == 2), 1, 0)
    scal = jnp.stack(planes + [jnp.int32(m) for m in range(4)] + [middle])

    positions = jnp.arange(4 * rows, dtype=jnp.int32)
    angle = angles(positions)
    cos = jnp.concatenate([jnp.cos(angle)] * 2, axis=1)
    sin = jnp.concatenate([-jnp.sin(angle), jnp.sin(angle)], axis=1)
    gains = jnp.stack([q_gain, k_gain])

    calls = [
        [
            ((normed, normed), t * rows),
            ((pair1, pair1), planes[1] * rows),
            ((pair2, pair2), planes[1] * rows + half),
        ],
        [((swap1, on1), far_mid * rows), ((swap2, on2), far_mid * rows + half)],
        [((far1, on3), far_end * rows)],
        [((far2, on4), far_end * rows + half)],
    ]
    made, parts, places = [], [], []
    for call in calls:
        listed, first_row = [], 0
        for (block, _), place in call:
            listed.append((first_row, block.shape[0], len(places)))
            first_row += block.shape[0]
            places.append(place)
        parts.append(listed)
        made.append(
            project([b for b, _ in call], [p for _, p in call], pieces, scal, cos, sin, gains)
        )
    return attend_blocks(made, parts, places, lengths[0])


def solution(mesh):
    placed = (
        P(("groups", "fsdp", "tensor"), None),
        P(("groups", "fsdp", "tensor"), None),
        P(),
        P(),
        P(),
        P(("groups", "fsdp")),
    )
    sizes = dict(mesh.shape)
    body = four_planes if sizes["tensor"] == 4 and sizes["fsdp"] == 4 else any_mesh
    return jax.shard_map(
        body,
        mesh=mesh,
        in_specs=placed,
        out_specs=P(("groups", "fsdp"), "tensor"),
        check_vma=False,
    )
```

```python
import functools
import jax
import jax.numpy as jnp
from jax import lax
from jax.experimental import pallas as pl
from jax.experimental.pallas import tpu as pltpu
from jax.sharding import PartitionSpec as P

KV = 8
HD = 128
GQ = 4
LOG2E = 1.4426950408889634
VMEM_BYTES = 48 * 1024 * 1024


def head_norm(vec, gain):
    scale = lax.rsqrt(jnp.mean(vec * vec, axis=-1, keepdims=True) + 1e-06)
    return vec * scale * gain


def angles(positions):
    half = HD // 2
    freqs = 1000000.0 ** (-2.0 * jnp.arange(half, dtype=jnp.float32) / HD)
    return positions.astype(jnp.float32)[:, None] * freqs[None, :]


def rotate(vec, positions):
    half = vec.shape[-1] // 2
    angle = angles(positions)
    cosine = jnp.cos(angle)[:, None, None, :]
    sine = jnp.sin(angle)[:, None, None, :]
    first = vec[..., :half]
    second = vec[..., half:]
    return jnp.concatenate(
        [first * cosine - second * sine, second * cosine + first * sine], axis=-1
    )


def attend(qkv, q_gain, k_gain, length):
    rows = qkv.shape[0]
    group = qkv.shape[2] - 2
    positions = jnp.arange(rows, dtype=jnp.int32)
    query = rotate(head_norm(qkv[:, :, :group], q_gain), positions).astype(jnp.bfloat16)
    keyed = rotate(head_norm(qkv[:, :, group : group + 1], k_gain), positions)[:, :, 0].astype(
        jnp.bfloat16
    )
    value = qkv[:, :, group + 1].astype(jnp.bfloat16)
    scores = jnp.einsum(
        "ikgd,jkd->kgij", query, keyed, preferred_element_type=jnp.float32
    ) / jnp.sqrt(jnp.float32(qkv.shape[3]))
    allowed = (positions[None, :] <= positions[:, None]) & (positions[None, :] < length)
    scores = jnp.where(allowed[None, None], scores, jnp.float32(-1e30))
    top = jnp.max(scores, axis=-1, keepdims=True)
    weights = jnp.exp(scores - top)
    probs = (weights / jnp.sum(weights, axis=-1, keepdims=True)).astype(jnp.bfloat16)
    out = jnp.einsum("kgij,jkd->ikgd", probs, value, preferred_element_type=jnp.float32)
    return out.reshape(rows, -1).astype(jnp.bfloat16)


def any_mesh(tokens, w_qkv, norm_gain, q_gain, k_gain, lengths):
    tensor_count = lax.axis_size("tensor")
    moved = lax.all_to_all(w_qkv, "tensor", split_axis=1, concat_axis=0, tiled=True)
    weight_cols = lax.all_gather(moved, "fsdp", axis=0, tiled=True)
    normed = head_norm(tokens.astype(jnp.float32), norm_gain).astype(jnp.bfloat16)
    qkv = jnp.dot(
        lax.all_gather(normed, "tensor", axis=0, tiled=True),
        weight_cols,
        preferred_element_type=jnp.float32,
    )
    qkv = qkv.reshape(qkv.shape[0], KV // tensor_count, GQ + 2, HD)
    return attend(qkv, q_gain, k_gain, lengths[0])


def project_kernel(counts, sources, tile, scal, *refs):
    blocks = len(counts)
    arrays = max(source[0] for source in sources) + 1
    middle_rows, end_rows = refs[:blocks], refs[blocks : 2 * blocks]
    refs = refs[2 * blocks :]
    pieces = refs[:arrays]
    cos_ref, sin_ref, gain_ref, out = refs[arrays : arrays + 4]
    taken, held, made, row_sems, sems, out_sems = refs[arrays + 4 :]
    depth = taken.shape[1] // 16
    columns = made.shape[1]
    steps = columns // tile

    def copies(step):
        listed = []
        for index, (array, first, group, slot) in enumerate(sources):
            start = pl.multiple_of((scal[group] * 4 + scal[slot]) * depth, 16)
            low = step * tile
            listed.append(
                pltpu.make_async_copy(
                    pieces[array].at[first : first + depth, low : low + tile],
                    held.at[step % 2, pl.ds(start, depth), :],
                    sems.at[step % 2, index],
                )
            )
        return listed

    starts = [sum(counts[:n]) for n in range(blocks)]
    row_copies = [
        [
            pltpu.make_async_copy(ref, taken.at[first : first + rows, :], row_sems.at[number])
            for ref in (middle_rows[number], end_rows[number])
        ]
        for number, (first, rows) in enumerate(zip(starts, counts))
    ]
    out_copies = []
    for copy in copies(0):
        copy.start()
    for in_middle, in_end in row_copies:
        pl.when(scal[8] == 1)(in_middle.start)
        pl.when(scal[8] == 0)(in_end.start)
    for step in range(steps):
        if step + 1 < steps:
            for copy in copies(step + 1):
                copy.start()
        if step == 0:
            for in_middle, _ in row_copies:
                in_middle.wait()
        for copy in copies(step):
            copy.wait()
        total = jnp.dot(taken[...], held[step % 2], preferred_element_type=jnp.float32)
        for number, (first, rows) in enumerate(zip(starts, counts)):
            place = pl.ds(pl.multiple_of(scal[9 + number], 128), rows)
            cosine = cos_ref[place, :]
            sine = sin_ref[place, :]
            for head in range(tile // HD):
                kind = (step * (tile // HD) + head) % (GQ + 2)
                vec = total[first : first + rows, head * HD : (head + 1) * HD]
                if kind <= GQ:
                    scale = lax.rsqrt(jnp.mean(vec * vec, axis=-1, keepdims=True) + 1e-06)
                    gain = gain_ref[0:1, :] if kind < GQ else gain_ref[1:2, :]
                    vec = vec * scale * gain
                    vec = vec * cosine + pltpu.roll(vec, HD // 2, 1) * sine
                at = step * tile + head * HD
                made[first : first + rows, at : at + HD] = vec.astype(made.dtype)
        at = slice(step * tile, (step + 1) * tile)
        out_copies.append(pltpu.make_async_copy(made.at[:, at], out.at[:, at], out_sems.at[step]))
        out_copies[-1].start()
    for copy in out_copies:
        copy.wait()


def project(rows_list, places, pieces, scal, cos, sin, gains):
    depth = rows_list[0][0].shape[1] // 16
    columns = pieces[0].shape[1]
    sources = [(n, m * depth, 4 + m, n) for n in range(4) for m in range(4)]
    counts = [r.shape[0] for r, _ in rows_list]
    steps = 3
    tile = columns // steps
    count = sum(counts)
    width = rows_list[0][0].shape[1]
    scal = jnp.concatenate([scal, jnp.stack(places)]).astype(jnp.int32)
    vmem = pl.BlockSpec(memory_space=pltpu.VMEM)
    hbm = pl.BlockSpec(memory_space=pltpu.HBM)
    return pl.pallas_call(
        functools.partial(project_kernel, counts, sources, tile),
        out_shape=pltpu.HBM((count, columns), jnp.bfloat16),
        in_specs=[pl.BlockSpec(memory_space=pltpu.SMEM)]
        + [hbm] * (2 * len(counts) + len(pieces))
        + [vmem] * 3,
        out_specs=hbm,
        scratch_shapes=[
            pltpu.VMEM((count, width), jnp.bfloat16),
            pltpu.VMEM((2, width, tile), jnp.bfloat16),
            pltpu.VMEM((count, columns), jnp.bfloat16),
            pltpu.SemaphoreType.DMA((len(counts),)),
            pltpu.SemaphoreType.DMA((2, 16)),
            pltpu.SemaphoreType.DMA((steps,)),
        ],
        compiler_params=pltpu.CompilerParams(vmem_limit_bytes=VMEM_BYTES),
        cost_estimate=pl.CostEstimate(
            flops=2 * count * width * columns,
            bytes_accessed=2 * (width * columns + count * (width + columns)),
            transcendentals=0,
        ),
        name="project",
    )(scal, *[r for r, _ in rows_list], *[r for _, r in rows_list], *pieces, cos, sin, gains)


def attend_kernel(parts, block, scal, *refs):
    out, held, sems = refs[len(parts) :]
    length = scal[0]

    copies = []
    for ref, blocks in zip(refs, parts):
        for first, rows, number in blocks:
            place = pl.ds(pl.multiple_of(scal[1 + number], 128), rows)
            copies.append(
                pltpu.make_async_copy(
                    ref.at[first : first + rows, :], held.at[place, :], sems.at[number]
                )
            )
    for copy in copies:
        copy.start()
    for copy in copies:
        copy.wait()

    total = held.shape[0]
    heads = held.shape[1] // ((GQ + 2) * HD)
    factor = LOG2E / float(HD) ** 0.5
    row = lax.broadcasted_iota(jnp.int32, (block, block), 0)
    col = lax.broadcasted_iota(jnp.int32, (block, block), 1)
    contract = (((1,), (1,)), ((), ()))
    for group in range(heads):
        base = group * (GQ + 2) * HD
        key_at = slice(base + GQ * HD, base + (GQ + 1) * HD)
        value_at = slice(base + (GQ + 1) * HD, base + (GQ + 2) * HD)

        @pl.loop(0, GQ)
        def _(j, base=base, key_at=key_at, value_at=value_at, group=group):
            query_at = pl.ds(pl.multiple_of(base + j * HD, HD), HD)
            out_at = pl.ds(pl.multiple_of((group * GQ + j) * HD, HD), HD)
            for step in range(total // block):
                low = step * block
                high = low + block
                query = held[low:high, query_at]
                last = lax.dot_general(
                    query, held[low:high, key_at], contract, preferred_element_type=jnp.float32
                )
                last = jnp.where((col <= row) & (col + low < length), last, -1e30)
                top = jnp.max(last, axis=-1, keepdims=True)
                if step:
                    rest = lax.dot_general(
                        query, held[:low, key_at], contract, preferred_element_type=jnp.float32
                    )
                    keys = lax.broadcasted_iota(jnp.int32, (1, low), 1)
                    rest = rest + jnp.where(keys < length, 0.0, -1e30)
                    top = jnp.maximum(top, jnp.max(rest, axis=-1, keepdims=True))
                shift = top * factor
                probs = jnp.exp2(last * factor - shift)
                norm = jnp.sum(probs, axis=-1, keepdims=True)
                value = jnp.dot(
                    probs.astype(jnp.bfloat16),
                    held[low:high, value_at],
                    preferred_element_type=jnp.float32,
                )
                if step:
                    probs = jnp.exp2(rest * factor - shift)
                    norm = norm + jnp.sum(probs, axis=-1, keepdims=True)
                    value = value + jnp.dot(
                        probs.astype(jnp.bfloat16),
                        held[:low, value_at],
                        preferred_element_type=jnp.float32,
                    )
                out[low:high, out_at] = (value / norm).astype(out.dtype)


def attend_blocks(arrays, parts, places, length):
    rows = sum(a.shape[0] for a in arrays)
    columns = arrays[0].shape[1]
    wide = columns // (GQ + 2) * GQ
    scal = jnp.stack([length] + list(places)).astype(jnp.int32)
    hbm = pl.BlockSpec(memory_space=pltpu.HBM)
    return pl.pallas_call(
        functools.partial(attend_kernel, parts, 256),
        out_shape=jax.ShapeDtypeStruct((rows, wide), jnp.bfloat16),
        in_specs=[pl.BlockSpec(memory_space=pltpu.SMEM)] + [hbm] * len(arrays),
        out_specs=pl.BlockSpec(memory_space=pltpu.VMEM),
        scratch_shapes=[
            pltpu.VMEM((rows, columns), jnp.bfloat16),
            pltpu.SemaphoreType.DMA((len(places),)),
        ],
        compiler_params=pltpu.CompilerParams(vmem_limit_bytes=VMEM_BYTES),
        cost_estimate=pl.CostEstimate(
            flops=4 * rows * rows * wide,
            bytes_accessed=2 * rows * (columns + wide),
            transcendentals=rows * rows * wide // HD // 2,
        ),
        name="attend",
    )(scal, *arrays)


def after(x, *earlier):
    return lax.optimization_barrier((x,) + earlier)[0]


def four_planes(tokens, w_qkv, norm_gain, q_gain, k_gain, lengths):
    t = lax.axis_index("tensor")
    rows = tokens.shape[0]
    half = rows // 2
    columns = w_qkv.shape[1] // 4
    side = t // 2
    far_end = 3 * (1 - side)
    far_mid = 2 - side

    def slab(block):
        return lax.dynamic_slice(w_qkv, (0, block * columns), (w_qkv.shape[0], columns))

    def across(x, pairs):
        return lax.ppermute(x, "tensor", pairs)

    def exchange(x, bits):
        return across(x, [(i, i ^ bits) for i in range(4)])

    def spread(x):
        return lax.all_gather(x, "fsdp", axis=0, tiled=True)

    swap = [(1, 2), (2, 1)]
    far = [(0, 2), (3, 1)]
    outward = [(1, 0), (2, 3)]

    planes = [t] + [jnp.bitwise_xor(t, m) for m in (1, 2, 3)]
    own, out1, out2, out3 = [slab(p) for p in planes]
    normed = head_norm(tokens.astype(jnp.float32), norm_gain).astype(jnp.bfloat16)
    first, second = normed[:half], normed[half:]

    in2, in3, in1 = exchange(out2, 2), exchange(out3, 3), exchange(out1, 1)
    pair1 = exchange(first, 1)
    in1, in2, in3, pair1 = lax.optimization_barrier((in1, in2, in3, pair1))
    swap1 = across(after(first, in1), swap)
    swap2 = across(after(second, in1), swap)
    pair2 = exchange(after(second, swap1), 1)
    far1 = across(after(first, swap1), far)
    far2 = across(after(second, swap1), far)
    on1, on2 = across(swap1, outward), across(after(swap2, pair2), outward)
    on3, on4 = across(after(far1, on1), outward), across(after(far2, on2), outward)

    pieces = [spread(x) for x in (own, in1, in2, in3)]
    middle = jnp.where((t == 1) | (t == 2), 1, 0)
    scal = jnp.stack(planes + [jnp.int32(m) for m in range(4)] + [middle])

    positions = jnp.arange(4 * rows, dtype=jnp.int32)
    angle = angles(positions)
    cos = jnp.concatenate([jnp.cos(angle)] * 2, axis=1)
    sin = jnp.concatenate([-jnp.sin(angle), jnp.sin(angle)], axis=1)
    gains = jnp.stack([q_gain, k_gain])

    calls = [
        [
            ((normed, normed), t * rows),
            ((pair1, pair1), planes[1] * rows),
            ((pair2, pair2), planes[1] * rows + half),
        ],
        [((swap1, on1), far_mid * rows), ((swap2, on2), far_mid * rows + half)],
        [((far1, on3), far_end * rows)],
        [((far2, on4), far_end * rows + half)],
    ]
    made, parts, places = [], [], []
    for call in calls:
        listed, first_row = [], 0
        for (block, _), place in call:
            listed.append((first_row, block.shape[0], len(places)))
            first_row += block.shape[0]
            places.append(place)
        parts.append(listed)
        made.append(
            project([b for b, _ in call], [p for _, p in call], pieces, scal, cos, sin, gains)
        )
    return attend_blocks(made, parts, places, lengths[0])


def solution(mesh):
    placed = (
        P(("groups", "fsdp", "tensor"), None),
        P(("groups", "fsdp", "tensor"), None),
        P(),
        P(),
        P(),
        P(("groups", "fsdp")),
    )
    sizes = dict(mesh.shape)
    body = four_planes if sizes["tensor"] == 4 and sizes["fsdp"] == 4 else any_mesh
    return jax.shard_map(
        body,
        mesh=mesh,
        in_specs=placed,
        out_specs=P(("groups", "fsdp"), "tensor"),
        check_vma=False,
    )
```

```python
import functools
import jax
import jax.numpy as jnp
from jax import lax
from jax.experimental import pallas as pl
from jax.experimental.pallas import tpu as pltpu
from jax.sharding import PartitionSpec as P

KV = 8
HD = 128
GQ = 4
LOG2E = 1.4426950408889634
VMEM_BYTES = 48 * 1024 * 1024


def head_norm(vec, gain):
    scale = lax.rsqrt(jnp.mean(vec * vec, axis=-1, keepdims=True) + 1e-06)
    return vec * scale * gain


def angles(positions):
    half = HD // 2
    freqs = 1000000.0 ** (-2.0 * jnp.arange(half, dtype=jnp.float32) / HD)
    return positions.astype(jnp.float32)[:, None] * freqs[None, :]


def rotate(vec, positions):
    half = vec.shape[-1] // 2
    angle = angles(positions)
    cosine = jnp.cos(angle)[:, None, None, :]
    sine = jnp.sin(angle)[:, None, None, :]
    first = vec[..., :half]
    second = vec[..., half:]
    return jnp.concatenate(
        [first * cosine - second * sine, second * cosine + first * sine], axis=-1
    )


def attend(qkv, q_gain, k_gain, length):
    rows = qkv.shape[0]
    group = qkv.shape[2] - 2
    positions = jnp.arange(rows, dtype=jnp.int32)
    query = rotate(head_norm(qkv[:, :, :group], q_gain), positions).astype(jnp.bfloat16)
    keyed = rotate(head_norm(qkv[:, :, group : group + 1], k_gain), positions)[:, :, 0].astype(
        jnp.bfloat16
    )
    value = qkv[:, :, group + 1].astype(jnp.bfloat16)
    scores = jnp.einsum(
        "ikgd,jkd->kgij", query, keyed, preferred_element_type=jnp.float32
    ) / jnp.sqrt(jnp.float32(qkv.shape[3]))
    allowed = (positions[None, :] <= positions[:, None]) & (positions[None, :] < length)
    scores = jnp.where(allowed[None, None], scores, jnp.float32(-1e30))
    top = jnp.max(scores, axis=-1, keepdims=True)
    weights = jnp.exp(scores - top)
    probs = (weights / jnp.sum(weights, axis=-1, keepdims=True)).astype(jnp.bfloat16)
    out = jnp.einsum("kgij,jkd->ikgd", probs, value, preferred_element_type=jnp.float32)
    return out.reshape(rows, -1).astype(jnp.bfloat16)


def any_mesh(tokens, w_qkv, norm_gain, q_gain, k_gain, lengths):
    tensor_count = lax.axis_size("tensor")
    moved = lax.all_to_all(w_qkv, "tensor", split_axis=1, concat_axis=0, tiled=True)
    weight_cols = lax.all_gather(moved, "fsdp", axis=0, tiled=True)
    normed = head_norm(tokens.astype(jnp.float32), norm_gain).astype(jnp.bfloat16)
    qkv = jnp.dot(
        lax.all_gather(normed, "tensor", axis=0, tiled=True),
        weight_cols,
        preferred_element_type=jnp.float32,
    )
    qkv = qkv.reshape(qkv.shape[0], KV // tensor_count, GQ + 2, HD)
    return attend(qkv, q_gain, k_gain, lengths[0])


def project_kernel(counts, sources, tile, scal, *refs):
    blocks = len(counts)
    arrays = max(source[0] for source in sources) + 1
    middle_rows, end_rows = refs[:blocks], refs[blocks : 2 * blocks]
    refs = refs[2 * blocks :]
    pieces = refs[:arrays]
    cos_ref, sin_ref, gain_ref, out = refs[arrays : arrays + 4]
    taken, held, made, row_sems, sems, out_sems = refs[arrays + 4 :]
    depth = taken.shape[1] // 16
    columns = made.shape[1]
    steps = columns // tile

    def copies(step):
        listed = []
        for index, (array, first, group, slot) in enumerate(sources):
            start = pl.multiple_of((scal[group] * 4 + scal[slot]) * depth, 16)
            low = step * tile
            listed.append(
                pltpu.make_async_copy(
                    pieces[array].at[first : first + depth, low : low + tile],
                    held.at[step % 2, pl.ds(start, depth), :],
                    sems.at[step % 2, index],
                )
            )
        return listed

    starts = [sum(counts[:n]) for n in range(blocks)]
    row_copies = [
        [
            pltpu.make_async_copy(ref, taken.at[first : first + rows, :], row_sems.at[number])
            for ref in (middle_rows[number], end_rows[number])
        ]
        for number, (first, rows) in enumerate(zip(starts, counts))
    ]
    out_copies = []
    for copy in copies(0):
        copy.start()
    for in_middle, in_end in row_copies:
        pl.when(scal[8] == 1)(in_middle.start)
        pl.when(scal[8] == 0)(in_end.start)
    for step in range(steps):
        if step + 1 < steps:
            for copy in copies(step + 1):
                copy.start()
        if step == 0:
            for in_middle, _ in row_copies:
                in_middle.wait()
        for copy in copies(step):
            copy.wait()
        total = jnp.dot(taken[...], held[step % 2], preferred_element_type=jnp.float32)
        for number, (first, rows) in enumerate(zip(starts, counts)):
            place = pl.ds(pl.multiple_of(scal[9 + number], 16), rows)
            cosine = cos_ref[place, :]
            sine = sin_ref[place, :]
            for head in range(tile // HD):
                kind = (step * (tile // HD) + head) % (GQ + 2)
                vec = total[first : first + rows, head * HD : (head + 1) * HD]
                if kind <= GQ:
                    scale = lax.rsqrt(jnp.mean(vec * vec, axis=-1, keepdims=True) + 1e-06)
                    gain = gain_ref[0:1, :] if kind < GQ else gain_ref[1:2, :]
                    vec = vec * scale * gain
                    vec = vec * cosine + pltpu.roll(vec, HD // 2, 1) * sine
                at = step * tile + head * HD
                made[first : first + rows, at : at + HD] = vec.astype(made.dtype)
        at = slice(step * tile, (step + 1) * tile)
        out_copies.append(pltpu.make_async_copy(made.at[:, at], out.at[:, at], out_sems.at[step]))
        out_copies[-1].start()
    for copy in out_copies:
        copy.wait()


def project(rows_list, places, pieces, scal, cos, sin, gains):
    depth = rows_list[0][0].shape[1] // 16
    columns = pieces[0].shape[1]
    sources = [(n, m * depth, 4 + m, n) for n in range(4) for m in range(4)]
    counts = [r.shape[0] for r, _ in rows_list]
    steps = 3
    tile = columns // steps
    count = sum(counts)
    width = rows_list[0][0].shape[1]
    scal = jnp.concatenate([scal, jnp.stack(places)]).astype(jnp.int32)
    vmem = pl.BlockSpec(memory_space=pltpu.VMEM)
    hbm = pl.BlockSpec(memory_space=pltpu.HBM)
    return pl.pallas_call(
        functools.partial(project_kernel, counts, sources, tile),
        out_shape=pltpu.HBM((count, columns), jnp.bfloat16),
        in_specs=[pl.BlockSpec(memory_space=pltpu.SMEM)]
        + [hbm] * (2 * len(counts) + len(pieces))
        + [vmem] * 3,
        out_specs=hbm,
        scratch_shapes=[
            pltpu.VMEM((count, width), jnp.bfloat16),
            pltpu.VMEM((2, width, tile), jnp.bfloat16),
            pltpu.VMEM((count, columns), jnp.bfloat16),
            pltpu.SemaphoreType.DMA((len(counts),)),
            pltpu.SemaphoreType.DMA((2, 16)),
            pltpu.SemaphoreType.DMA((steps,)),
        ],
        compiler_params=pltpu.CompilerParams(vmem_limit_bytes=VMEM_BYTES),
        cost_estimate=pl.CostEstimate(
            flops=2 * count * width * columns,
            bytes_accessed=2 * (width * columns + count * (width + columns)),
            transcendentals=0,
        ),
        name="project",
    )(scal, *[r for r, _ in rows_list], *[r for _, r in rows_list], *pieces, cos, sin, gains)


def attend_kernel(parts, block, scal, *refs):
    out, held, sems = refs[len(parts) :]
    length = scal[0]

    copies = []
    for ref, blocks in zip(refs, parts):
        for first, rows, number in blocks:
            place = pl.ds(pl.multiple_of(scal[1 + number], 16), rows)
            copies.append(
                pltpu.make_async_copy(
                    ref.at[first : first + rows, :], held.at[place, :], sems.at[number]
                )
            )
    for copy in copies:
        copy.start()
    for copy in copies:
        copy.wait()

    total = held.shape[0]
    heads = held.shape[1] // ((GQ + 2) * HD)
    factor = LOG2E / float(HD) ** 0.5
    row = lax.broadcasted_iota(jnp.int32, (block, block), 0)
    col = lax.broadcasted_iota(jnp.int32, (block, block), 1)
    contract = (((1,), (1,)), ((), ()))
    for group in range(heads):
        base = group * (GQ + 2) * HD
        key_at = slice(base + GQ * HD, base + (GQ + 1) * HD)
        value_at = slice(base + (GQ + 1) * HD, base + (GQ + 2) * HD)

        @pl.loop(0, GQ)
        def _(j, base=base, key_at=key_at, value_at=value_at, group=group):
            query_at = pl.ds(pl.multiple_of(base + j * HD, HD), HD)
            out_at = pl.ds(pl.multiple_of((group * GQ + j) * HD, HD), HD)
            for step in range(total // block):
                low = step * block
                high = low + block
                query = held[low:high, query_at]
                last = lax.dot_general(
                    query, held[low:high, key_at], contract, preferred_element_type=jnp.float32
                )
                last = jnp.where((col <= row) & (col + low < length), last, -1e30)
                top = jnp.max(last, axis=-1, keepdims=True)
                if step:
                    rest = lax.dot_general(
                        query, held[:low, key_at], contract, preferred_element_type=jnp.float32
                    )
                    keys = lax.broadcasted_iota(jnp.int32, (1, low), 1)
                    rest = rest + jnp.where(keys < length, 0.0, -1e30)
                    top = jnp.maximum(top, jnp.max(rest, axis=-1, keepdims=True))
                shift = top * factor
                probs = jnp.exp2(last * factor - shift)
                norm = jnp.sum(probs, axis=-1, keepdims=True)
                value = jnp.dot(
                    probs.astype(jnp.bfloat16),
                    held[low:high, value_at],
                    preferred_element_type=jnp.float32,
                )
                if step:
                    probs = jnp.exp2(rest * factor - shift)
                    norm = norm + jnp.sum(probs, axis=-1, keepdims=True)
                    value = value + jnp.dot(
                        probs.astype(jnp.bfloat16),
                        held[:low, value_at],
                        preferred_element_type=jnp.float32,
                    )
                out[low:high, out_at] = (value / norm).astype(out.dtype)


def attend_blocks(arrays, parts, places, length):
    rows = sum(a.shape[0] for a in arrays)
    columns = arrays[0].shape[1]
    wide = columns // (GQ + 2) * GQ
    scal = jnp.stack([length] + list(places)).astype(jnp.int32)
    hbm = pl.BlockSpec(memory_space=pltpu.HBM)
    return pl.pallas_call(
        functools.partial(attend_kernel, parts, 256),
        out_shape=jax.ShapeDtypeStruct((rows, wide), jnp.bfloat16),
        in_specs=[pl.BlockSpec(memory_space=pltpu.SMEM)] + [hbm] * len(arrays),
        out_specs=pl.BlockSpec(memory_space=pltpu.VMEM),
        scratch_shapes=[
            pltpu.VMEM((rows, columns), jnp.bfloat16),
            pltpu.SemaphoreType.DMA((len(places),)),
        ],
        compiler_params=pltpu.CompilerParams(vmem_limit_bytes=VMEM_BYTES),
        cost_estimate=pl.CostEstimate(
            flops=4 * rows * rows * wide,
            bytes_accessed=2 * rows * (columns + wide),
            transcendentals=rows * rows * wide // HD // 2,
        ),
        name="attend",
    )(scal, *arrays)


def after(x, *earlier):
    return lax.optimization_barrier((x,) + earlier)[0]


def four_planes(tokens, w_qkv, norm_gain, q_gain, k_gain, lengths):
    t = lax.axis_index("tensor")
    rows = tokens.shape[0]
    half = rows // 2
    columns = w_qkv.shape[1] // 4
    side = t // 2
    far_end = 3 * (1 - side)
    far_mid = 2 - side

    def slab(block):
        return lax.dynamic_slice(w_qkv, (0, block * columns), (w_qkv.shape[0], columns))

    def across(x, pairs):
        return lax.ppermute(x, "tensor", pairs)

    def exchange(x, bits):
        return across(x, [(i, i ^ bits) for i in range(4)])

    def spread(x):
        return lax.all_gather(x, "fsdp", axis=0, tiled=True)

    swap = [(1, 2), (2, 1)]
    far = [(0, 2), (3, 1)]
    outward = [(1, 0), (2, 3)]

    planes = [t] + [jnp.bitwise_xor(t, m) for m in (1, 2, 3)]
    own, out1, out2, out3 = [slab(p) for p in planes]
    normed = head_norm(tokens.astype(jnp.float32), norm_gain).astype(jnp.bfloat16)
    first, second = normed[:half], normed[half:]

    in2, in3, in1 = exchange(out2, 2), exchange(out3, 3), exchange(out1, 1)
    pair1 = exchange(normed[: rows // 4], 1)
    in1, in2, in3, pair1 = lax.optimization_barrier((in1, in2, in3, pair1))
    swap1 = across(after(first, in1), swap)
    pair2 = exchange(after(normed[rows // 4 : rows // 4 + half], in1), 1)
    swap2 = across(after(second, swap1, pair2), swap)
    pair3 = exchange(after(normed[rows // 4 + half :], pair2), 1)
    on1 = across(swap1, outward)
    far1 = across(after(first, swap2, on1), far)
    on2 = across(swap2, outward)
    far2 = across(after(second, far1, pair3), far)
    on3, on4 = across(far1, outward), across(after(far2, on2), outward)

    pieces = [spread(x) for x in (own, in1, in2, in3)]
    middle = jnp.where((t == 1) | (t == 2), 1, 0)
    scal = jnp.stack(planes + [jnp.int32(m) for m in range(4)] + [middle])

    positions = jnp.arange(4 * rows, dtype=jnp.int32)
    angle = angles(positions)
    cos = jnp.concatenate([jnp.cos(angle)] * 2, axis=1)
    sin = jnp.concatenate([-jnp.sin(angle), jnp.sin(angle)], axis=1)
    gains = jnp.stack([q_gain, k_gain])

    calls = [
        [
            ((normed, normed), t * rows),
            ((pair1, pair1), planes[1] * rows),
            ((pair2, pair2), planes[1] * rows + rows // 4),
            ((pair3, pair3), planes[1] * rows + rows // 4 + half),
        ],
        [((swap1, on1), far_mid * rows), ((swap2, on2), far_mid * rows + half)],
        [((far1, on3), far_end * rows)],
        [((far2, on4), far_end * rows + half)],
    ]
    made, parts, places = [], [], []
    for number, call in enumerate(calls):
        listed, first_row = [], 0
        for (block, _), place in call:
            listed.append((first_row, block.shape[0], len(places)))
            first_row += block.shape[0]
            places.append(place)
        parts.append(listed)
        arrays = [b for b, _ in call]
        if number >= 2:
            arrays = [(after(x, *made[:2]), after(y, *made[:2])) for x, y in arrays]
        made.append(
            project(arrays, [p for _, p in call], pieces, scal, cos, sin, gains)
        )
    return attend_blocks(made, parts, places, lengths[0])


def solution(mesh):
    placed = (
        P(("groups", "fsdp", "tensor"), None),
        P(("groups", "fsdp", "tensor"), None),
        P(),
        P(),
        P(),
        P(("groups", "fsdp")),
    )
    sizes = dict(mesh.shape)
    body = four_planes if sizes["tensor"] == 4 and sizes["fsdp"] == 4 else any_mesh
    return jax.shard_map(
        body,
        mesh=mesh,
        in_specs=placed,
        out_specs=P(("groups", "fsdp"), "tensor"),
        check_vma=False,
    )
```

```python
import functools
import jax
import jax.numpy as jnp
from jax import lax
from jax.experimental import pallas as pl
from jax.experimental.pallas import tpu as pltpu
from jax.sharding import PartitionSpec as P

KV = 8
HD = 128
GQ = 4
LOG2E = 1.4426950408889634
VMEM_BYTES = 48 * 1024 * 1024


def head_norm(vec, gain):
    scale = lax.rsqrt(jnp.mean(vec * vec, axis=-1, keepdims=True) + 1e-06)
    return vec * scale * gain


def angles(positions):
    half = HD // 2
    freqs = 1000000.0 ** (-2.0 * jnp.arange(half, dtype=jnp.float32) / HD)
    return positions.astype(jnp.float32)[:, None] * freqs[None, :]


def rotate(vec, positions):
    half = vec.shape[-1] // 2
    angle = angles(positions)
    cosine = jnp.cos(angle)[:, None, None, :]
    sine = jnp.sin(angle)[:, None, None, :]
    first = vec[..., :half]
    second = vec[..., half:]
    return jnp.concatenate(
        [first * cosine - second * sine, second * cosine + first * sine], axis=-1
    )


def attend(qkv, q_gain, k_gain, length):
    rows = qkv.shape[0]
    group = qkv.shape[2] - 2
    positions = jnp.arange(rows, dtype=jnp.int32)
    query = rotate(head_norm(qkv[:, :, :group], q_gain), positions).astype(jnp.bfloat16)
    keyed = rotate(head_norm(qkv[:, :, group : group + 1], k_gain), positions)[:, :, 0].astype(
        jnp.bfloat16
    )
    value = qkv[:, :, group + 1].astype(jnp.bfloat16)
    scores = jnp.einsum(
        "ikgd,jkd->kgij", query, keyed, preferred_element_type=jnp.float32
    ) / jnp.sqrt(jnp.float32(qkv.shape[3]))
    allowed = (positions[None, :] <= positions[:, None]) & (positions[None, :] < length)
    scores = jnp.where(allowed[None, None], scores, jnp.float32(-1e30))
    top = jnp.max(scores, axis=-1, keepdims=True)
    weights = jnp.exp(scores - top)
    probs = (weights / jnp.sum(weights, axis=-1, keepdims=True)).astype(jnp.bfloat16)
    out = jnp.einsum("kgij,jkd->ikgd", probs, value, preferred_element_type=jnp.float32)
    return out.reshape(rows, -1).astype(jnp.bfloat16)


def any_mesh(tokens, w_qkv, norm_gain, q_gain, k_gain, lengths):
    tensor_count = lax.axis_size("tensor")
    moved = lax.all_to_all(w_qkv, "tensor", split_axis=1, concat_axis=0, tiled=True)
    weight_cols = lax.all_gather(moved, "fsdp", axis=0, tiled=True)
    normed = head_norm(tokens.astype(jnp.float32), norm_gain).astype(jnp.bfloat16)
    qkv = jnp.dot(
        lax.all_gather(normed, "tensor", axis=0, tiled=True),
        weight_cols,
        preferred_element_type=jnp.float32,
    )
    qkv = qkv.reshape(qkv.shape[0], KV // tensor_count, GQ + 2, HD)
    return attend(qkv, q_gain, k_gain, lengths[0])


def project_kernel(counts, sources, tile, scal, *refs):
    blocks = len(counts)
    arrays = max(source[0] for source in sources) + 1
    middle_rows, end_rows = refs[:blocks], refs[blocks : 2 * blocks]
    refs = refs[2 * blocks :]
    pieces = refs[:arrays]
    cos_ref, sin_ref, gain_ref, out = refs[arrays : arrays + 4]
    taken, held, made, row_sems, sems, out_sems = refs[arrays + 4 :]
    depth = taken.shape[1] // 16
    columns = made.shape[1]
    steps = columns // tile

    def copies(step):
        listed = []
        for index, (array, first, group, slot) in enumerate(sources):
            start = pl.multiple_of((scal[group] * 4 + scal[slot]) * depth, 16)
            low = step * tile
            listed.append(
                pltpu.make_async_copy(
                    pieces[array].at[first : first + depth, low : low + tile],
                    held.at[step % 2, pl.ds(start, depth), :],
                    sems.at[step % 2, index],
                )
            )
        return listed

    starts = [sum(counts[:n]) for n in range(blocks)]
    row_copies = [
        [
            pltpu.make_async_copy(ref, taken.at[first : first + rows, :], row_sems.at[number])
            for ref in (middle_rows[number], end_rows[number])
        ]
        for number, (first, rows) in enumerate(zip(starts, counts))
    ]
    out_copies = []
    for copy in copies(0):
        copy.start()
    for in_middle, in_end in row_copies:
        pl.when(scal[8] == 1)(in_middle.start)
        pl.when(scal[8] == 0)(in_end.start)
    for step in range(steps):
        if step + 1 < steps:
            for copy in copies(step + 1):
                copy.start()
        if step == 0:
            for in_middle, _ in row_copies:
                in_middle.wait()
        for copy in copies(step):
            copy.wait()
        total = jnp.dot(taken[...], held[step % 2], preferred_element_type=jnp.float32)
        for number, (first, rows) in enumerate(zip(starts, counts)):
            place = pl.ds(pl.multiple_of(scal[9 + number], 16), rows)
            cosine = cos_ref[place, :]
            sine = sin_ref[place, :]
            for head in range(tile // HD):
                kind = (step * (tile // HD) + head) % (GQ + 2)
                vec = total[first : first + rows, head * HD : (head + 1) * HD]
                if kind <= GQ:
                    scale = lax.rsqrt(jnp.mean(vec * vec, axis=-1, keepdims=True) + 1e-06)
                    gain = gain_ref[0:1, :] if kind < GQ else gain_ref[1:2, :]
                    vec = vec * scale * gain
                    vec = vec * cosine + pltpu.roll(vec, HD // 2, 1) * sine
                at = step * tile + head * HD
                made[first : first + rows, at : at + HD] = vec.astype(made.dtype)
        at = slice(step * tile, (step + 1) * tile)
        out_copies.append(pltpu.make_async_copy(made.at[:, at], out.at[:, at], out_sems.at[step]))
        out_copies[-1].start()
    for copy in out_copies:
        copy.wait()


def project(rows_list, places, pieces, scal, cos, sin, gains):
    depth = rows_list[0][0].shape[1] // 16
    columns = pieces[0].shape[1]
    sources = [(n, m * depth, 4 + m, n) for n in range(4) for m in range(4)]
    counts = [r.shape[0] for r, _ in rows_list]
    steps = 3
    tile = columns // steps
    count = sum(counts)
    width = rows_list[0][0].shape[1]
    scal = jnp.concatenate([scal, jnp.stack(places)]).astype(jnp.int32)
    vmem = pl.BlockSpec(memory_space=pltpu.VMEM)
    hbm = pl.BlockSpec(memory_space=pltpu.HBM)
    return pl.pallas_call(
        functools.partial(project_kernel, counts, sources, tile),
        out_shape=pltpu.HBM((count, columns), jnp.bfloat16),
        in_specs=[pl.BlockSpec(memory_space=pltpu.SMEM)]
        + [hbm] * (2 * len(counts) + len(pieces))
        + [vmem] * 3,
        out_specs=hbm,
        scratch_shapes=[
            pltpu.VMEM((count, width), jnp.bfloat16),
            pltpu.VMEM((2, width, tile), jnp.bfloat16),
            pltpu.VMEM((count, columns), jnp.bfloat16),
            pltpu.SemaphoreType.DMA((len(counts),)),
            pltpu.SemaphoreType.DMA((2, 16)),
            pltpu.SemaphoreType.DMA((steps,)),
        ],
        compiler_params=pltpu.CompilerParams(vmem_limit_bytes=VMEM_BYTES),
        cost_estimate=pl.CostEstimate(
            flops=2 * count * width * columns,
            bytes_accessed=2 * (width * columns + count * (width + columns)),
            transcendentals=0,
        ),
        name="project",
    )(scal, *[r for r, _ in rows_list], *[r for _, r in rows_list], *pieces, cos, sin, gains)


def attend_kernel(parts, block, scal, *refs):
    out, held, sems = refs[len(parts) :]
    length = scal[0]

    copies = []
    for ref, blocks in zip(refs, parts):
        for first, rows, number in blocks:
            place = pl.ds(pl.multiple_of(scal[1 + number], 16), rows)
            copies.append(
                pltpu.make_async_copy(
                    ref.at[first : first + rows, :], held.at[place, :], sems.at[number]
                )
            )
    for copy in copies:
        copy.start()
    for copy in copies:
        copy.wait()

    total = held.shape[0]
    heads = held.shape[1] // ((GQ + 2) * HD)
    factor = LOG2E / float(HD) ** 0.5
    row = lax.broadcasted_iota(jnp.int32, (block, block), 0)
    col = lax.broadcasted_iota(jnp.int32, (block, block), 1)
    contract = (((1,), (1,)), ((), ()))
    for group in range(heads):
        base = group * (GQ + 2) * HD
        key_at = slice(base + GQ * HD, base + (GQ + 1) * HD)
        value_at = slice(base + (GQ + 1) * HD, base + (GQ + 2) * HD)

        @pl.loop(0, GQ)
        def _(j, base=base, key_at=key_at, value_at=value_at, group=group):
            query_at = pl.ds(pl.multiple_of(base + j * HD, HD), HD)
            out_at = pl.ds(pl.multiple_of((group * GQ + j) * HD, HD), HD)
            for step in range(total // block):
                low = step * block
                high = low + block
                query = held[low:high, query_at]
                last = lax.dot_general(
                    query, held[low:high, key_at], contract, preferred_element_type=jnp.float32
                )
                last = jnp.where((col <= row) & (col + low < length), last, -1e30)
                top = jnp.max(last, axis=-1, keepdims=True)
                if step:
                    rest = lax.dot_general(
                        query, held[:low, key_at], contract, preferred_element_type=jnp.float32
                    )
                    keys = lax.broadcasted_iota(jnp.int32, (1, low), 1)
                    rest = rest + jnp.where(keys < length, 0.0, -1e30)
                    top = jnp.maximum(top, jnp.max(rest, axis=-1, keepdims=True))
                shift = top * factor
                probs = jnp.exp2(last * factor - shift)
                norm = jnp.sum(probs, axis=-1, keepdims=True)
                value = jnp.dot(
                    probs.astype(jnp.bfloat16),
                    held[low:high, value_at],
                    preferred_element_type=jnp.float32,
                )
                if step:
                    probs = jnp.exp2(rest * factor - shift)
                    norm = norm + jnp.sum(probs, axis=-1, keepdims=True)
                    value = value + jnp.dot(
                        probs.astype(jnp.bfloat16),
                        held[:low, value_at],
                        preferred_element_type=jnp.float32,
                    )
                out[low:high, out_at] = (value / norm).astype(out.dtype)


def attend_blocks(arrays, parts, places, length):
    rows = sum(a.shape[0] for a in arrays)
    columns = arrays[0].shape[1]
    wide = columns // (GQ + 2) * GQ
    scal = jnp.stack([length] + list(places)).astype(jnp.int32)
    hbm = pl.BlockSpec(memory_space=pltpu.HBM)
    return pl.pallas_call(
        functools.partial(attend_kernel, parts, 256),
        out_shape=jax.ShapeDtypeStruct((rows, wide), jnp.bfloat16),
        in_specs=[pl.BlockSpec(memory_space=pltpu.SMEM)] + [hbm] * len(arrays),
        out_specs=pl.BlockSpec(memory_space=pltpu.VMEM),
        scratch_shapes=[
            pltpu.VMEM((rows, columns), jnp.bfloat16),
            pltpu.SemaphoreType.DMA((len(places),)),
        ],
        compiler_params=pltpu.CompilerParams(vmem_limit_bytes=VMEM_BYTES),
        cost_estimate=pl.CostEstimate(
            flops=4 * rows * rows * wide,
            bytes_accessed=2 * rows * (columns + wide),
            transcendentals=rows * rows * wide // HD // 2,
        ),
        name="attend",
    )(scal, *arrays)


def after(x, *earlier):
    return lax.optimization_barrier((x,) + earlier)[0]


def four_planes(tokens, w_qkv, norm_gain, q_gain, k_gain, lengths):
    t = lax.axis_index("tensor")
    rows = tokens.shape[0]
    half = rows // 2
    columns = w_qkv.shape[1] // 4
    side = t // 2
    far_end = 3 * (1 - side)
    far_mid = 2 - side

    def slab(block):
        return lax.dynamic_slice(w_qkv, (0, block * columns), (w_qkv.shape[0], columns))

    def across(x, pairs):
        return lax.ppermute(x, "tensor", pairs)

    def exchange(x, bits):
        return across(x, [(i, i ^ bits) for i in range(4)])

    def spread(x):
        return lax.all_gather(x, "fsdp", axis=0, tiled=True)

    swap = [(1, 2), (2, 1)]
    far = [(0, 2), (3, 1)]
    outward = [(1, 0), (2, 3)]

    planes = [t] + [jnp.bitwise_xor(t, m) for m in (1, 2, 3)]
    own, out1, out2, out3 = [slab(p) for p in planes]
    normed = head_norm(tokens.astype(jnp.float32), norm_gain).astype(jnp.bfloat16)
    first, second = normed[:half], normed[half:]

    in2, in3, in1 = exchange(out2, 2), exchange(out3, 3), exchange(out1, 1)
    pair1 = exchange(normed[: rows // 4], 1)
    in1, in2, in3, pair1 = lax.optimization_barrier((in1, in2, in3, pair1))
    swap1 = across(after(first, in1), swap)
    pair2 = exchange(after(normed[rows // 4 : rows // 4 + half], in1), 1)
    swap2 = across(after(second, swap1, pair2), swap)
    pair3 = exchange(after(normed[rows // 4 + half :], pair2), 1)
    on1 = across(swap1, outward)
    far1 = across(after(first, swap2, on1, pair3), far)
    on2 = across(swap2, outward)
    far2 = across(after(second, far1), far)
    on3 = across(far1, outward)

    pieces = [spread(x) for x in (own, in1, in2, in3)]
    middle = jnp.where((t == 1) | (t == 2), 1, 0)
    scal = jnp.stack(planes + [jnp.int32(m) for m in range(4)] + [middle])

    positions = jnp.arange(4 * rows, dtype=jnp.int32)
    angle = angles(positions)
    cos = jnp.concatenate([jnp.cos(angle)] * 2, axis=1)
    sin = jnp.concatenate([-jnp.sin(angle), jnp.sin(angle)], axis=1)
    gains = jnp.stack([q_gain, k_gain])

    made, parts, places = [], [], []

    def run(call):
        listed, first_row = [], 0
        for (block, _), place in call:
            listed.append((first_row, block.shape[0], len(places)))
            first_row += block.shape[0]
            places.append(place)
        parts.append(listed)
        made.append(
            project([b for b, _ in call], [p for _, p in call], pieces, scal, cos, sin, gains)
        )

    pair_place = planes[1] * rows
    run(
        [
            ((normed, normed), t * rows),
            ((pair1, pair1), pair_place),
            ((pair2, pair2), pair_place + rows // 4),
            ((pair3, pair3), pair_place + rows // 4 + half),
        ]
    )
    on4 = across(after(far2, on2, made[0]), outward)
    run([((swap1, on1), far_mid * rows), ((swap2, on2), far_mid * rows + half)])
    far1, on3, far2, on4 = [after(x, *made) for x in (far1, on3, far2, on4)]
    run([((far1, on3), far_end * rows)])
    run([((far2, on4), far_end * rows + half)])
    return attend_blocks(made, parts, places, lengths[0])


def solution(mesh):
    placed = (
        P(("groups", "fsdp", "tensor"), None),
        P(("groups", "fsdp", "tensor"), None),
        P(),
        P(),
        P(),
        P(("groups", "fsdp")),
    )
    sizes = dict(mesh.shape)
    body = four_planes if sizes["tensor"] == 4 and sizes["fsdp"] == 4 else any_mesh
    return jax.shard_map(
        body,
        mesh=mesh,
        in_specs=placed,
        out_specs=P(("groups", "fsdp"), "tensor"),
        check_vma=False,
    )
```

```python
import functools
import jax
import jax.numpy as jnp
from jax import lax
from jax.experimental import pallas as pl
from jax.experimental.pallas import tpu as pltpu
from jax.sharding import PartitionSpec as P

KV = 8
HD = 128
GQ = 4
LOG2E = 1.4426950408889634
VMEM_BYTES = 48 * 1024 * 1024


def head_norm(vec, gain):
    scale = lax.rsqrt(jnp.mean(vec * vec, axis=-1, keepdims=True) + 1e-06)
    return vec * scale * gain


def angles(positions):
    half = HD // 2
    freqs = 1000000.0 ** (-2.0 * jnp.arange(half, dtype=jnp.float32) / HD)
    return positions.astype(jnp.float32)[:, None] * freqs[None, :]


def rotate(vec, positions):
    half = vec.shape[-1] // 2
    angle = angles(positions)
    cosine = jnp.cos(angle)[:, None, None, :]
    sine = jnp.sin(angle)[:, None, None, :]
    first = vec[..., :half]
    second = vec[..., half:]
    return jnp.concatenate(
        [first * cosine - second * sine, second * cosine + first * sine], axis=-1
    )


def attend(qkv, q_gain, k_gain, length):
    rows = qkv.shape[0]
    group = qkv.shape[2] - 2
    positions = jnp.arange(rows, dtype=jnp.int32)
    query = rotate(head_norm(qkv[:, :, :group], q_gain), positions).astype(jnp.bfloat16)
    keyed = rotate(head_norm(qkv[:, :, group : group + 1], k_gain), positions)[:, :, 0].astype(
        jnp.bfloat16
    )
    value = qkv[:, :, group + 1].astype(jnp.bfloat16)
    scores = jnp.einsum(
        "ikgd,jkd->kgij", query, keyed, preferred_element_type=jnp.float32
    ) / jnp.sqrt(jnp.float32(qkv.shape[3]))
    allowed = (positions[None, :] <= positions[:, None]) & (positions[None, :] < length)
    scores = jnp.where(allowed[None, None], scores, jnp.float32(-1e30))
    top = jnp.max(scores, axis=-1, keepdims=True)
    weights = jnp.exp(scores - top)
    probs = (weights / jnp.sum(weights, axis=-1, keepdims=True)).astype(jnp.bfloat16)
    out = jnp.einsum("kgij,jkd->ikgd", probs, value, preferred_element_type=jnp.float32)
    return out.reshape(rows, -1).astype(jnp.bfloat16)


def any_mesh(tokens, w_qkv, norm_gain, q_gain, k_gain, lengths):
    tensor_count = lax.axis_size("tensor")
    moved = lax.all_to_all(w_qkv, "tensor", split_axis=1, concat_axis=0, tiled=True)
    weight_cols = lax.all_gather(moved, "fsdp", axis=0, tiled=True)
    normed = head_norm(tokens.astype(jnp.float32), norm_gain).astype(jnp.bfloat16)
    qkv = jnp.dot(
        lax.all_gather(normed, "tensor", axis=0, tiled=True),
        weight_cols,
        preferred_element_type=jnp.float32,
    )
    qkv = qkv.reshape(qkv.shape[0], KV // tensor_count, GQ + 2, HD)
    return attend(qkv, q_gain, k_gain, lengths[0])


def project_kernel(counts, sources, tile, scal, *refs):
    blocks = len(counts)
    arrays = max(source[0] for source in sources) + 1
    middle_rows, end_rows = refs[:blocks], refs[blocks : 2 * blocks]
    refs = refs[2 * blocks :]
    pieces = refs[:arrays]
    cos_ref, sin_ref, gain_ref, out = refs[arrays : arrays + 4]
    taken, held, made, row_sems, sems, out_sems = refs[arrays + 4 :]
    depth = taken.shape[1] // 16
    columns = made.shape[1]
    steps = columns // tile

    def copies(step):
        listed = []
        for index, (array, first, group, slot) in enumerate(sources):
            start = pl.multiple_of((scal[group] * 4 + scal[slot]) * depth, 16)
            low = step * tile
            listed.append(
                pltpu.make_async_copy(
                    pieces[array].at[first : first + depth, low : low + tile],
                    held.at[step % 2, pl.ds(start, depth), :],
                    sems.at[step % 2, index],
                )
            )
        return listed

    starts = [sum(counts[:n]) for n in range(blocks)]
    row_copies = [
        [
            pltpu.make_async_copy(ref, taken.at[first : first + rows, :], row_sems.at[number])
            for ref in (middle_rows[number], end_rows[number])
        ]
        for number, (first, rows) in enumerate(zip(starts, counts))
    ]
    out_copies = []
    for copy in copies(0):
        copy.start()
    for in_middle, in_end in row_copies:
        pl.when(scal[8] == 1)(in_middle.start)
        pl.when(scal[8] == 0)(in_end.start)
    for step in range(steps):
        if step + 1 < steps:
            for copy in copies(step + 1):
                copy.start()
        if step == 0:
            for in_middle, _ in row_copies:
                in_middle.wait()
        for copy in copies(step):
            copy.wait()
        total = jnp.dot(taken[...], held[step % 2], preferred_element_type=jnp.float32)
        for number, (first, rows) in enumerate(zip(starts, counts)):
            place = pl.ds(pl.multiple_of(scal[9 + number], 16), rows)
            cosine = cos_ref[place, :]
            sine = sin_ref[place, :]
            for head in range(tile // HD):
                kind = (step * (tile // HD) + head) % (GQ + 2)
                vec = total[first : first + rows, head * HD : (head + 1) * HD]
                if kind <= GQ:
                    scale = lax.rsqrt(jnp.mean(vec * vec, axis=-1, keepdims=True) + 1e-06)
                    gain = gain_ref[0:1, :] if kind < GQ else gain_ref[1:2, :]
                    vec = vec * scale * gain
                    vec = vec * cosine + pltpu.roll(vec, HD // 2, 1) * sine
                at = step * tile + head * HD
                made[first : first + rows, at : at + HD] = vec.astype(made.dtype)
        at = slice(step * tile, (step + 1) * tile)
        out_copies.append(pltpu.make_async_copy(made.at[:, at], out.at[:, at], out_sems.at[step]))
        out_copies[-1].start()
    for copy in out_copies:
        copy.wait()


def project(rows_list, places, pieces, scal, cos, sin, gains):
    depth = rows_list[0][0].shape[1] // 16
    columns = pieces[0].shape[1]
    sources = [(n, m * depth, 4 + m, n) for n in range(4) for m in range(4)]
    counts = [r.shape[0] for r, _ in rows_list]
    steps = 3
    tile = columns // steps
    count = sum(counts)
    width = rows_list[0][0].shape[1]
    scal = jnp.concatenate([scal, jnp.stack(places)]).astype(jnp.int32)
    vmem = pl.BlockSpec(memory_space=pltpu.VMEM)
    hbm = pl.BlockSpec(memory_space=pltpu.HBM)
    return pl.pallas_call(
        functools.partial(project_kernel, counts, sources, tile),
        out_shape=pltpu.HBM((count, columns), jnp.bfloat16),
        in_specs=[pl.BlockSpec(memory_space=pltpu.SMEM)]
        + [hbm] * (2 * len(counts) + len(pieces))
        + [vmem] * 3,
        out_specs=hbm,
        scratch_shapes=[
            pltpu.VMEM((count, width), jnp.bfloat16),
            pltpu.VMEM((2, width, tile), jnp.bfloat16),
            pltpu.VMEM((count, columns), jnp.bfloat16),
            pltpu.SemaphoreType.DMA((len(counts),)),
            pltpu.SemaphoreType.DMA((2, 16)),
            pltpu.SemaphoreType.DMA((steps,)),
        ],
        compiler_params=pltpu.CompilerParams(vmem_limit_bytes=VMEM_BYTES),
        cost_estimate=pl.CostEstimate(
            flops=2 * count * width * columns,
            bytes_accessed=2 * (width * columns + count * (width + columns)),
            transcendentals=0,
        ),
        name="project",
    )(scal, *[r for r, _ in rows_list], *[r for _, r in rows_list], *pieces, cos, sin, gains)


FACTOR = LOG2E / float(HD) ** 0.5
CONTRACT = (((1,), (1,)), ((), ()))


def fetch_blocks(refs, parts, places, held, sems):
    copies = []
    for ref, blocks in zip(refs, parts):
        for first, rows, number in blocks:
            place = pl.ds(pl.multiple_of(places(number), 16), rows)
            copies.append(
                pltpu.make_async_copy(
                    ref.at[first : first + rows, :], held.at[place, :], sems.at[number]
                )
            )
    for copy in copies:
        copy.start()
    for copy in copies:
        copy.wait()


def head_columns(head):
    base = head // GQ * (GQ + 2) * HD
    query = base + head % GQ * HD
    key = base + GQ * HD
    return (
        slice(query, query + HD),
        slice(key, key + HD),
        slice(key + HD, key + 2 * HD),
        slice(head * HD, (head + 1) * HD),
    )


def attend_rows(held, head, low, block, length):
    query_at, key_at, value_at, _ = head_columns(head)
    high = low + block
    row = lax.broadcasted_iota(jnp.int32, (block, block), 0)
    col = lax.broadcasted_iota(jnp.int32, (block, block), 1)
    query = held[low:high, query_at]
    last = lax.dot_general(
        query, held[low:high, key_at], CONTRACT, preferred_element_type=jnp.float32
    )
    last = jnp.where((col <= row) & (col + low < length), last, -1e30)
    top = jnp.max(last, axis=-1, keepdims=True)
    if low:
        rest = lax.dot_general(
            query, held[:low, key_at], CONTRACT, preferred_element_type=jnp.float32
        )
        keys = lax.broadcasted_iota(jnp.int32, (1, low), 1)
        rest = rest + jnp.where(keys < length, 0.0, -1e30)
        top = jnp.maximum(top, jnp.max(rest, axis=-1, keepdims=True))
    shift = top * FACTOR
    probs = jnp.exp2(last * FACTOR - shift)
    norm = jnp.sum(probs, axis=-1, keepdims=True)
    value = jnp.dot(
        probs.astype(jnp.bfloat16), held[low:high, value_at], preferred_element_type=jnp.float32
    )
    if low:
        probs = jnp.exp2(rest * FACTOR - shift)
        norm = norm + jnp.sum(probs, axis=-1, keepdims=True)
        value = value + jnp.dot(
            probs.astype(jnp.bfloat16), held[:low, value_at], preferred_element_type=jnp.float32
        )
    return top, norm, value


def attend_near_kernel(parts, block, scal, *refs):
    partial, stats, held, sems = refs[len(parts) :]
    fetch_blocks(refs, parts, lambda number: scal[2 + number], held, sems)
    heads = partial.shape[1] // HD
    for head in range(heads):
        out_at = head_columns(head)[3]
        for low in range(0, held.shape[0], block):
            top, norm, value = attend_rows(held, head, low, block, scal[0])
            partial[low : low + block, out_at] = value
            stats[low : low + block, head : head + 1] = top
            stats[low : low + block, heads + head : heads + head + 1] = norm


def attend_far_kernel(parts, block, scal, *refs):
    partial, stats, out, held, sems = refs[len(parts) :]
    fetch_blocks(refs, parts, lambda number: scal[2 + number], held, sems)
    heads = out.shape[1] // HD
    total = held.shape[0]
    length = scal[0]

    @pl.when(scal[1] == 0)
    def _():
        low = total - block
        for head in range(heads):
            out_at = head_columns(head)[3]
            _, norm, value = attend_rows(held, head, low, block, length)
            out[low:, out_at] = (value / norm).astype(out.dtype)
            norm = stats[:, heads + head : heads + head + 1]
            out[:low, out_at] = (partial[:, out_at] / norm).astype(out.dtype)

    @pl.when(scal[1] == 1)
    def _():
        for head in range(heads):
            query_at, key_at, value_at, out_at = head_columns(head)
            _, norm, value = attend_rows(held, head, 0, block, length)
            out[:block, out_at] = (value / norm).astype(out.dtype)
            for low in range(0, total - block, block):
                near = slice(low, low + block)
                scores = lax.dot_general(
                    held[low + block : low + 2 * block, query_at],
                    held[:block, key_at],
                    CONTRACT,
                    preferred_element_type=jnp.float32,
                )
                keys = lax.broadcasted_iota(jnp.int32, (1, block), 1)
                scores = scores + jnp.where(keys < length, 0.0, -1e30)
                before = stats[near, head : head + 1]
                top = jnp.maximum(before, jnp.max(scores, axis=-1, keepdims=True))
                probs = jnp.exp2((scores - top) * FACTOR)
                scale = jnp.exp2((before - top) * FACTOR)
                norm = stats[near, heads + head : heads + head + 1] * scale
                norm = norm + jnp.sum(probs, axis=-1, keepdims=True)
                value = partial[near, out_at] * scale + jnp.dot(
                    probs.astype(jnp.bfloat16),
                    held[:block, value_at],
                    preferred_element_type=jnp.float32,
                )
                out[low + block : low + 2 * block, out_at] = (value / norm).astype(out.dtype)


def attend_blocks(arrays, parts, places, length, side, block, partial=None):
    rows = sum(a.shape[0] for a in arrays)
    columns = arrays[0].shape[1]
    wide = columns // (GQ + 2) * GQ
    scal = jnp.stack([length, side] + list(places)).astype(jnp.int32)
    hbm = pl.BlockSpec(memory_space=pltpu.HBM)
    vmem = pl.BlockSpec(memory_space=pltpu.VMEM)
    if partial is None:
        body, name = attend_near_kernel, "attend_near"
        out_shape = [
            jax.ShapeDtypeStruct((rows, wide), jnp.float32),
            jax.ShapeDtypeStruct((rows, HD), jnp.float32),
        ]
    else:
        body, name = attend_far_kernel, "attend_far"
        out_shape = [jax.ShapeDtypeStruct((rows, wide), jnp.bfloat16)]
    extra = [] if partial is None else list(partial)
    return pl.pallas_call(
        functools.partial(body, parts, block),
        out_shape=out_shape,
        in_specs=[pl.BlockSpec(memory_space=pltpu.SMEM)]
        + [hbm] * len(arrays)
        + [vmem] * len(extra),
        out_specs=[vmem] * len(out_shape),
        scratch_shapes=[
            pltpu.VMEM((rows, columns), jnp.bfloat16),
            pltpu.SemaphoreType.DMA((len(places),)),
        ],
        compiler_params=pltpu.CompilerParams(vmem_limit_bytes=VMEM_BYTES),
        cost_estimate=pl.CostEstimate(
            flops=2 * rows * rows * wide,
            bytes_accessed=2 * rows * (columns + wide),
            transcendentals=rows * rows * wide // HD // 2,
        ),
        name=name,
    )(scal, *arrays, *extra)


def after(x, *earlier):
    return lax.optimization_barrier((x,) + earlier)[0]


def four_planes(tokens, w_qkv, norm_gain, q_gain, k_gain, lengths):
    t = lax.axis_index("tensor")
    rows = tokens.shape[0]
    half = rows // 2
    columns = w_qkv.shape[1] // 4
    side = t // 2
    far_end = 3 * (1 - side)
    far_mid = 2 - side

    def slab(block):
        return lax.dynamic_slice(w_qkv, (0, block * columns), (w_qkv.shape[0], columns))

    def across(x, pairs):
        return lax.ppermute(x, "tensor", pairs)

    def exchange(x, bits):
        return across(x, [(i, i ^ bits) for i in range(4)])

    def spread(x):
        return lax.all_gather(x, "fsdp", axis=0, tiled=True)

    swap = [(1, 2), (2, 1)]
    far = [(0, 2), (3, 1)]
    outward = [(1, 0), (2, 3)]

    planes = [t] + [jnp.bitwise_xor(t, m) for m in (1, 2, 3)]
    own, out1, out2, out3 = [slab(p) for p in planes]
    normed = head_norm(tokens.astype(jnp.float32), norm_gain).astype(jnp.bfloat16)
    first, second = normed[:half], normed[half:]

    in2, in3, in1 = exchange(out2, 2), exchange(out3, 3), exchange(out1, 1)
    pair1 = exchange(normed[: rows // 4], 1)
    in1, in2, in3, pair1 = lax.optimization_barrier((in1, in2, in3, pair1))
    swap1 = across(after(first, in1), swap)
    pair2 = exchange(after(normed[rows // 4 : rows // 4 + half], in1), 1)
    swap2 = across(after(second, swap1, pair2), swap)
    pair3 = exchange(after(normed[rows // 4 + half :], pair2), 1)
    on1 = across(swap1, outward)
    far1 = across(after(first, swap2, on1, pair3), far)
    on2 = across(swap2, outward)
    far2 = across(after(second, far1), far)
    on3 = across(far1, outward)

    pieces = [spread(x) for x in (own, in1, in2, in3)]
    middle = jnp.where((t == 1) | (t == 2), 1, 0)
    scal = jnp.stack(planes + [jnp.int32(m) for m in range(4)] + [middle])

    positions = jnp.arange(4 * rows, dtype=jnp.int32)
    angle = angles(positions)
    cos = jnp.concatenate([jnp.cos(angle)] * 2, axis=1)
    sin = jnp.concatenate([-jnp.sin(angle), jnp.sin(angle)], axis=1)
    gains = jnp.stack([q_gain, k_gain])

    made, parts, places = [], [], []

    def run(call):
        listed, first_row = [], 0
        for (block, _), place in call:
            listed.append((first_row, block.shape[0], len(places)))
            first_row += block.shape[0]
            places.append(place)
        parts.append(listed)
        made.append(
            project([b for b, _ in call], [p for _, p in call], pieces, scal, cos, sin, gains)
        )

    pair_place = planes[1] * rows
    run(
        [
            ((normed, normed), t * rows),
            ((pair1, pair1), pair_place),
            ((pair2, pair2), pair_place + rows // 4),
            ((pair3, pair3), pair_place + rows // 4 + half),
        ]
    )
    on4 = across(after(far2, on2, made[0]), outward)
    run([((swap1, on1), far_mid * rows), ((swap2, on2), far_mid * rows + half)])
    near_places = [place - side * rows for place in places]
    partial = attend_blocks(made, parts, near_places, lengths[0] - side * rows, side, rows)
    far1, on3, far2, on4 = [after(x, *partial) for x in (far1, on3, far2, on4)]
    run([((far1, on3), far_end * rows)])
    run([((far2, on4), far_end * rows + half)])
    return attend_blocks(made, parts, places, lengths[0], side, rows, partial)[0]


def solution(mesh):
    placed = (
        P(("groups", "fsdp", "tensor"), None),
        P(("groups", "fsdp", "tensor"), None),
        P(),
        P(),
        P(),
        P(("groups", "fsdp")),
    )
    sizes = dict(mesh.shape)
    body = four_planes if sizes["tensor"] == 4 and sizes["fsdp"] == 4 else any_mesh
    return jax.shard_map(
        body,
        mesh=mesh,
        in_specs=placed,
        out_specs=P(("groups", "fsdp"), "tensor"),
        check_vma=False,
    )
```

```python
import functools
import jax
import jax.numpy as jnp
from jax import lax
from jax.experimental import pallas as pl
from jax.experimental.pallas import tpu as pltpu
from jax.sharding import PartitionSpec as P

KV = 8
HD = 128
GQ = 4
LOG2E = 1.4426950408889634
VMEM_BYTES = 48 * 1024 * 1024


def head_norm(vec, gain):
    scale = lax.rsqrt(jnp.mean(vec * vec, axis=-1, keepdims=True) + 1e-06)
    return vec * scale * gain


def angles(positions):
    half = HD // 2
    freqs = 1000000.0 ** (-2.0 * jnp.arange(half, dtype=jnp.float32) / HD)
    return positions.astype(jnp.float32)[:, None] * freqs[None, :]


def rotate(vec, positions):
    half = vec.shape[-1] // 2
    angle = angles(positions)
    cosine = jnp.cos(angle)[:, None, None, :]
    sine = jnp.sin(angle)[:, None, None, :]
    first = vec[..., :half]
    second = vec[..., half:]
    return jnp.concatenate(
        [first * cosine - second * sine, second * cosine + first * sine], axis=-1
    )


def attend(qkv, q_gain, k_gain, length):
    rows = qkv.shape[0]
    group = qkv.shape[2] - 2
    positions = jnp.arange(rows, dtype=jnp.int32)
    query = rotate(head_norm(qkv[:, :, :group], q_gain), positions).astype(jnp.bfloat16)
    keyed = rotate(head_norm(qkv[:, :, group : group + 1], k_gain), positions)[:, :, 0].astype(
        jnp.bfloat16
    )
    value = qkv[:, :, group + 1].astype(jnp.bfloat16)
    scores = jnp.einsum(
        "ikgd,jkd->kgij", query, keyed, preferred_element_type=jnp.float32
    ) / jnp.sqrt(jnp.float32(qkv.shape[3]))
    allowed = (positions[None, :] <= positions[:, None]) & (positions[None, :] < length)
    scores = jnp.where(allowed[None, None], scores, jnp.float32(-1e30))
    top = jnp.max(scores, axis=-1, keepdims=True)
    weights = jnp.exp(scores - top)
    probs = (weights / jnp.sum(weights, axis=-1, keepdims=True)).astype(jnp.bfloat16)
    out = jnp.einsum("kgij,jkd->ikgd", probs, value, preferred_element_type=jnp.float32)
    return out.reshape(rows, -1).astype(jnp.bfloat16)


def any_mesh(tokens, w_qkv, norm_gain, q_gain, k_gain, lengths):
    tensor_count = lax.axis_size("tensor")
    moved = lax.all_to_all(w_qkv, "tensor", split_axis=1, concat_axis=0, tiled=True)
    weight_cols = lax.all_gather(moved, "fsdp", axis=0, tiled=True)
    normed = head_norm(tokens.astype(jnp.float32), norm_gain).astype(jnp.bfloat16)
    qkv = jnp.dot(
        lax.all_gather(normed, "tensor", axis=0, tiled=True),
        weight_cols,
        preferred_element_type=jnp.float32,
    )
    qkv = qkv.reshape(qkv.shape[0], KV // tensor_count, GQ + 2, HD)
    return attend(qkv, q_gain, k_gain, lengths[0])


def project_kernel(counts, sources, tile, scal, *refs):
    blocks = len(counts)
    arrays = max(source[0] for source in sources) + 1
    middle_rows, end_rows = refs[:blocks], refs[blocks : 2 * blocks]
    refs = refs[2 * blocks :]
    pieces = refs[:arrays]
    cos_ref, sin_ref, gain_ref, out = refs[arrays : arrays + 4]
    taken, held, made, row_sems, sems, out_sems = refs[arrays + 4 :]
    depth = taken.shape[1] // 16
    columns = made.shape[1]
    steps = columns // tile

    def copies(step):
        listed = []
        for index, (array, first, group, slot) in enumerate(sources):
            start = pl.multiple_of((scal[group] * 4 + scal[slot]) * depth, 16)
            low = step * tile
            listed.append(
                pltpu.make_async_copy(
                    pieces[array].at[first : first + depth, low : low + tile],
                    held.at[step % 2, pl.ds(start, depth), :],
                    sems.at[step % 2, index],
                )
            )
        return listed

    starts = [sum(counts[:n]) for n in range(blocks)]
    row_copies = [
        [
            pltpu.make_async_copy(ref, taken.at[first : first + rows, :], row_sems.at[number])
            for ref in (middle_rows[number], end_rows[number])
        ]
        for number, (first, rows) in enumerate(zip(starts, counts))
    ]
    out_copies = []
    for copy in copies(0):
        copy.start()
    for in_middle, in_end in row_copies:
        pl.when(scal[8] == 1)(in_middle.start)
        pl.when(scal[8] == 0)(in_end.start)
    for step in range(steps):
        if step + 1 < steps:
            for copy in copies(step + 1):
                copy.start()
        if step == 0:
            for in_middle, _ in row_copies:
                in_middle.wait()
        for copy in copies(step):
            copy.wait()
        total = jnp.dot(taken[...], held[step % 2], preferred_element_type=jnp.float32)
        for number, (first, rows) in enumerate(zip(starts, counts)):
            place = pl.ds(pl.multiple_of(scal[9 + number], 16), rows)
            cosine = cos_ref[place, :]
            sine = sin_ref[place, :]
            for head in range(tile // HD):
                kind = (step * (tile // HD) + head) % (GQ + 2)
                vec = total[first : first + rows, head * HD : (head + 1) * HD]
                if kind <= GQ:
                    scale = lax.rsqrt(jnp.mean(vec * vec, axis=-1, keepdims=True) + 1e-06)
                    gain = gain_ref[0:1, :] if kind < GQ else gain_ref[1:2, :]
                    vec = vec * scale * gain
                    vec = vec * cosine + pltpu.roll(vec, HD // 2, 1) * sine
                at = step * tile + head * HD
                made[first : first + rows, at : at + HD] = vec.astype(made.dtype)
        at = slice(step * tile, (step + 1) * tile)
        out_copies.append(pltpu.make_async_copy(made.at[:, at], out.at[:, at], out_sems.at[step]))
        out_copies[-1].start()
    for copy in out_copies:
        copy.wait()


def project(rows_list, places, pieces, scal, cos, sin, gains):
    depth = rows_list[0][0].shape[1] // 16
    columns = pieces[0].shape[1]
    sources = [(n, m * depth, 4 + m, n) for n in range(4) for m in range(4)]
    counts = [r.shape[0] for r, _ in rows_list]
    steps = 3
    tile = columns // steps
    count = sum(counts)
    width = rows_list[0][0].shape[1]
    scal = jnp.concatenate([scal, jnp.stack(places)]).astype(jnp.int32)
    vmem = pl.BlockSpec(memory_space=pltpu.VMEM)
    hbm = pl.BlockSpec(memory_space=pltpu.HBM)
    return pl.pallas_call(
        functools.partial(project_kernel, counts, sources, tile),
        out_shape=pltpu.HBM((count, columns), jnp.bfloat16),
        in_specs=[pl.BlockSpec(memory_space=pltpu.SMEM)]
        + [hbm] * (2 * len(counts) + len(pieces))
        + [vmem] * 3,
        out_specs=hbm,
        scratch_shapes=[
            pltpu.VMEM((count, width), jnp.bfloat16),
            pltpu.VMEM((2, width, tile), jnp.bfloat16),
            pltpu.VMEM((count, columns), jnp.bfloat16),
            pltpu.SemaphoreType.DMA((len(counts),)),
            pltpu.SemaphoreType.DMA((2, 16)),
            pltpu.SemaphoreType.DMA((steps,)),
        ],
        compiler_params=pltpu.CompilerParams(vmem_limit_bytes=VMEM_BYTES),
        cost_estimate=pl.CostEstimate(
            flops=2 * count * width * columns,
            bytes_accessed=2 * (width * columns + count * (width + columns)),
            transcendentals=0,
        ),
        name="project",
    )(scal, *[r for r, _ in rows_list], *[r for _, r in rows_list], *pieces, cos, sin, gains)


FACTOR = LOG2E / float(HD) ** 0.5
CONTRACT = (((1,), (1,)), ((), ()))


def fetch_blocks(refs, parts, places, held, sems):
    copies = []
    for ref, blocks in zip(refs, parts):
        for first, rows, number in blocks:
            place = pl.ds(pl.multiple_of(places(number), 16), rows)
            copies.append(
                pltpu.make_async_copy(
                    ref.at[first : first + rows, :], held.at[place, :], sems.at[number]
                )
            )
    for copy in copies:
        copy.start()
    for copy in copies:
        copy.wait()


def head_columns(head):
    base = head // GQ * (GQ + 2) * HD
    query = base + head % GQ * HD
    key = base + GQ * HD
    return (
        slice(query, query + HD),
        slice(key, key + HD),
        slice(key + HD, key + 2 * HD),
        slice(head * HD, (head + 1) * HD),
    )


def attend_rows(held, head, low, block, length):
    query_at, key_at, value_at, _ = head_columns(head)
    high = low + block
    row = lax.broadcasted_iota(jnp.int32, (block, block), 0)
    col = lax.broadcasted_iota(jnp.int32, (block, block), 1)
    query = held[low:high, query_at]
    last = lax.dot_general(
        query, held[low:high, key_at], CONTRACT, preferred_element_type=jnp.float32
    )
    last = jnp.where((col <= row) & (col + low < length), last, -1e30)
    top = jnp.max(last, axis=-1, keepdims=True)
    if low:
        rest = lax.dot_general(
            query, held[:low, key_at], CONTRACT, preferred_element_type=jnp.float32
        )
        keys = lax.broadcasted_iota(jnp.int32, (1, low), 1)
        rest = rest + jnp.where(keys < length, 0.0, -1e30)
        top = jnp.maximum(top, jnp.max(rest, axis=-1, keepdims=True))
    probs = jnp.exp2((last - top) * FACTOR)
    norm = jnp.sum(probs, axis=-1, keepdims=True)
    value = jnp.dot(
        probs.astype(jnp.bfloat16), held[low:high, value_at], preferred_element_type=jnp.float32
    )
    if low:
        probs = jnp.exp2((rest - top) * FACTOR)
        norm = norm + jnp.sum(probs, axis=-1, keepdims=True)
        value = value + jnp.dot(
            probs.astype(jnp.bfloat16), held[:low, value_at], preferred_element_type=jnp.float32
        )
    return top, norm, value


def attend_near_kernel(parts, block, scal, *refs):
    partial, stats, held, sems = refs[len(parts) :]
    fetch_blocks(refs, parts, lambda number: scal[2 + number], held, sems)
    heads = partial.shape[1] // HD
    for head in range(heads):
        out_at = head_columns(head)[3]
        for low in range(0, held.shape[0], block):
            top, norm, value = attend_rows(held, head, low, block, scal[0])
            partial[low : low + block, out_at] = value / norm
            stats[low : low + block, head : head + 1] = top * FACTOR + jnp.log(norm) * LOG2E


def attend_far_kernel(parts, block, scal, *refs):
    partial, stats, out, held, sems = refs[len(parts) :]
    fetch_blocks(refs, parts, lambda number: scal[2 + number], held, sems)
    heads = out.shape[1] // HD
    total = held.shape[0]
    length = scal[0]

    @pl.when(scal[1] == 0)
    def _():
        low = total - block
        for head in range(heads):
            out_at = head_columns(head)[3]
            _, norm, value = attend_rows(held, head, low, block, length)
            out[low:, out_at] = (value / norm).astype(out.dtype)
        out[:low, :] = partial[...].astype(out.dtype)

    @pl.when(scal[1] == 1)
    def _():
        for head in range(heads):
            query_at, key_at, value_at, out_at = head_columns(head)
            _, norm, value = attend_rows(held, head, 0, block, length)
            out[:block, out_at] = (value / norm).astype(out.dtype)
            scores = lax.dot_general(
                held[block:, query_at],
                held[:block, key_at],
                CONTRACT,
                preferred_element_type=jnp.float32,
            )
            keys = lax.broadcasted_iota(jnp.int32, (1, block), 1)
            scores = scores * FACTOR + jnp.where(keys < length, 0.0, -1e30)
            before = stats[:, head : head + 1]
            top = jnp.maximum(before, jnp.max(scores, axis=-1, keepdims=True))
            probs = jnp.exp2(scores - top)
            scale = jnp.exp2(before - top)
            norm = scale + jnp.sum(probs, axis=-1, keepdims=True)
            value = partial[:, out_at] * scale + jnp.dot(
                probs.astype(jnp.bfloat16),
                held[:block, value_at],
                preferred_element_type=jnp.float32,
            )
            out[block:, out_at] = (value / norm).astype(out.dtype)


def attend_blocks(arrays, parts, places, length, side, block, partial=None):
    rows = sum(a.shape[0] for a in arrays)
    columns = arrays[0].shape[1]
    wide = columns // (GQ + 2) * GQ
    scal = jnp.stack([length, side] + list(places)).astype(jnp.int32)
    hbm = pl.BlockSpec(memory_space=pltpu.HBM)
    vmem = pl.BlockSpec(memory_space=pltpu.VMEM)
    if partial is None:
        body, name = attend_near_kernel, "attend_near"
        out_shape = [
            jax.ShapeDtypeStruct((rows, wide), jnp.float32),
            jax.ShapeDtypeStruct((rows, HD), jnp.float32),
        ]
    else:
        body, name = attend_far_kernel, "attend_far"
        out_shape = [jax.ShapeDtypeStruct((rows, wide), jnp.bfloat16)]
    extra = [] if partial is None else list(partial)
    return pl.pallas_call(
        functools.partial(body, parts, block),
        out_shape=out_shape,
        in_specs=[pl.BlockSpec(memory_space=pltpu.SMEM)]
        + [hbm] * len(arrays)
        + [vmem] * len(extra),
        out_specs=[vmem] * len(out_shape),
        scratch_shapes=[
            pltpu.VMEM((rows, columns), jnp.bfloat16),
            pltpu.SemaphoreType.DMA((len(places),)),
        ],
        compiler_params=pltpu.CompilerParams(vmem_limit_bytes=VMEM_BYTES),
        cost_estimate=pl.CostEstimate(
            flops=2 * rows * rows * wide,
            bytes_accessed=2 * rows * (columns + wide),
            transcendentals=rows * rows * wide // HD // 2,
        ),
        name=name,
    )(scal, *arrays, *extra)


def after(x, *earlier):
    return lax.optimization_barrier((x,) + earlier)[0]


def four_planes(tokens, w_qkv, norm_gain, q_gain, k_gain, lengths):
    t = lax.axis_index("tensor")
    rows = tokens.shape[0]
    half = rows // 2
    columns = w_qkv.shape[1] // 4
    side = t // 2
    far_end = 3 * (1 - side)
    far_mid = 2 - side

    def slab(block):
        return lax.dynamic_slice(w_qkv, (0, block * columns), (w_qkv.shape[0], columns))

    def across(x, pairs):
        return lax.ppermute(x, "tensor", pairs)

    def exchange(x, bits):
        return across(x, [(i, i ^ bits) for i in range(4)])

    def spread(x):
        return lax.all_gather(x, "fsdp", axis=0, tiled=True)

    swap = [(1, 2), (2, 1)]
    far = [(0, 2), (3, 1)]
    outward = [(1, 0), (2, 3)]

    planes = [t] + [jnp.bitwise_xor(t, m) for m in (1, 2, 3)]
    own, out1, out2, out3 = [slab(p) for p in planes]
    normed = head_norm(tokens.astype(jnp.float32), norm_gain).astype(jnp.bfloat16)
    first, second = normed[:half], normed[half:]

    in2, in3, in1 = exchange(out2, 2), exchange(out3, 3), exchange(out1, 1)
    pair1 = exchange(first, 1)
    in1, in2, in3, pair1 = lax.optimization_barrier((in1, in2, in3, pair1))
    swap1 = across(after(first, in1), swap)
    pair2 = exchange(after(second, swap1), 1)
    on1 = across(swap1, outward)
    swap2 = across(after(second, swap1), swap)
    far1 = across(after(first, swap2), far)
    on2 = across(swap2, outward)
    far2 = across(after(second, far1, pair2, on1), far)
    on3 = across(far1, outward)

    pieces = [spread(x) for x in (own, in1, in2, in3)]
    middle = jnp.where((t == 1) | (t == 2), 1, 0)
    scal = jnp.stack(planes + [jnp.int32(m) for m in range(4)] + [middle])

    positions = jnp.arange(4 * rows, dtype=jnp.int32)
    angle = angles(positions)
    cos = jnp.concatenate([jnp.cos(angle)] * 2, axis=1)
    sin = jnp.concatenate([-jnp.sin(angle), jnp.sin(angle)], axis=1)
    gains = jnp.stack([q_gain, k_gain])

    made, parts, places = [], [], []

    def run(call):
        listed, first_row = [], 0
        for (block, _), place in call:
            listed.append((first_row, block.shape[0], len(places)))
            first_row += block.shape[0]
            places.append(place)
        parts.append(listed)
        made.append(
            project([b for b, _ in call], [p for _, p in call], pieces, scal, cos, sin, gains)
        )

    pair_place = planes[1] * rows
    run(
        [
            ((normed, normed), t * rows),
            ((pair1, pair1), pair_place),
            ((pair2, pair2), pair_place + half),
        ]
    )
    on4 = across(after(far2, on2, made[0]), outward)
    swap2, on2 = after(swap2, on3), after(on2, on3)
    run([((swap1, on1), far_mid * rows), ((swap2, on2), far_mid * rows + half)])
    near_places = [place - side * rows for place in places]
    partial = attend_blocks(made, parts, near_places, lengths[0] - side * rows, side, rows)
    far1, on3, far2, on4 = [after(x, *partial) for x in (far1, on3, far2, on4)]
    run([((far1, on3), far_end * rows), ((far2, on4), far_end * rows + half)])
    return attend_blocks(made, parts, places, lengths[0], side, rows, partial)[0]


def solution(mesh):
    placed = (
        P(("groups", "fsdp", "tensor"), None),
        P(("groups", "fsdp", "tensor"), None),
        P(),
        P(),
        P(),
        P(("groups", "fsdp")),
    )
    sizes = dict(mesh.shape)
    body = four_planes if sizes["tensor"] == 4 and sizes["fsdp"] == 4 else any_mesh
    return jax.shard_map(
        body,
        mesh=mesh,
        in_specs=placed,
        out_specs=P(("groups", "fsdp"), "tensor"),
        check_vma=False,
    )
```

```python
import functools
import jax
import jax.numpy as jnp
from jax import lax
from jax.experimental import pallas as pl
from jax.experimental.pallas import tpu as pltpu
from jax.sharding import PartitionSpec as P

KV = 8
HD = 128
GQ = 4
LOG2E = 1.4426950408889634
VMEM_BYTES = 48 * 1024 * 1024


def head_norm(vec, gain):
    scale = lax.rsqrt(jnp.mean(vec * vec, axis=-1, keepdims=True) + 1e-06)
    return vec * scale * gain


def angles(positions):
    half = HD // 2
    freqs = 1000000.0 ** (-2.0 * jnp.arange(half, dtype=jnp.float32) / HD)
    return positions.astype(jnp.float32)[:, None] * freqs[None, :]


def rotate(vec, positions):
    half = vec.shape[-1] // 2
    angle = angles(positions)
    cosine = jnp.cos(angle)[:, None, None, :]
    sine = jnp.sin(angle)[:, None, None, :]
    first = vec[..., :half]
    second = vec[..., half:]
    return jnp.concatenate(
        [first * cosine - second * sine, second * cosine + first * sine], axis=-1
    )


def attend(qkv, q_gain, k_gain, length):
    rows = qkv.shape[0]
    group = qkv.shape[2] - 2
    positions = jnp.arange(rows, dtype=jnp.int32)
    query = rotate(head_norm(qkv[:, :, :group], q_gain), positions).astype(jnp.bfloat16)
    keyed = rotate(head_norm(qkv[:, :, group : group + 1], k_gain), positions)[:, :, 0].astype(
        jnp.bfloat16
    )
    value = qkv[:, :, group + 1].astype(jnp.bfloat16)
    scores = jnp.einsum(
        "ikgd,jkd->kgij", query, keyed, preferred_element_type=jnp.float32
    ) / jnp.sqrt(jnp.float32(qkv.shape[3]))
    allowed = (positions[None, :] <= positions[:, None]) & (positions[None, :] < length)
    scores = jnp.where(allowed[None, None], scores, jnp.float32(-1e30))
    top = jnp.max(scores, axis=-1, keepdims=True)
    weights = jnp.exp(scores - top)
    probs = (weights / jnp.sum(weights, axis=-1, keepdims=True)).astype(jnp.bfloat16)
    out = jnp.einsum("kgij,jkd->ikgd", probs, value, preferred_element_type=jnp.float32)
    return out.reshape(rows, -1).astype(jnp.bfloat16)


def any_mesh(tokens, w_qkv, norm_gain, q_gain, k_gain, lengths):
    tensor_count = lax.axis_size("tensor")
    moved = lax.all_to_all(w_qkv, "tensor", split_axis=1, concat_axis=0, tiled=True)
    weight_cols = lax.all_gather(moved, "fsdp", axis=0, tiled=True)
    normed = head_norm(tokens.astype(jnp.float32), norm_gain).astype(jnp.bfloat16)
    qkv = jnp.dot(
        lax.all_gather(normed, "tensor", axis=0, tiled=True),
        weight_cols,
        preferred_element_type=jnp.float32,
    )
    qkv = qkv.reshape(qkv.shape[0], KV // tensor_count, GQ + 2, HD)
    return attend(qkv, q_gain, k_gain, lengths[0])


def project_kernel(counts, sources, tile, scal, *refs):
    blocks = len(counts)
    arrays = max(source[0] for source in sources) + 1
    middle_rows, end_rows = refs[:blocks], refs[blocks : 2 * blocks]
    refs = refs[2 * blocks :]
    pieces = refs[:arrays]
    cos_ref, sin_ref, gain_ref, out = refs[arrays : arrays + 4]
    taken, held, made, row_sems, sems, out_sems = refs[arrays + 4 :]
    depth = taken.shape[1] // 16
    columns = made.shape[1]
    steps = columns // tile

    def copies(step):
        listed = []
        for index, (array, first, group, slot) in enumerate(sources):
            start = pl.multiple_of((scal[group] * 4 + scal[slot]) * depth, 16)
            low = step * tile
            listed.append(
                pltpu.make_async_copy(
                    pieces[array].at[first : first + depth, low : low + tile],
                    held.at[step % 2, pl.ds(start, depth), :],
                    sems.at[step % 2, index],
                )
            )
        return listed

    starts = [sum(counts[:n]) for n in range(blocks)]
    row_copies = [
        [
            pltpu.make_async_copy(ref, taken.at[first : first + rows, :], row_sems.at[number])
            for ref in (middle_rows[number], end_rows[number])
        ]
        for number, (first, rows) in enumerate(zip(starts, counts))
    ]
    out_copies = []
    for copy in copies(0):
        copy.start()
    for in_middle, in_end in row_copies:
        pl.when(scal[8] == 1)(in_middle.start)
        pl.when(scal[8] == 0)(in_end.start)
    for step in range(steps):
        if step + 1 < steps:
            for copy in copies(step + 1):
                copy.start()
        if step == 0:
            for in_middle, _ in row_copies:
                in_middle.wait()
        for copy in copies(step):
            copy.wait()
        total = jnp.dot(taken[...], held[step % 2], preferred_element_type=jnp.float32)
        for number, (first, rows) in enumerate(zip(starts, counts)):
            place = pl.ds(pl.multiple_of(scal[9 + number], 16), rows)
            cosine = cos_ref[place, :]
            sine = sin_ref[place, :]
            for head in range(tile // HD):
                kind = (step * (tile // HD) + head) % (GQ + 2)
                vec = total[first : first + rows, head * HD : (head + 1) * HD]
                if kind <= GQ:
                    scale = lax.rsqrt(jnp.mean(vec * vec, axis=-1, keepdims=True) + 1e-06)
                    gain = gain_ref[0:1, :] if kind < GQ else gain_ref[1:2, :]
                    vec = vec * scale * gain
                    vec = vec * cosine + pltpu.roll(vec, HD // 2, 1) * sine
                at = step * tile + head * HD
                made[first : first + rows, at : at + HD] = vec.astype(made.dtype)
        at = slice(step * tile, (step + 1) * tile)
        out_copies.append(pltpu.make_async_copy(made.at[:, at], out.at[:, at], out_sems.at[step]))
        out_copies[-1].start()
    for copy in out_copies:
        copy.wait()


def project(rows_list, places, pieces, scal, cos, sin, gains):
    depth = rows_list[0][0].shape[1] // 16
    columns = pieces[0].shape[1]
    sources = [(n, m * depth, 4 + m, n) for n in range(4) for m in range(4)]
    counts = [r.shape[0] for r, _ in rows_list]
    steps = 3
    tile = columns // steps
    count = sum(counts)
    width = rows_list[0][0].shape[1]
    scal = jnp.concatenate([scal, jnp.stack(places)]).astype(jnp.int32)
    vmem = pl.BlockSpec(memory_space=pltpu.VMEM)
    hbm = pl.BlockSpec(memory_space=pltpu.HBM)
    return pl.pallas_call(
        functools.partial(project_kernel, counts, sources, tile),
        out_shape=pltpu.HBM((count, columns), jnp.bfloat16),
        in_specs=[pl.BlockSpec(memory_space=pltpu.SMEM)]
        + [hbm] * (2 * len(counts) + len(pieces))
        + [vmem] * 3,
        out_specs=hbm,
        scratch_shapes=[
            pltpu.VMEM((count, width), jnp.bfloat16),
            pltpu.VMEM((2, width, tile), jnp.bfloat16),
            pltpu.VMEM((count, columns), jnp.bfloat16),
            pltpu.SemaphoreType.DMA((len(counts),)),
            pltpu.SemaphoreType.DMA((2, 16)),
            pltpu.SemaphoreType.DMA((steps,)),
        ],
        compiler_params=pltpu.CompilerParams(vmem_limit_bytes=VMEM_BYTES),
        cost_estimate=pl.CostEstimate(
            flops=2 * count * width * columns,
            bytes_accessed=2 * (width * columns + count * (width + columns)),
            transcendentals=0,
        ),
        name="project",
    )(scal, *[r for r, _ in rows_list], *[r for _, r in rows_list], *pieces, cos, sin, gains)


FACTOR = LOG2E / float(HD) ** 0.5
CONTRACT = (((1,), (1,)), ((), ()))


def fetch_blocks(refs, parts, places, held, sems):
    copies = []
    for ref, blocks in zip(refs, parts):
        for first, rows, number in blocks:
            place = pl.ds(pl.multiple_of(places(number), 16), rows)
            copies.append(
                pltpu.make_async_copy(
                    ref.at[first : first + rows, :], held.at[place, :], sems.at[number]
                )
            )
    for copy in copies:
        copy.start()
    for copy in copies:
        copy.wait()


def head_columns(head):
    base = head // GQ * (GQ + 2) * HD
    query = base + head % GQ * HD
    key = base + GQ * HD
    return (
        slice(query, query + HD),
        slice(key, key + HD),
        slice(key + HD, key + 2 * HD),
        slice(head * HD, (head + 1) * HD),
    )


def attend_rows(held, head, low, block, length):
    query_at, key_at, value_at, _ = head_columns(head)
    high = low + block
    row = lax.broadcasted_iota(jnp.int32, (block, block), 0)
    col = lax.broadcasted_iota(jnp.int32, (block, block), 1)
    query = held[low:high, query_at]
    last = lax.dot_general(
        query, held[low:high, key_at], CONTRACT, preferred_element_type=jnp.float32
    )
    last = jnp.where((col <= row) & (col + low < length), last, -1e30)
    top = jnp.max(last, axis=-1, keepdims=True)
    if low:
        rest = lax.dot_general(
            query, held[:low, key_at], CONTRACT, preferred_element_type=jnp.float32
        )
        keys = lax.broadcasted_iota(jnp.int32, (1, low), 1)
        rest = rest + jnp.where(keys < length, 0.0, -1e30)
        top = jnp.maximum(top, jnp.max(rest, axis=-1, keepdims=True))
    probs = jnp.exp2((last - top) * FACTOR)
    norm = jnp.sum(probs, axis=-1, keepdims=True)
    value = jnp.dot(
        probs.astype(jnp.bfloat16), held[low:high, value_at], preferred_element_type=jnp.float32
    )
    if low:
        probs = jnp.exp2((rest - top) * FACTOR)
        norm = norm + jnp.sum(probs, axis=-1, keepdims=True)
        value = value + jnp.dot(
            probs.astype(jnp.bfloat16), held[:low, value_at], preferred_element_type=jnp.float32
        )
    return top, norm, value


def attend_near_kernel(parts, block, scal, *refs):
    partial, stats, held, sems = refs[len(parts) :]
    fetch_blocks(refs, parts, lambda number: scal[2 + number], held, sems)
    heads = partial.shape[1] // HD
    for head in range(heads):
        out_at = head_columns(head)[3]
        for low in range(0, held.shape[0], block):
            top, norm, value = attend_rows(held, head, low, block, scal[0])
            partial[low : low + block, out_at] = value / norm
            stats[low : low + block, head : head + 1] = top * FACTOR + jnp.log(norm) * LOG2E


def attend_far_kernel(parts, block, scal, *refs):
    partial, stats, out, held, sems = refs[len(parts) :]
    fetch_blocks(refs, parts, lambda number: scal[2 + number], held, sems)
    heads = out.shape[1] // HD
    total = held.shape[0]
    length = scal[0]

    @pl.when(scal[1] == 0)
    def _():
        low = total - block
        for head in range(heads):
            out_at = head_columns(head)[3]
            _, norm, value = attend_rows(held, head, low, block, length)
            out[low:, out_at] = (value / norm).astype(out.dtype)
        out[:low, :] = partial[...].astype(out.dtype)

    @pl.when(scal[1] == 1)
    def _():
        for head in range(heads):
            query_at, key_at, value_at, out_at = head_columns(head)
            _, norm, value = attend_rows(held, head, 0, block, length)
            out[:block, out_at] = (value / norm).astype(out.dtype)
            scores = lax.dot_general(
                held[block:, query_at],
                held[:block, key_at],
                CONTRACT,
                preferred_element_type=jnp.float32,
            )
            keys = lax.broadcasted_iota(jnp.int32, (1, block), 1)
            scores = scores * FACTOR + jnp.where(keys < length, 0.0, -1e30)
            before = stats[:, head : head + 1]
            top = jnp.maximum(before, jnp.max(scores, axis=-1, keepdims=True))
            probs = jnp.exp2(scores - top)
            scale = jnp.exp2(before - top)
            norm = scale + jnp.sum(probs, axis=-1, keepdims=True)
            value = partial[:, out_at] * scale + jnp.dot(
                probs.astype(jnp.bfloat16),
                held[:block, value_at],
                preferred_element_type=jnp.float32,
            )
            out[block:, out_at] = (value / norm).astype(out.dtype)


def attend_blocks(arrays, parts, places, length, side, block, partial=None):
    rows = sum(a.shape[0] for a in arrays)
    columns = arrays[0].shape[1]
    wide = columns // (GQ + 2) * GQ
    scal = jnp.stack([length, side] + list(places)).astype(jnp.int32)
    hbm = pl.BlockSpec(memory_space=pltpu.HBM)
    vmem = pl.BlockSpec(memory_space=pltpu.VMEM)
    if partial is None:
        body, name = attend_near_kernel, "attend_near"
        out_shape = [
            jax.ShapeDtypeStruct((rows, wide), jnp.float32),
            jax.ShapeDtypeStruct((rows, HD), jnp.float32),
        ]
    else:
        body, name = attend_far_kernel, "attend_far"
        out_shape = [jax.ShapeDtypeStruct((rows, wide), jnp.bfloat16)]
    extra = [] if partial is None else list(partial)
    return pl.pallas_call(
        functools.partial(body, parts, block),
        out_shape=out_shape,
        in_specs=[pl.BlockSpec(memory_space=pltpu.SMEM)]
        + [hbm] * len(arrays)
        + [vmem] * len(extra),
        out_specs=[vmem] * len(out_shape),
        scratch_shapes=[
            pltpu.VMEM((rows, columns), jnp.bfloat16),
            pltpu.SemaphoreType.DMA((len(places),)),
        ],
        compiler_params=pltpu.CompilerParams(vmem_limit_bytes=VMEM_BYTES),
        cost_estimate=pl.CostEstimate(
            flops=2 * rows * rows * wide,
            bytes_accessed=2 * rows * (columns + wide),
            transcendentals=rows * rows * wide // HD // 2,
        ),
        name=name,
    )(scal, *arrays, *extra)


def after(x, *earlier):
    return lax.optimization_barrier((x,) + earlier)[0]


def four_planes(tokens, w_qkv, norm_gain, q_gain, k_gain, lengths):
    t = lax.axis_index("tensor")
    rows = tokens.shape[0]
    half = rows // 2
    columns = w_qkv.shape[1] // 4
    side = t // 2
    far_end = 3 * (1 - side)
    far_mid = 2 - side

    def slab(block):
        return lax.dynamic_slice(w_qkv, (0, block * columns), (w_qkv.shape[0], columns))

    def across(x, pairs):
        return lax.ppermute(x, "tensor", pairs)

    def exchange(x, bits):
        return across(x, [(i, i ^ bits) for i in range(4)])

    def spread(x):
        return lax.all_gather(x, "fsdp", axis=0, tiled=True)

    swap = [(1, 2), (2, 1)]
    far = [(0, 2), (3, 1)]
    outward = [(1, 0), (2, 3)]

    planes = [t] + [jnp.bitwise_xor(t, m) for m in (1, 2, 3)]
    own, out1, out2, out3 = [slab(p) for p in planes]
    normed = head_norm(tokens.astype(jnp.float32), norm_gain).astype(jnp.bfloat16)
    first, second = normed[:half], normed[half:]

    in2, in3, in1 = exchange(out2, 2), exchange(out3, 3), exchange(out1, 1)
    quarter = rows // 4
    pair1 = exchange(normed[:quarter], 1)
    in1, in2, in3, pair1 = lax.optimization_barrier((in1, in2, in3, pair1))
    swap1 = across(after(first, in1), swap)
    pair2 = exchange(after(normed[quarter : quarter + half], in1), 1)
    pair3 = exchange(after(normed[quarter + half :], in1), 1)
    swap2 = across(after(second, swap1, pair2), swap)
    on1 = across(after(swap1, pair3), outward)
    far1 = across(after(first, swap2), far)
    on2 = across(swap2, outward)
    far2 = across(after(second, far1, on1), far)
    on3 = across(far1, outward)

    pieces = [spread(x) for x in (own, in1, in2, in3)]
    middle = jnp.where((t == 1) | (t == 2), 1, 0)
    scal = jnp.stack(planes + [jnp.int32(m) for m in range(4)] + [middle])

    positions = jnp.arange(4 * rows, dtype=jnp.int32)
    angle = angles(positions)
    cos = jnp.concatenate([jnp.cos(angle)] * 2, axis=1)
    sin = jnp.concatenate([-jnp.sin(angle), jnp.sin(angle)], axis=1)
    gains = jnp.stack([q_gain, k_gain])

    made, parts, places = [], [], []

    def run(call):
        listed, first_row = [], 0
        for (block, _), place in call:
            listed.append((first_row, block.shape[0], len(places)))
            first_row += block.shape[0]
            places.append(place)
        parts.append(listed)
        made.append(
            project([b for b, _ in call], [p for _, p in call], pieces, scal, cos, sin, gains)
        )

    pair_place = planes[1] * rows
    run(
        [
            ((normed, normed), t * rows),
            ((pair1, pair1), pair_place),
            ((pair2, pair2), pair_place + quarter),
            ((pair3, pair3), pair_place + quarter + half),
        ]
    )
    on4 = across(after(far2, on2, made[0]), outward)
    swap2, on2 = after(swap2, on3), after(on2, on3)
    run([((swap1, on1), far_mid * rows), ((swap2, on2), far_mid * rows + half)])
    near_places = [place - side * rows for place in places]
    partial = attend_blocks(made, parts, near_places, lengths[0] - side * rows, side, rows)
    far1, on3, far2, on4 = [after(x, *partial) for x in (far1, on3, far2, on4)]
    run([((far1, on3), far_end * rows), ((far2, on4), far_end * rows + half)])
    return attend_blocks(made, parts, places, lengths[0], side, rows, partial)[0]


def solution(mesh):
    placed = (
        P(("groups", "fsdp", "tensor"), None),
        P(("groups", "fsdp", "tensor"), None),
        P(),
        P(),
        P(),
        P(("groups", "fsdp")),
    )
    sizes = dict(mesh.shape)
    body = four_planes if sizes["tensor"] == 4 and sizes["fsdp"] == 4 else any_mesh
    return jax.shard_map(
        body,
        mesh=mesh,
        in_specs=placed,
        out_specs=P(("groups", "fsdp"), "tensor"),
        check_vma=False,
    )
```

```python
import functools
import jax
import jax.numpy as jnp
from jax import lax
from jax.experimental import pallas as pl
from jax.experimental.pallas import tpu as pltpu
from jax.sharding import PartitionSpec as P

KV = 8
HD = 128
GQ = 4
LOG2E = 1.4426950408889634
VMEM_BYTES = 48 * 1024 * 1024


def head_norm(vec, gain):
    scale = lax.rsqrt(jnp.mean(vec * vec, axis=-1, keepdims=True) + 1e-06)
    return vec * scale * gain


def angles(positions):
    half = HD // 2
    freqs = 1000000.0 ** (-2.0 * jnp.arange(half, dtype=jnp.float32) / HD)
    return positions.astype(jnp.float32)[:, None] * freqs[None, :]


def rotate(vec, positions):
    half = vec.shape[-1] // 2
    angle = angles(positions)
    cosine = jnp.cos(angle)[:, None, None, :]
    sine = jnp.sin(angle)[:, None, None, :]
    first = vec[..., :half]
    second = vec[..., half:]
    return jnp.concatenate(
        [first * cosine - second * sine, second * cosine + first * sine], axis=-1
    )


def attend(qkv, q_gain, k_gain, length):
    rows = qkv.shape[0]
    group = qkv.shape[2] - 2
    positions = jnp.arange(rows, dtype=jnp.int32)
    query = rotate(head_norm(qkv[:, :, :group], q_gain), positions).astype(jnp.bfloat16)
    keyed = rotate(head_norm(qkv[:, :, group : group + 1], k_gain), positions)[:, :, 0].astype(
        jnp.bfloat16
    )
    value = qkv[:, :, group + 1].astype(jnp.bfloat16)
    scores = jnp.einsum(
        "ikgd,jkd->kgij", query, keyed, preferred_element_type=jnp.float32
    ) / jnp.sqrt(jnp.float32(qkv.shape[3]))
    allowed = (positions[None, :] <= positions[:, None]) & (positions[None, :] < length)
    scores = jnp.where(allowed[None, None], scores, jnp.float32(-1e30))
    top = jnp.max(scores, axis=-1, keepdims=True)
    weights = jnp.exp(scores - top)
    probs = (weights / jnp.sum(weights, axis=-1, keepdims=True)).astype(jnp.bfloat16)
    out = jnp.einsum("kgij,jkd->ikgd", probs, value, preferred_element_type=jnp.float32)
    return out.reshape(rows, -1).astype(jnp.bfloat16)


def any_mesh(tokens, w_qkv, norm_gain, q_gain, k_gain, lengths):
    tensor_count = lax.axis_size("tensor")
    moved = lax.all_to_all(w_qkv, "tensor", split_axis=1, concat_axis=0, tiled=True)
    weight_cols = lax.all_gather(moved, "fsdp", axis=0, tiled=True)
    normed = head_norm(tokens.astype(jnp.float32), norm_gain).astype(jnp.bfloat16)
    qkv = jnp.dot(
        lax.all_gather(normed, "tensor", axis=0, tiled=True),
        weight_cols,
        preferred_element_type=jnp.float32,
    )
    qkv = qkv.reshape(qkv.shape[0], KV // tensor_count, GQ + 2, HD)
    return attend(qkv, q_gain, k_gain, lengths[0])


def project_kernel(counts, sources, tile, scal, *refs):
    blocks = len(counts)
    arrays = max(source[0] for source in sources) + 1
    middle_rows, end_rows = refs[:blocks], refs[blocks : 2 * blocks]
    refs = refs[2 * blocks :]
    pieces = refs[:arrays]
    cos_ref, sin_ref, gain_ref, out = refs[arrays : arrays + 4]
    taken, held, made, row_sems, sems, out_sems = refs[arrays + 4 :]
    depth = taken.shape[1] // 16
    columns = made.shape[1]
    steps = columns // tile

    def copies(step):
        listed = []
        for index, (array, first, group, slot) in enumerate(sources):
            start = pl.multiple_of((scal[group] * 4 + scal[slot]) * depth, 16)
            low = step * tile
            listed.append(
                pltpu.make_async_copy(
                    pieces[array].at[first : first + depth, low : low + tile],
                    held.at[step % 2, pl.ds(start, depth), :],
                    sems.at[step % 2, index],
                )
            )
        return listed

    starts = [sum(counts[:n]) for n in range(blocks)]
    row_copies = [
        [
            pltpu.make_async_copy(ref, taken.at[first : first + rows, :], row_sems.at[number])
            for ref in (middle_rows[number], end_rows[number])
        ]
        for number, (first, rows) in enumerate(zip(starts, counts))
    ]
    out_copies = []
    for copy in copies(0):
        copy.start()
    for in_middle, in_end in row_copies:
        pl.when(scal[8] == 1)(in_middle.start)
        pl.when(scal[8] == 0)(in_end.start)
    for step in range(steps):
        if step + 1 < steps:
            for copy in copies(step + 1):
                copy.start()
        if step == 0:
            for in_middle, _ in row_copies:
                in_middle.wait()
        for copy in copies(step):
            copy.wait()
        total = jnp.dot(taken[...], held[step % 2], preferred_element_type=jnp.float32)
        for number, (first, rows) in enumerate(zip(starts, counts)):
            place = pl.ds(pl.multiple_of(scal[9 + number], 16), rows)
            cosine = cos_ref[place, :]
            sine = sin_ref[place, :]
            for head in range(tile // HD):
                kind = (step * (tile // HD) + head) % (GQ + 2)
                vec = total[first : first + rows, head * HD : (head + 1) * HD]
                if kind <= GQ:
                    scale = lax.rsqrt(jnp.mean(vec * vec, axis=-1, keepdims=True) + 1e-06)
                    gain = gain_ref[0:1, :] if kind < GQ else gain_ref[1:2, :]
                    vec = vec * scale * gain
                    vec = vec * cosine + pltpu.roll(vec, HD // 2, 1) * sine
                at = step * tile + head * HD
                made[first : first + rows, at : at + HD] = vec.astype(made.dtype)
        at = slice(step * tile, (step + 1) * tile)
        out_copies.append(pltpu.make_async_copy(made.at[:, at], out.at[:, at], out_sems.at[step]))
        out_copies[-1].start()
    for copy in out_copies:
        copy.wait()


def project(rows_list, places, pieces, scal, cos, sin, gains):
    depth = rows_list[0][0].shape[1] // 16
    columns = pieces[0].shape[1]
    sources = [(n, m * depth, 4 + m, n) for n in range(4) for m in range(4)]
    counts = [r.shape[0] for r, _ in rows_list]
    steps = 3
    tile = columns // steps
    count = sum(counts)
    width = rows_list[0][0].shape[1]
    scal = jnp.concatenate([scal, jnp.stack(places)]).astype(jnp.int32)
    vmem = pl.BlockSpec(memory_space=pltpu.VMEM)
    hbm = pl.BlockSpec(memory_space=pltpu.HBM)
    return pl.pallas_call(
        functools.partial(project_kernel, counts, sources, tile),
        out_shape=pltpu.HBM((count, columns), jnp.bfloat16),
        in_specs=[pl.BlockSpec(memory_space=pltpu.SMEM)]
        + [hbm] * (2 * len(counts) + len(pieces))
        + [vmem] * 3,
        out_specs=hbm,
        scratch_shapes=[
            pltpu.VMEM((count, width), jnp.bfloat16),
            pltpu.VMEM((2, width, tile), jnp.bfloat16),
            pltpu.VMEM((count, columns), jnp.bfloat16),
            pltpu.SemaphoreType.DMA((len(counts),)),
            pltpu.SemaphoreType.DMA((2, 16)),
            pltpu.SemaphoreType.DMA((steps,)),
        ],
        compiler_params=pltpu.CompilerParams(vmem_limit_bytes=VMEM_BYTES),
        cost_estimate=pl.CostEstimate(
            flops=2 * count * width * columns,
            bytes_accessed=2 * (width * columns + count * (width + columns)),
            transcendentals=0,
        ),
        name="project",
    )(scal, *[r for r, _ in rows_list], *[r for _, r in rows_list], *pieces, cos, sin, gains)


FACTOR = LOG2E / float(HD) ** 0.5
CONTRACT = (((1,), (1,)), ((), ()))


def fetch_blocks(refs, parts, places, held, sems):
    copies = []
    for ref, blocks in zip(refs, parts):
        for first, rows, number in blocks:
            place = pl.ds(pl.multiple_of(places(number), 16), rows)
            copies.append(
                pltpu.make_async_copy(
                    ref.at[first : first + rows, :], held.at[place, :], sems.at[number]
                )
            )
    for copy in copies:
        copy.start()
    for copy in copies:
        copy.wait()


def head_columns(head):
    base = head // GQ * (GQ + 2) * HD
    query = base + head % GQ * HD
    key = base + GQ * HD
    return (
        slice(query, query + HD),
        slice(key, key + HD),
        slice(key + HD, key + 2 * HD),
        slice(head * HD, (head + 1) * HD),
    )


def attend_rows(held, head, low, block, length):
    query_at, key_at, value_at, _ = head_columns(head)
    high = low + block
    row = lax.broadcasted_iota(jnp.int32, (block, block), 0)
    col = lax.broadcasted_iota(jnp.int32, (block, block), 1)
    query = held[low:high, query_at]
    last = lax.dot_general(
        query, held[low:high, key_at], CONTRACT, preferred_element_type=jnp.float32
    )
    last = jnp.where((col <= row) & (col + low < length), last, -1e30)
    top = jnp.max(last, axis=-1, keepdims=True)
    if low:
        rest = lax.dot_general(
            query, held[:low, key_at], CONTRACT, preferred_element_type=jnp.float32
        )
        keys = lax.broadcasted_iota(jnp.int32, (1, low), 1)
        rest = rest + jnp.where(keys < length, 0.0, -1e30)
        top = jnp.maximum(top, jnp.max(rest, axis=-1, keepdims=True))
    probs = jnp.exp2((last - top) * FACTOR)
    norm = jnp.sum(probs, axis=-1, keepdims=True)
    value = jnp.dot(
        probs.astype(jnp.bfloat16), held[low:high, value_at], preferred_element_type=jnp.float32
    )
    if low:
        probs = jnp.exp2((rest - top) * FACTOR)
        norm = norm + jnp.sum(probs, axis=-1, keepdims=True)
        value = value + jnp.dot(
            probs.astype(jnp.bfloat16), held[:low, value_at], preferred_element_type=jnp.float32
        )
    return top, norm, value


def attend_near_kernel(parts, block, scal, *refs):
    partial, stats, held, sems = refs[len(parts) :]
    fetch_blocks(refs, parts, lambda number: scal[2 + number], held, sems)
    heads = partial.shape[1] // HD
    for head in range(heads):
        out_at = head_columns(head)[3]
        for low in range(0, held.shape[0], block):
            top, norm, value = attend_rows(held, head, low, block, scal[0])
            partial[low : low + block, out_at] = value / norm
            stats[low : low + block, head : head + 1] = top * FACTOR + jnp.log(norm) * LOG2E


def attend_far_kernel(parts, block, scal, *refs):
    partial, stats, out, held, sems = refs[len(parts) :]
    fetch_blocks(refs, parts, lambda number: scal[2 + number], held, sems)
    heads = out.shape[1] // HD
    total = held.shape[0]
    length = scal[0]

    @pl.when(scal[1] == 0)
    def _():
        low = total - block
        for head in range(heads):
            out_at = head_columns(head)[3]
            _, norm, value = attend_rows(held, head, low, block, length)
            out[low:, out_at] = (value / norm).astype(out.dtype)
        out[:low, :] = partial[...].astype(out.dtype)

    @pl.when(scal[1] == 1)
    def _():
        for head in range(heads):
            query_at, key_at, value_at, out_at = head_columns(head)
            _, norm, value = attend_rows(held, head, 0, block, length)
            out[:block, out_at] = (value / norm).astype(out.dtype)
            scores = lax.dot_general(
                held[block:, query_at],
                held[:block, key_at],
                CONTRACT,
                preferred_element_type=jnp.float32,
            )
            keys = lax.broadcasted_iota(jnp.int32, (1, block), 1)
            scores = scores * FACTOR + jnp.where(keys < length, 0.0, -1e30)
            before = stats[:, head : head + 1]
            top = jnp.maximum(before, jnp.max(scores, axis=-1, keepdims=True))
            probs = jnp.exp2(scores - top)
            scale = jnp.exp2(before - top)
            norm = scale + jnp.sum(probs, axis=-1, keepdims=True)
            value = partial[:, out_at] * scale + jnp.dot(
                probs.astype(jnp.bfloat16),
                held[:block, value_at],
                preferred_element_type=jnp.float32,
            )
            out[block:, out_at] = (value / norm).astype(out.dtype)


def attend_blocks(arrays, parts, places, length, side, block, partial=None):
    rows = sum(a.shape[0] for a in arrays)
    columns = arrays[0].shape[1]
    wide = columns // (GQ + 2) * GQ
    scal = jnp.stack([length, side] + list(places)).astype(jnp.int32)
    hbm = pl.BlockSpec(memory_space=pltpu.HBM)
    vmem = pl.BlockSpec(memory_space=pltpu.VMEM)
    if partial is None:
        body, name = attend_near_kernel, "attend_near"
        out_shape = [
            jax.ShapeDtypeStruct((rows, wide), jnp.float32),
            jax.ShapeDtypeStruct((rows, HD), jnp.float32),
        ]
    else:
        body, name = attend_far_kernel, "attend_far"
        out_shape = [jax.ShapeDtypeStruct((rows, wide), jnp.bfloat16)]
    extra = [] if partial is None else list(partial)
    return pl.pallas_call(
        functools.partial(body, parts, block),
        out_shape=out_shape,
        in_specs=[pl.BlockSpec(memory_space=pltpu.SMEM)]
        + [hbm] * len(arrays)
        + [vmem] * len(extra),
        out_specs=[vmem] * len(out_shape),
        scratch_shapes=[
            pltpu.VMEM((rows, columns), jnp.bfloat16),
            pltpu.SemaphoreType.DMA((len(places),)),
        ],
        compiler_params=pltpu.CompilerParams(vmem_limit_bytes=VMEM_BYTES),
        cost_estimate=pl.CostEstimate(
            flops=2 * rows * rows * wide,
            bytes_accessed=2 * rows * (columns + wide),
            transcendentals=rows * rows * wide // HD // 2,
        ),
        name=name,
    )(scal, *arrays, *extra)


def after(x, *earlier):
    return lax.optimization_barrier((x,) + earlier)[0]


def four_planes(tokens, w_qkv, norm_gain, q_gain, k_gain, lengths):
    t = lax.axis_index("tensor")
    rows = tokens.shape[0]
    half = rows // 2
    columns = w_qkv.shape[1] // 4
    side = t // 2
    far_end = 3 * (1 - side)
    far_mid = 2 - side

    def slab(block):
        return lax.dynamic_slice(w_qkv, (0, block * columns), (w_qkv.shape[0], columns))

    def across(x, pairs):
        return lax.ppermute(x, "tensor", pairs)

    def exchange(x, bits):
        return across(x, [(i, i ^ bits) for i in range(4)])

    def spread(x):
        return lax.all_gather(x, "fsdp", axis=0, tiled=True)

    swap = [(1, 2), (2, 1)]
    far = [(0, 2), (3, 1)]
    outward = [(1, 0), (2, 3)]

    planes = [t] + [jnp.bitwise_xor(t, m) for m in (1, 2, 3)]
    own, out1, out2, out3 = [slab(p) for p in planes]
    normed = head_norm(tokens.astype(jnp.float32), norm_gain).astype(jnp.bfloat16)
    first, second = normed[:half], normed[half:]

    in2, in3, in1 = exchange(out2, 2), exchange(out3, 3), exchange(out1, 1)
    quarter = rows // 4
    pair1 = exchange(normed[:quarter], 1)
    in1, in2, in3, pair1 = lax.optimization_barrier((in1, in2, in3, pair1))
    swap1 = across(after(first, in1), swap)
    pair2 = exchange(after(normed[quarter : quarter + half], in1), 1)
    pair3 = exchange(after(normed[quarter + half :], in1), 1)
    swap2 = across(after(second, swap1, pair2), swap)
    on1 = across(after(swap1, pair3), outward)
    far1 = across(after(first, swap2), far)
    on2 = across(swap2, outward)
    far2 = across(after(second, far1, on1), far)
    on3 = across(far1, outward)

    pieces = [spread(x) for x in (own, in1, in2, in3)]
    middle = jnp.where((t == 1) | (t == 2), 1, 0)
    scal = jnp.stack(planes + [jnp.int32(m) for m in range(4)] + [middle])

    positions = jnp.arange(4 * rows, dtype=jnp.int32)
    angle = angles(positions)
    cos = jnp.concatenate([jnp.cos(angle)] * 2, axis=1)
    sin = jnp.concatenate([-jnp.sin(angle), jnp.sin(angle)], axis=1)
    gains = jnp.stack([q_gain, k_gain])

    made, parts, places = [], [], []

    def run(call):
        listed, first_row = [], 0
        for (block, _), place in call:
            listed.append((first_row, block.shape[0], len(places)))
            first_row += block.shape[0]
            places.append(place)
        parts.append(listed)
        made.append(
            project([b for b, _ in call], [p for _, p in call], pieces, scal, cos, sin, gains)
        )

    pair_place = planes[1] * rows
    run(
        [
            ((normed, normed), t * rows),
            ((pair1, pair1), pair_place),
            ((pair2, pair2), pair_place + quarter),
            ((pair3, pair3), pair_place + quarter + half),
        ]
    )
    on4 = across(after(far2, on2, made[0]), outward)
    run([((swap1, on1), far_mid * rows), ((swap2, on2), far_mid * rows + half)])
    near_places = [place - side * rows for place in places]
    made[1] = after(made[1], on3)
    partial = attend_blocks(made, parts, near_places, lengths[0] - side * rows, side, rows)
    far1, on3, far2, on4 = [after(x, *partial) for x in (far1, on3, far2, on4)]
    run([((far1, on3), far_end * rows), ((far2, on4), far_end * rows + half)])
    return attend_blocks(made, parts, places, lengths[0], side, rows, partial)[0]


def solution(mesh):
    placed = (
        P(("groups", "fsdp", "tensor"), None),
        P(("groups", "fsdp", "tensor"), None),
        P(),
        P(),
        P(),
        P(("groups", "fsdp")),
    )
    sizes = dict(mesh.shape)
    body = four_planes if sizes["tensor"] == 4 and sizes["fsdp"] == 4 else any_mesh
    return jax.shard_map(
        body,
        mesh=mesh,
        in_specs=placed,
        out_specs=P(("groups", "fsdp"), "tensor"),
        check_vma=False,
    )
```

```python
import functools
import jax
import jax.numpy as jnp
from jax import lax
from jax.experimental import pallas as pl
from jax.experimental.pallas import tpu as pltpu
from jax.sharding import PartitionSpec as P

KV = 8
HD = 128
GQ = 4
LOG2E = 1.4426950408889634
VMEM_BYTES = 48 * 1024 * 1024


def head_norm(vec, gain):
    scale = lax.rsqrt(jnp.mean(vec * vec, axis=-1, keepdims=True) + 1e-06)
    return vec * scale * gain


def angles(positions):
    half = HD // 2
    freqs = 1000000.0 ** (-2.0 * jnp.arange(half, dtype=jnp.float32) / HD)
    return positions.astype(jnp.float32)[:, None] * freqs[None, :]


def rotate(vec, positions):
    half = vec.shape[-1] // 2
    angle = angles(positions)
    cosine = jnp.cos(angle)[:, None, None, :]
    sine = jnp.sin(angle)[:, None, None, :]
    first = vec[..., :half]
    second = vec[..., half:]
    return jnp.concatenate(
        [first * cosine - second * sine, second * cosine + first * sine], axis=-1
    )


def attend(qkv, q_gain, k_gain, length):
    rows = qkv.shape[0]
    group = qkv.shape[2] - 2
    positions = jnp.arange(rows, dtype=jnp.int32)
    query = rotate(head_norm(qkv[:, :, :group], q_gain), positions).astype(jnp.bfloat16)
    keyed = rotate(head_norm(qkv[:, :, group : group + 1], k_gain), positions)[:, :, 0].astype(
        jnp.bfloat16
    )
    value = qkv[:, :, group + 1].astype(jnp.bfloat16)
    scores = jnp.einsum(
        "ikgd,jkd->kgij", query, keyed, preferred_element_type=jnp.float32
    ) / jnp.sqrt(jnp.float32(qkv.shape[3]))
    allowed = (positions[None, :] <= positions[:, None]) & (positions[None, :] < length)
    scores = jnp.where(allowed[None, None], scores, jnp.float32(-1e30))
    top = jnp.max(scores, axis=-1, keepdims=True)
    weights = jnp.exp(scores - top)
    probs = (weights / jnp.sum(weights, axis=-1, keepdims=True)).astype(jnp.bfloat16)
    out = jnp.einsum("kgij,jkd->ikgd", probs, value, preferred_element_type=jnp.float32)
    return out.reshape(rows, -1).astype(jnp.bfloat16)


def any_mesh(tokens, w_qkv, norm_gain, q_gain, k_gain, lengths):
    tensor_count = lax.axis_size("tensor")
    moved = lax.all_to_all(w_qkv, "tensor", split_axis=1, concat_axis=0, tiled=True)
    weight_cols = lax.all_gather(moved, "fsdp", axis=0, tiled=True)
    normed = head_norm(tokens.astype(jnp.float32), norm_gain).astype(jnp.bfloat16)
    qkv = jnp.dot(
        lax.all_gather(normed, "tensor", axis=0, tiled=True),
        weight_cols,
        preferred_element_type=jnp.float32,
    )
    qkv = qkv.reshape(qkv.shape[0], KV // tensor_count, GQ + 2, HD)
    return attend(qkv, q_gain, k_gain, lengths[0])


def project_kernel(counts, sources, tile, scal, *refs):
    blocks = len(counts)
    arrays = max(source[0] for source in sources) + 1
    middle_rows, end_rows = refs[:blocks], refs[blocks : 2 * blocks]
    refs = refs[2 * blocks :]
    pieces = refs[:arrays]
    cos_ref, sin_ref, gain_ref, out = refs[arrays : arrays + 4]
    taken, held, made, row_sems, sems, out_sems = refs[arrays + 4 :]
    depth = taken.shape[1] // 16
    columns = made.shape[1]
    steps = columns // tile

    def copies(step):
        listed = []
        for index, (array, first, group, slot) in enumerate(sources):
            start = pl.multiple_of((scal[group] * 4 + scal[slot]) * depth, 16)
            low = step * tile
            listed.append(
                pltpu.make_async_copy(
                    pieces[array].at[first : first + depth, low : low + tile],
                    held.at[step % 2, pl.ds(start, depth), :],
                    sems.at[step % 2, index],
                )
            )
        return listed

    starts = [sum(counts[:n]) for n in range(blocks)]
    row_copies = [
        [
            pltpu.make_async_copy(ref, taken.at[first : first + rows, :], row_sems.at[number])
            for ref in (middle_rows[number], end_rows[number])
        ]
        for number, (first, rows) in enumerate(zip(starts, counts))
    ]
    out_copies = []
    for copy in copies(0):
        copy.start()
    for in_middle, in_end in row_copies:
        pl.when(scal[8] == 1)(in_middle.start)
        pl.when(scal[8] == 0)(in_end.start)
    for step in range(steps):
        if step + 1 < steps:
            for copy in copies(step + 1):
                copy.start()
        if step == 0:
            for in_middle, _ in row_copies:
                in_middle.wait()
        for copy in copies(step):
            copy.wait()
        total = jnp.dot(taken[...], held[step % 2], preferred_element_type=jnp.float32)
        for number, (first, rows) in enumerate(zip(starts, counts)):
            place = pl.ds(pl.multiple_of(scal[9 + number], 16), rows)
            cosine = cos_ref[place, :]
            sine = sin_ref[place, :]
            for head in range(tile // HD):
                kind = (step * (tile // HD) + head) % (GQ + 2)
                vec = total[first : first + rows, head * HD : (head + 1) * HD]
                if kind <= GQ:
                    scale = lax.rsqrt(jnp.mean(vec * vec, axis=-1, keepdims=True) + 1e-06)
                    gain = gain_ref[0:1, :] if kind < GQ else gain_ref[1:2, :]
                    vec = vec * scale * gain
                    vec = vec * cosine + pltpu.roll(vec, HD // 2, 1) * sine
                at = step * tile + head * HD
                made[first : first + rows, at : at + HD] = vec.astype(made.dtype)
        at = slice(step * tile, (step + 1) * tile)
        out_copies.append(pltpu.make_async_copy(made.at[:, at], out.at[:, at], out_sems.at[step]))
        out_copies[-1].start()
    for copy in out_copies:
        copy.wait()


def project(rows_list, places, pieces, scal, cos, sin, gains):
    depth = rows_list[0][0].shape[1] // 16
    columns = pieces[0].shape[1]
    sources = [(n, m * depth, 4 + m, n) for n in range(4) for m in range(4)]
    counts = [r.shape[0] for r, _ in rows_list]
    steps = 3
    tile = columns // steps
    count = sum(counts)
    width = rows_list[0][0].shape[1]
    scal = jnp.concatenate([scal, jnp.stack(places)]).astype(jnp.int32)
    vmem = pl.BlockSpec(memory_space=pltpu.VMEM)
    hbm = pl.BlockSpec(memory_space=pltpu.HBM)
    return pl.pallas_call(
        functools.partial(project_kernel, counts, sources, tile),
        out_shape=pltpu.HBM((count, columns), jnp.bfloat16),
        in_specs=[pl.BlockSpec(memory_space=pltpu.SMEM)]
        + [hbm] * (2 * len(counts) + len(pieces))
        + [vmem] * 3,
        out_specs=hbm,
        scratch_shapes=[
            pltpu.VMEM((count, width), jnp.bfloat16),
            pltpu.VMEM((2, width, tile), jnp.bfloat16),
            pltpu.VMEM((count, columns), jnp.bfloat16),
            pltpu.SemaphoreType.DMA((len(counts),)),
            pltpu.SemaphoreType.DMA((2, 16)),
            pltpu.SemaphoreType.DMA((steps,)),
        ],
        compiler_params=pltpu.CompilerParams(vmem_limit_bytes=VMEM_BYTES),
        cost_estimate=pl.CostEstimate(
            flops=2 * count * width * columns,
            bytes_accessed=2 * (width * columns + count * (width + columns)),
            transcendentals=0,
        ),
        name="project",
    )(scal, *[r for r, _ in rows_list], *[r for _, r in rows_list], *pieces, cos, sin, gains)


FACTOR = LOG2E / float(HD) ** 0.5
CONTRACT = (((1,), (1,)), ((), ()))


def fetch_blocks(refs, parts, places, held, sems):
    copies = []
    for ref, blocks in zip(refs, parts):
        for first, rows, number in blocks:
            place = pl.ds(pl.multiple_of(places(number), 16), rows)
            copies.append(
                pltpu.make_async_copy(
                    ref.at[first : first + rows, :], held.at[place, :], sems.at[number]
                )
            )
    for copy in copies:
        copy.start()
    for copy in copies:
        copy.wait()


def head_columns(head):
    base = head // GQ * (GQ + 2) * HD
    query = base + head % GQ * HD
    key = base + GQ * HD
    return (
        slice(query, query + HD),
        slice(key, key + HD),
        slice(key + HD, key + 2 * HD),
        slice(head * HD, (head + 1) * HD),
    )


def attend_rows(held, head, low, block, length):
    query_at, key_at, value_at, _ = head_columns(head)
    high = low + block
    row = lax.broadcasted_iota(jnp.int32, (block, block), 0)
    col = lax.broadcasted_iota(jnp.int32, (block, block), 1)
    query = held[low:high, query_at]
    last = lax.dot_general(
        query, held[low:high, key_at], CONTRACT, preferred_element_type=jnp.float32
    )
    last = jnp.where((col <= row) & (col + low < length), last, -1e30)
    top = jnp.max(last, axis=-1, keepdims=True)
    if low:
        rest = lax.dot_general(
            query, held[:low, key_at], CONTRACT, preferred_element_type=jnp.float32
        )
        keys = lax.broadcasted_iota(jnp.int32, (1, low), 1)
        rest = rest + jnp.where(keys < length, 0.0, -1e30)
        top = jnp.maximum(top, jnp.max(rest, axis=-1, keepdims=True))
    probs = jnp.exp2((last - top) * FACTOR)
    norm = jnp.sum(probs, axis=-1, keepdims=True)
    value = jnp.dot(
        probs.astype(jnp.bfloat16), held[low:high, value_at], preferred_element_type=jnp.float32
    )
    if low:
        probs = jnp.exp2((rest - top) * FACTOR)
        norm = norm + jnp.sum(probs, axis=-1, keepdims=True)
        value = value + jnp.dot(
            probs.astype(jnp.bfloat16), held[:low, value_at], preferred_element_type=jnp.float32
        )
    return top, norm, value


def attend_near_kernel(parts, block, scal, *refs):
    partial, stats, held, sems = refs[len(parts) :]
    fetch_blocks(refs, parts, lambda number: scal[2 + number], held, sems)
    heads = partial.shape[1] // HD
    for head in range(heads):
        out_at = head_columns(head)[3]
        for low in range(0, held.shape[0], block):
            top, norm, value = attend_rows(held, head, low, block, scal[0])
            partial[low : low + block, out_at] = value / norm
            stats[low : low + block, head : head + 1] = top * FACTOR + jnp.log(norm) * LOG2E


def attend_far_kernel(parts, block, scal, *refs):
    partial, stats, out, held, sems = refs[len(parts) :]
    fetch_blocks(refs, parts, lambda number: scal[2 + number], held, sems)
    heads = out.shape[1] // HD
    total = held.shape[0]
    length = scal[0]

    @pl.when(scal[1] == 0)
    def _():
        low = total - block
        for head in range(heads):
            out_at = head_columns(head)[3]
            _, norm, value = attend_rows(held, head, low, block, length)
            out[low:, out_at] = (value / norm).astype(out.dtype)
        out[:low, :] = partial[...].astype(out.dtype)

    @pl.when(scal[1] == 1)
    def _():
        for head in range(heads):
            query_at, key_at, value_at, out_at = head_columns(head)
            _, norm, value = attend_rows(held, head, 0, block, length)
            out[:block, out_at] = (value / norm).astype(out.dtype)
            scores = lax.dot_general(
                held[block:, query_at],
                held[:block, key_at],
                CONTRACT,
                preferred_element_type=jnp.float32,
            )
            keys = lax.broadcasted_iota(jnp.int32, (1, block), 1)
            scores = scores * FACTOR + jnp.where(keys < length, 0.0, -1e30)
            before = stats[:, head : head + 1]
            top = jnp.maximum(before, jnp.max(scores, axis=-1, keepdims=True))
            probs = jnp.exp2(scores - top)
            scale = jnp.exp2(before - top)
            norm = scale + jnp.sum(probs, axis=-1, keepdims=True)
            value = partial[:, out_at] * scale + jnp.dot(
                probs.astype(jnp.bfloat16),
                held[:block, value_at],
                preferred_element_type=jnp.float32,
            )
            out[block:, out_at] = (value / norm).astype(out.dtype)


def attend_blocks(arrays, parts, places, length, side, block, partial=None):
    rows = sum(a.shape[0] for a in arrays)
    columns = arrays[0].shape[1]
    wide = columns // (GQ + 2) * GQ
    scal = jnp.stack([length, side] + list(places)).astype(jnp.int32)
    hbm = pl.BlockSpec(memory_space=pltpu.HBM)
    vmem = pl.BlockSpec(memory_space=pltpu.VMEM)
    if partial is None:
        body, name = attend_near_kernel, "attend_near"
        out_shape = [
            jax.ShapeDtypeStruct((rows, wide), jnp.float32),
            jax.ShapeDtypeStruct((rows, HD), jnp.float32),
        ]
    else:
        body, name = attend_far_kernel, "attend_far"
        out_shape = [jax.ShapeDtypeStruct((rows, wide), jnp.bfloat16)]
    extra = [] if partial is None else list(partial)
    return pl.pallas_call(
        functools.partial(body, parts, block),
        out_shape=out_shape,
        in_specs=[pl.BlockSpec(memory_space=pltpu.SMEM)]
        + [hbm] * len(arrays)
        + [vmem] * len(extra),
        out_specs=[vmem] * len(out_shape),
        scratch_shapes=[
            pltpu.VMEM((rows, columns), jnp.bfloat16),
            pltpu.SemaphoreType.DMA((len(places),)),
        ],
        compiler_params=pltpu.CompilerParams(vmem_limit_bytes=VMEM_BYTES),
        cost_estimate=pl.CostEstimate(
            flops=2 * rows * rows * wide,
            bytes_accessed=2 * rows * (columns + wide),
            transcendentals=rows * rows * wide // HD // 2,
        ),
        name=name,
    )(scal, *arrays, *extra)


def after(x, *earlier):
    return lax.optimization_barrier((x,) + earlier)[0]


def four_planes(tokens, w_qkv, norm_gain, q_gain, k_gain, lengths):
    t = lax.axis_index("tensor")
    rows = tokens.shape[0]
    half = rows // 2
    columns = w_qkv.shape[1] // 4
    side = t // 2
    far_end = 3 * (1 - side)
    far_mid = 2 - side

    def slab(block):
        return lax.dynamic_slice(w_qkv, (0, block * columns), (w_qkv.shape[0], columns))

    def across(x, pairs):
        return lax.ppermute(x, "tensor", pairs)

    def exchange(x, bits):
        return across(x, [(i, i ^ bits) for i in range(4)])

    def spread(x):
        return lax.all_gather(x, "fsdp", axis=0, tiled=True)

    swap = [(1, 2), (2, 1)]
    far = [(0, 2), (3, 1)]
    outward = [(1, 0), (2, 3)]

    planes = [t] + [jnp.bitwise_xor(t, m) for m in (1, 2, 3)]
    own, out1, out2, out3 = [slab(p) for p in planes]
    normed = head_norm(tokens.astype(jnp.float32), norm_gain).astype(jnp.bfloat16)
    first, second = normed[:half], normed[half:]

    in2, in3, in1 = exchange(out2, 2), exchange(out3, 3), exchange(out1, 1)
    quarter = rows // 4
    pair1 = exchange(normed[:quarter], 1)
    second_pair, third_pair = normed[quarter : quarter + half], normed[quarter + half :]
    in1, in2, in3, pair1, first, second, second_pair, third_pair = lax.optimization_barrier(
        (in1, in2, in3, pair1, first, second, second_pair, third_pair)
    )
    swap1 = across(first, swap)
    pair2 = exchange(second_pair, 1)
    swap2 = across(after(second, swap1, pair2), swap)
    pair3 = exchange(after(third_pair, pair2), 1)
    on1 = across(swap1, outward)
    far1 = across(after(first, swap2, pair3), far)
    on2 = across(swap2, outward)
    far2 = across(after(second, far1, on1), far)
    on3 = across(far1, outward)

    pieces = [spread(x) for x in (own, in1, in2, in3)]
    middle = jnp.where((t == 1) | (t == 2), 1, 0)
    scal = jnp.stack(planes + [jnp.int32(m) for m in range(4)] + [middle])

    positions = jnp.arange(4 * rows, dtype=jnp.int32)
    angle = angles(positions)
    cos = jnp.concatenate([jnp.cos(angle)] * 2, axis=1)
    sin = jnp.concatenate([-jnp.sin(angle), jnp.sin(angle)], axis=1)
    gains = jnp.stack([q_gain, k_gain])

    made, parts, places = [], [], []

    def run(call):
        listed, first_row = [], 0
        for (block, _), place in call:
            listed.append((first_row, block.shape[0], len(places)))
            first_row += block.shape[0]
            places.append(place)
        parts.append(listed)
        made.append(
            project([b for b, _ in call], [p for _, p in call], pieces, scal, cos, sin, gains)
        )

    pair_place = planes[1] * rows
    run(
        [
            ((normed, normed), t * rows),
            ((pair1, pair1), pair_place),
            ((pair2, pair2), pair_place + quarter),
            ((pair3, pair3), pair_place + quarter + half),
        ]
    )
    on4 = across(after(far2, on2, made[0]), outward)
    run([((swap1, on1), far_mid * rows), ((swap2, on2), far_mid * rows + half)])
    near_places = [place - side * rows for place in places]
    made[1] = after(made[1], on3)
    partial = attend_blocks(made, parts, near_places, lengths[0] - side * rows, side, rows)
    far1, on3, far2, on4 = [after(x, *partial) for x in (far1, on3, far2, on4)]
    run([((far1, on3), far_end * rows), ((far2, on4), far_end * rows + half)])
    return attend_blocks(made, parts, places, lengths[0], side, rows, partial)[0]


def solution(mesh):
    placed = (
        P(("groups", "fsdp", "tensor"), None),
        P(("groups", "fsdp", "tensor"), None),
        P(),
        P(),
        P(),
        P(("groups", "fsdp")),
    )
    sizes = dict(mesh.shape)
    body = four_planes if sizes["tensor"] == 4 and sizes["fsdp"] == 4 else any_mesh
    return jax.shard_map(
        body,
        mesh=mesh,
        in_specs=placed,
        out_specs=P(("groups", "fsdp"), "tensor"),
        check_vma=False,
    )
```

```python
import functools
import jax
import jax.numpy as jnp
from jax import lax
from jax.experimental import pallas as pl
from jax.experimental.pallas import tpu as pltpu
from jax.sharding import PartitionSpec as P

KV = 8
HD = 128
GQ = 4
LOG2E = 1.4426950408889634
VMEM_BYTES = 48 * 1024 * 1024


def head_norm(vec, gain):
    scale = lax.rsqrt(jnp.mean(vec * vec, axis=-1, keepdims=True) + 1e-06)
    return vec * scale * gain


def angles(positions):
    half = HD // 2
    freqs = 1000000.0 ** (-2.0 * jnp.arange(half, dtype=jnp.float32) / HD)
    return positions.astype(jnp.float32)[:, None] * freqs[None, :]


def rotate(vec, positions):
    half = vec.shape[-1] // 2
    angle = angles(positions)
    cosine = jnp.cos(angle)[:, None, None, :]
    sine = jnp.sin(angle)[:, None, None, :]
    first = vec[..., :half]
    second = vec[..., half:]
    return jnp.concatenate(
        [first * cosine - second * sine, second * cosine + first * sine], axis=-1
    )


def attend(qkv, q_gain, k_gain, length):
    rows = qkv.shape[0]
    group = qkv.shape[2] - 2
    positions = jnp.arange(rows, dtype=jnp.int32)
    query = rotate(head_norm(qkv[:, :, :group], q_gain), positions).astype(jnp.bfloat16)
    keyed = rotate(head_norm(qkv[:, :, group : group + 1], k_gain), positions)[:, :, 0].astype(
        jnp.bfloat16
    )
    value = qkv[:, :, group + 1].astype(jnp.bfloat16)
    scores = jnp.einsum(
        "ikgd,jkd->kgij", query, keyed, preferred_element_type=jnp.float32
    ) / jnp.sqrt(jnp.float32(qkv.shape[3]))
    allowed = (positions[None, :] <= positions[:, None]) & (positions[None, :] < length)
    scores = jnp.where(allowed[None, None], scores, jnp.float32(-1e30))
    top = jnp.max(scores, axis=-1, keepdims=True)
    weights = jnp.exp(scores - top)
    probs = (weights / jnp.sum(weights, axis=-1, keepdims=True)).astype(jnp.bfloat16)
    out = jnp.einsum("kgij,jkd->ikgd", probs, value, preferred_element_type=jnp.float32)
    return out.reshape(rows, -1).astype(jnp.bfloat16)


def any_mesh(tokens, w_qkv, norm_gain, q_gain, k_gain, lengths):
    tensor_count = lax.axis_size("tensor")
    moved = lax.all_to_all(w_qkv, "tensor", split_axis=1, concat_axis=0, tiled=True)
    weight_cols = lax.all_gather(moved, "fsdp", axis=0, tiled=True)
    normed = head_norm(tokens.astype(jnp.float32), norm_gain).astype(jnp.bfloat16)
    qkv = jnp.dot(
        lax.all_gather(normed, "tensor", axis=0, tiled=True),
        weight_cols,
        preferred_element_type=jnp.float32,
    )
    qkv = qkv.reshape(qkv.shape[0], KV // tensor_count, GQ + 2, HD)
    return attend(qkv, q_gain, k_gain, lengths[0])


def project_kernel(counts, sources, tile, scal, *refs):
    blocks = len(counts)
    arrays = max(source[0] for source in sources) + 1
    middle_rows, end_rows = refs[:blocks], refs[blocks : 2 * blocks]
    refs = refs[2 * blocks :]
    pieces = refs[:arrays]
    cos_ref, sin_ref, gain_ref, out = refs[arrays : arrays + 4]
    taken, held, made, row_sems, sems, out_sems = refs[arrays + 4 :]
    depth = taken.shape[1] // 16
    columns = made.shape[1]
    steps = columns // tile

    def copies(step):
        listed = []
        for index, (array, first, group, slot) in enumerate(sources):
            start = pl.multiple_of((scal[group] * 4 + scal[slot]) * depth, 16)
            low = step * tile
            listed.append(
                pltpu.make_async_copy(
                    pieces[array].at[first : first + depth, low : low + tile],
                    held.at[step % 2, pl.ds(start, depth), :],
                    sems.at[step % 2, index],
                )
            )
        return listed

    starts = [sum(counts[:n]) for n in range(blocks)]
    row_copies = [
        [
            pltpu.make_async_copy(ref, taken.at[first : first + rows, :], row_sems.at[number])
            for ref in (middle_rows[number], end_rows[number])
        ]
        for number, (first, rows) in enumerate(zip(starts, counts))
    ]
    out_copies = []
    for copy in copies(0):
        copy.start()
    for in_middle, in_end in row_copies:
        pl.when(scal[8] == 1)(in_middle.start)
        pl.when(scal[8] == 0)(in_end.start)
    for step in range(steps):
        if step + 1 < steps:
            for copy in copies(step + 1):
                copy.start()
        if step == 0:
            for in_middle, _ in row_copies:
                in_middle.wait()
        for copy in copies(step):
            copy.wait()
        total = jnp.dot(taken[...], held[step % 2], preferred_element_type=jnp.float32)
        for number, (first, rows) in enumerate(zip(starts, counts)):
            place = pl.ds(pl.multiple_of(scal[9 + number], 16), rows)
            cosine = cos_ref[place, :]
            sine = sin_ref[place, :]
            for head in range(tile // HD):
                kind = (step * (tile // HD) + head) % (GQ + 2)
                vec = total[first : first + rows, head * HD : (head + 1) * HD]
                if kind <= GQ:
                    scale = lax.rsqrt(jnp.mean(vec * vec, axis=-1, keepdims=True) + 1e-06)
                    gain = gain_ref[0:1, :] if kind < GQ else gain_ref[1:2, :]
                    vec = vec * scale * gain
                    vec = vec * cosine + pltpu.roll(vec, HD // 2, 1) * sine
                at = step * tile + head * HD
                made[first : first + rows, at : at + HD] = vec.astype(made.dtype)
        at = slice(step * tile, (step + 1) * tile)
        out_copies.append(pltpu.make_async_copy(made.at[:, at], out.at[:, at], out_sems.at[step]))
        out_copies[-1].start()
    for copy in out_copies:
        copy.wait()


def project(rows_list, places, pieces, scal, cos, sin, gains, vmem_bytes):
    depth = rows_list[0][0].shape[1] // 16
    columns = pieces[0].shape[1]
    sources = [(n, m * depth, 4 + m, n) for n in range(4) for m in range(4)]
    counts = [r.shape[0] for r, _ in rows_list]
    steps = 3
    tile = columns // steps
    count = sum(counts)
    width = rows_list[0][0].shape[1]
    scal = jnp.concatenate([scal, jnp.stack(places)]).astype(jnp.int32)
    vmem = pl.BlockSpec(memory_space=pltpu.VMEM)
    hbm = pl.BlockSpec(memory_space=pltpu.HBM)
    return pl.pallas_call(
        functools.partial(project_kernel, counts, sources, tile),
        out_shape=pltpu.HBM((count, columns), jnp.bfloat16),
        in_specs=[pl.BlockSpec(memory_space=pltpu.SMEM)]
        + [hbm] * (2 * len(counts) + len(pieces))
        + [vmem] * 3,
        out_specs=hbm,
        scratch_shapes=[
            pltpu.VMEM((count, width), jnp.bfloat16),
            pltpu.VMEM((2, width, tile), jnp.bfloat16),
            pltpu.VMEM((count, columns), jnp.bfloat16),
            pltpu.SemaphoreType.DMA((len(counts),)),
            pltpu.SemaphoreType.DMA((2, 16)),
            pltpu.SemaphoreType.DMA((steps,)),
        ],
        compiler_params=pltpu.CompilerParams(vmem_limit_bytes=vmem_bytes),
        cost_estimate=pl.CostEstimate(
            flops=2 * count * width * columns,
            bytes_accessed=2 * (width * columns + count * (width + columns)),
            transcendentals=0,
        ),
        name="project",
    )(scal, *[r for r, _ in rows_list], *[r for _, r in rows_list], *pieces, cos, sin, gains)


FACTOR = LOG2E / float(HD) ** 0.5
CONTRACT = (((1,), (1,)), ((), ()))


def fetch_blocks(refs, parts, places, held, sems):
    copies = []
    for ref, blocks in zip(refs, parts):
        for first, rows, number in blocks:
            place = pl.ds(pl.multiple_of(places(number), 16), rows)
            copies.append(
                pltpu.make_async_copy(
                    ref.at[first : first + rows, :], held.at[place, :], sems.at[number]
                )
            )
    for copy in copies:
        copy.start()
    for copy in copies:
        copy.wait()


def head_columns(head):
    base = head // GQ * (GQ + 2) * HD
    query = base + head % GQ * HD
    key = base + GQ * HD
    return (
        slice(query, query + HD),
        slice(key, key + HD),
        slice(key + HD, key + 2 * HD),
        slice(head * HD, (head + 1) * HD),
    )


def attend_rows(held, head, low, block, length):
    query_at, key_at, value_at, _ = head_columns(head)
    high = low + block
    row = lax.broadcasted_iota(jnp.int32, (block, block), 0)
    col = lax.broadcasted_iota(jnp.int32, (block, block), 1)
    query = held[low:high, query_at]
    last = lax.dot_general(
        query, held[low:high, key_at], CONTRACT, preferred_element_type=jnp.float32
    )
    last = jnp.where((col <= row) & (col + low < length), last, -1e30)
    top = jnp.max(last, axis=-1, keepdims=True)
    if low:
        rest = lax.dot_general(
            query, held[:low, key_at], CONTRACT, preferred_element_type=jnp.float32
        )
        keys = lax.broadcasted_iota(jnp.int32, (1, low), 1)
        rest = rest + jnp.where(keys < length, 0.0, -1e30)
        top = jnp.maximum(top, jnp.max(rest, axis=-1, keepdims=True))
    probs = jnp.exp2((last - top) * FACTOR)
    norm = jnp.sum(probs, axis=-1, keepdims=True)
    value = jnp.dot(
        probs.astype(jnp.bfloat16), held[low:high, value_at], preferred_element_type=jnp.float32
    )
    if low:
        probs = jnp.exp2((rest - top) * FACTOR)
        norm = norm + jnp.sum(probs, axis=-1, keepdims=True)
        value = value + jnp.dot(
            probs.astype(jnp.bfloat16), held[:low, value_at], preferred_element_type=jnp.float32
        )
    return top, norm, value


def attend_near_kernel(parts, block, scal, *refs):
    partial, stats, held, sems = refs[len(parts) :]
    fetch_blocks(refs, parts, lambda number: scal[2 + number], held, sems)
    heads = partial.shape[1] // HD
    for head in range(heads):
        out_at = head_columns(head)[3]
        for low in range(0, held.shape[0], block):
            top, norm, value = attend_rows(held, head, low, block, scal[0])
            partial[low : low + block, out_at] = value / norm
            stats[low : low + block, head : head + 1] = top * FACTOR + jnp.log(norm) * LOG2E


def attend_far_kernel(parts, block, scal, *refs):
    partial, stats, out, held, sems = refs[len(parts) :]
    fetch_blocks(refs, parts, lambda number: scal[2 + number], held, sems)
    heads = out.shape[1] // HD
    total = held.shape[0]
    length = scal[0]

    @pl.when(scal[1] == 0)
    def _():
        low = total - block
        for head in range(heads):
            out_at = head_columns(head)[3]
            _, norm, value = attend_rows(held, head, low, block, length)
            out[low:, out_at] = (value / norm).astype(out.dtype)
        out[:low, :] = partial[...].astype(out.dtype)

    @pl.when(scal[1] == 1)
    def _():
        for head in range(heads):
            query_at, key_at, value_at, out_at = head_columns(head)
            _, norm, value = attend_rows(held, head, 0, block, length)
            out[:block, out_at] = (value / norm).astype(out.dtype)
            scores = lax.dot_general(
                held[block:, query_at],
                held[:block, key_at],
                CONTRACT,
                preferred_element_type=jnp.float32,
            )
            keys = lax.broadcasted_iota(jnp.int32, (1, block), 1)
            scores = scores * FACTOR + jnp.where(keys < length, 0.0, -1e30)
            before = stats[:, head : head + 1]
            top = jnp.maximum(before, jnp.max(scores, axis=-1, keepdims=True))
            probs = jnp.exp2(scores - top)
            scale = jnp.exp2(before - top)
            norm = scale + jnp.sum(probs, axis=-1, keepdims=True)
            value = partial[:, out_at] * scale + jnp.dot(
                probs.astype(jnp.bfloat16),
                held[:block, value_at],
                preferred_element_type=jnp.float32,
            )
            out[block:, out_at] = (value / norm).astype(out.dtype)


def attend_blocks(arrays, parts, places, length, side, block, partial=None):
    rows = sum(a.shape[0] for a in arrays)
    columns = arrays[0].shape[1]
    wide = columns // (GQ + 2) * GQ
    scal = jnp.stack([length, side] + list(places)).astype(jnp.int32)
    hbm = pl.BlockSpec(memory_space=pltpu.HBM)
    vmem = pl.BlockSpec(memory_space=pltpu.VMEM)
    if partial is None:
        body, name = attend_near_kernel, "attend_near"
        out_shape = [
            jax.ShapeDtypeStruct((rows, wide), jnp.float32),
            jax.ShapeDtypeStruct((rows, HD), jnp.float32),
        ]
    else:
        body, name = attend_far_kernel, "attend_far"
        out_shape = [jax.ShapeDtypeStruct((rows, wide), jnp.bfloat16)]
    extra = [] if partial is None else list(partial)
    return pl.pallas_call(
        functools.partial(body, parts, block),
        out_shape=out_shape,
        in_specs=[pl.BlockSpec(memory_space=pltpu.SMEM)]
        + [hbm] * len(arrays)
        + [vmem] * len(extra),
        out_specs=[vmem] * len(out_shape),
        scratch_shapes=[
            pltpu.VMEM((rows, columns), jnp.bfloat16),
            pltpu.SemaphoreType.DMA((len(places),)),
        ],
        compiler_params=pltpu.CompilerParams(vmem_limit_bytes=VMEM_BYTES // 2),
        cost_estimate=pl.CostEstimate(
            flops=2 * rows * rows * wide,
            bytes_accessed=2 * rows * (columns + wide),
            transcendentals=rows * rows * wide // HD // 2,
        ),
        name=name,
    )(scal, *arrays, *extra)


def after(x, *earlier):
    return lax.optimization_barrier((x,) + earlier)[0]


def four_planes(tokens, w_qkv, norm_gain, q_gain, k_gain, lengths):
    t = lax.axis_index("tensor")
    rows = tokens.shape[0]
    half = rows // 2
    columns = w_qkv.shape[1] // 4
    side = t // 2
    far_end = 3 * (1 - side)
    far_mid = 2 - side

    def slab(block):
        return lax.dynamic_slice(w_qkv, (0, block * columns), (w_qkv.shape[0], columns))

    def across(x, pairs):
        return lax.ppermute(x, "tensor", pairs)

    def exchange(x, bits):
        return across(x, [(i, i ^ bits) for i in range(4)])

    def spread(x):
        return lax.all_gather(x, "fsdp", axis=0, tiled=True)

    swap = [(1, 2), (2, 1)]
    far = [(0, 2), (3, 1)]
    outward = [(1, 0), (2, 3)]

    planes = [t] + [jnp.bitwise_xor(t, m) for m in (1, 2, 3)]
    own, out1, out2, out3 = [slab(p) for p in planes]
    normed = head_norm(tokens.astype(jnp.float32), norm_gain).astype(jnp.bfloat16)
    first, second = normed[:half], normed[half:]

    in2, in3, in1 = exchange(out2, 2), exchange(out3, 3), exchange(out1, 1)
    quarter = rows // 4
    pair1 = exchange(normed[:quarter], 1)
    second_pair, third_pair = normed[quarter : quarter + half], normed[quarter + half :]
    in1, in2, in3, pair1, first, second, second_pair, third_pair = lax.optimization_barrier(
        (in1, in2, in3, pair1, first, second, second_pair, third_pair)
    )
    swap1 = across(first, swap)
    pair2 = exchange(second_pair, 1)
    swap2 = across(after(second, swap1, pair2), swap)
    pair3 = exchange(after(third_pair, pair2), 1)
    on1 = across(swap1, outward)
    far1 = across(after(first, swap2, pair3), far)
    on2 = across(swap2, outward)
    far2 = across(after(second, far1, on1), far)
    on3 = across(far1, outward)

    pieces = [spread(x) for x in (own, in1, in2, in3)]
    middle = jnp.where((t == 1) | (t == 2), 1, 0)
    scal = jnp.stack(planes + [jnp.int32(m) for m in range(4)] + [middle])

    positions = jnp.arange(4 * rows, dtype=jnp.int32)
    angle = angles(positions)
    cos = jnp.concatenate([jnp.cos(angle)] * 2, axis=1)
    sin = jnp.concatenate([-jnp.sin(angle), jnp.sin(angle)], axis=1)
    gains = jnp.stack([q_gain, k_gain])

    made, parts, places = [], [], []

    tables = (cos, sin, gains)

    def run(call, vmem_bytes=VMEM_BYTES):
        listed, first_row = [], 0
        for (block, _), place in call:
            listed.append((first_row, block.shape[0], len(places)))
            first_row += block.shape[0]
            places.append(place)
        parts.append(listed)
        made.append(
            project([b for b, _ in call], [p for _, p in call], pieces, scal, *tables, vmem_bytes)
        )

    pair_place = planes[1] * rows
    run(
        [
            ((normed, normed), t * rows),
            ((pair1, pair1), pair_place),
            ((pair2, pair2), pair_place + quarter),
            ((pair3, pair3), pair_place + quarter + half),
        ]
    )
    on4 = across(after(far2, on2, made[0]), outward)
    run([((swap1, on1), far_mid * rows), ((swap2, on2), far_mid * rows + half)])
    near_places = [place - side * rows for place in places]
    made[1] = after(made[1], on3)
    partial = attend_blocks(made, parts, near_places, lengths[0] - side * rows, side, rows)
    far1, on3, far2, on4 = [after(x, *partial) for x in (far1, on3, far2, on4)]
    run([((far1, on3), far_end * rows), ((far2, on4), far_end * rows + half)], VMEM_BYTES // 2)
    return attend_blocks(made, parts, places, lengths[0], side, rows, partial)[0]


def solution(mesh):
    placed = (
        P(("groups", "fsdp", "tensor"), None),
        P(("groups", "fsdp", "tensor"), None),
        P(),
        P(),
        P(),
        P(("groups", "fsdp")),
    )
    sizes = dict(mesh.shape)
    body = four_planes if sizes["tensor"] == 4 and sizes["fsdp"] == 4 else any_mesh
    return jax.shard_map(
        body,
        mesh=mesh,
        in_specs=placed,
        out_specs=P(("groups", "fsdp"), "tensor"),
        check_vma=False,
    )
```

```python
import functools
import jax
import jax.numpy as jnp
from jax import lax
from jax.experimental import pallas as pl
from jax.experimental.pallas import tpu as pltpu
from jax.sharding import PartitionSpec as P

KV = 8
HD = 128
GQ = 4
LOG2E = 1.4426950408889634
VMEM_BYTES = 48 * 1024 * 1024
SMALL_BYTES = 20 * 1024 * 1024


def head_norm(vec, gain):
    scale = lax.rsqrt(jnp.mean(vec * vec, axis=-1, keepdims=True) + 1e-06)
    return vec * scale * gain


def angles(positions):
    half = HD // 2
    freqs = 1000000.0 ** (-2.0 * jnp.arange(half, dtype=jnp.float32) / HD)
    return positions.astype(jnp.float32)[:, None] * freqs[None, :]


def rotate(vec, positions):
    half = vec.shape[-1] // 2
    angle = angles(positions)
    cosine = jnp.cos(angle)[:, None, None, :]
    sine = jnp.sin(angle)[:, None, None, :]
    first = vec[..., :half]
    second = vec[..., half:]
    return jnp.concatenate(
        [first * cosine - second * sine, second * cosine + first * sine], axis=-1
    )


def attend(qkv, q_gain, k_gain, length):
    rows = qkv.shape[0]
    group = qkv.shape[2] - 2
    positions = jnp.arange(rows, dtype=jnp.int32)
    query = rotate(head_norm(qkv[:, :, :group], q_gain), positions).astype(jnp.bfloat16)
    keyed = rotate(head_norm(qkv[:, :, group : group + 1], k_gain), positions)[:, :, 0].astype(
        jnp.bfloat16
    )
    value = qkv[:, :, group + 1].astype(jnp.bfloat16)
    scores = jnp.einsum(
        "ikgd,jkd->kgij", query, keyed, preferred_element_type=jnp.float32
    ) / jnp.sqrt(jnp.float32(qkv.shape[3]))
    allowed = (positions[None, :] <= positions[:, None]) & (positions[None, :] < length)
    scores = jnp.where(allowed[None, None], scores, jnp.float32(-1e30))
    top = jnp.max(scores, axis=-1, keepdims=True)
    weights = jnp.exp(scores - top)
    probs = (weights / jnp.sum(weights, axis=-1, keepdims=True)).astype(jnp.bfloat16)
    out = jnp.einsum("kgij,jkd->ikgd", probs, value, preferred_element_type=jnp.float32)
    return out.reshape(rows, -1).astype(jnp.bfloat16)


def any_mesh(tokens, w_qkv, norm_gain, q_gain, k_gain, lengths):
    tensor_count = lax.axis_size("tensor")
    moved = lax.all_to_all(w_qkv, "tensor", split_axis=1, concat_axis=0, tiled=True)
    weight_cols = lax.all_gather(moved, "fsdp", axis=0, tiled=True)
    normed = head_norm(tokens.astype(jnp.float32), norm_gain).astype(jnp.bfloat16)
    qkv = jnp.dot(
        lax.all_gather(normed, "tensor", axis=0, tiled=True),
        weight_cols,
        preferred_element_type=jnp.float32,
    )
    qkv = qkv.reshape(qkv.shape[0], KV // tensor_count, GQ + 2, HD)
    return attend(qkv, q_gain, k_gain, lengths[0])


def project_kernel(counts, sources, tile, scal, *refs):
    blocks = len(counts)
    arrays = max(source[0] for source in sources) + 1
    middle_rows, end_rows = refs[:blocks], refs[blocks : 2 * blocks]
    refs = refs[2 * blocks :]
    pieces = refs[:arrays]
    cos_ref, sin_ref, gain_ref, out = refs[arrays : arrays + 4]
    taken, held, made, row_sems, sems, out_sems = refs[arrays + 4 :]
    depth = taken.shape[1] // 16
    columns = made.shape[1]
    steps = columns // tile

    def copies(step):
        listed = []
        for index, (array, first, group, slot) in enumerate(sources):
            start = pl.multiple_of((scal[group] * 4 + scal[slot]) * depth, 16)
            low = step * tile
            listed.append(
                pltpu.make_async_copy(
                    pieces[array].at[first : first + depth, low : low + tile],
                    held.at[step % 2, pl.ds(start, depth), :],
                    sems.at[step % 2, index],
                )
            )
        return listed

    starts = [sum(counts[:n]) for n in range(blocks)]
    row_copies = [
        [
            pltpu.make_async_copy(ref, taken.at[first : first + rows, :], row_sems.at[number])
            for ref in (middle_rows[number], end_rows[number])
        ]
        for number, (first, rows) in enumerate(zip(starts, counts))
    ]
    out_copies = []
    for copy in copies(0):
        copy.start()
    for in_middle, in_end in row_copies:
        pl.when(scal[8] == 1)(in_middle.start)
        pl.when(scal[8] == 0)(in_end.start)
    for step in range(steps):
        if step + 1 < steps:
            for copy in copies(step + 1):
                copy.start()
        if step == 0:
            for in_middle, _ in row_copies:
                in_middle.wait()
        for copy in copies(step):
            copy.wait()
        total = jnp.dot(taken[...], held[step % 2], preferred_element_type=jnp.float32)
        for number, (first, rows) in enumerate(zip(starts, counts)):
            place = pl.ds(pl.multiple_of(scal[9 + number], 16), rows)
            cosine = cos_ref[place, :]
            sine = sin_ref[place, :]
            for head in range(tile // HD):
                kind = (step * (tile // HD) + head) % (GQ + 2)
                vec = total[first : first + rows, head * HD : (head + 1) * HD]
                if kind <= GQ:
                    scale = lax.rsqrt(jnp.mean(vec * vec, axis=-1, keepdims=True) + 1e-06)
                    gain = gain_ref[0:1, :] if kind < GQ else gain_ref[1:2, :]
                    vec = vec * scale * gain
                    vec = vec * cosine + pltpu.roll(vec, HD // 2, 1) * sine
                at = step * tile + head * HD
                made[first : first + rows, at : at + HD] = vec.astype(made.dtype)
        at = slice(step * tile, (step + 1) * tile)
        out_copies.append(pltpu.make_async_copy(made.at[:, at], out.at[:, at], out_sems.at[step]))
        out_copies[-1].start()
    for copy in out_copies:
        copy.wait()


def project(rows_list, places, pieces, scal, cos, sin, gains, vmem_bytes, space):
    depth = rows_list[0][0].shape[1] // 16
    columns = pieces[0].shape[1]
    sources = [(n, m * depth, 4 + m, n) for n in range(4) for m in range(4)]
    counts = [r.shape[0] for r, _ in rows_list]
    steps = 3
    tile = columns // steps
    count = sum(counts)
    width = rows_list[0][0].shape[1]
    scal = jnp.concatenate([scal, jnp.stack(places)]).astype(jnp.int32)
    vmem = pl.BlockSpec(memory_space=pltpu.VMEM)
    hbm = pl.BlockSpec(memory_space=pltpu.HBM)
    return pl.pallas_call(
        functools.partial(project_kernel, counts, sources, tile),
        out_shape=space((count, columns), jnp.bfloat16),
        in_specs=[pl.BlockSpec(memory_space=pltpu.SMEM)]
        + [hbm] * (2 * len(counts) + len(pieces))
        + [vmem] * 3,
        out_specs=pl.BlockSpec(memory_space=space),
        scratch_shapes=[
            pltpu.VMEM((count, width), jnp.bfloat16),
            pltpu.VMEM((2, width, tile), jnp.bfloat16),
            pltpu.VMEM((count, columns), jnp.bfloat16),
            pltpu.SemaphoreType.DMA((len(counts),)),
            pltpu.SemaphoreType.DMA((2, 16)),
            pltpu.SemaphoreType.DMA((steps,)),
        ],
        compiler_params=pltpu.CompilerParams(vmem_limit_bytes=vmem_bytes),
        cost_estimate=pl.CostEstimate(
            flops=2 * count * width * columns,
            bytes_accessed=2 * (width * columns + count * (width + columns)),
            transcendentals=0,
        ),
        name="project",
    )(scal, *[r for r, _ in rows_list], *[r for _, r in rows_list], *pieces, cos, sin, gains)


FACTOR = LOG2E / float(HD) ** 0.5
CONTRACT = (((1,), (1,)), ((), ()))


def fetch_blocks(refs, parts, places, held, sems):
    copies = []
    for ref, blocks in zip(refs, parts):
        for first, rows, number in blocks:
            place = pl.ds(pl.multiple_of(places(number), 16), rows)
            copies.append(
                pltpu.make_async_copy(
                    ref.at[first : first + rows, :], held.at[place, :], sems.at[number]
                )
            )
    for copy in copies:
        copy.start()
    for copy in copies:
        copy.wait()


def head_columns(head):
    base = head // GQ * (GQ + 2) * HD
    query = base + head % GQ * HD
    key = base + GQ * HD
    return (
        slice(query, query + HD),
        slice(key, key + HD),
        slice(key + HD, key + 2 * HD),
        slice(head * HD, (head + 1) * HD),
    )


def attend_rows(held, head, low, block, length):
    query_at, key_at, value_at, _ = head_columns(head)
    high = low + block
    row = lax.broadcasted_iota(jnp.int32, (block, block), 0)
    col = lax.broadcasted_iota(jnp.int32, (block, block), 1)
    query = held[low:high, query_at]
    last = lax.dot_general(
        query, held[low:high, key_at], CONTRACT, preferred_element_type=jnp.float32
    )
    last = jnp.where((col <= row) & (col + low < length), last, -1e30)
    top = jnp.max(last, axis=-1, keepdims=True)
    if low:
        rest = lax.dot_general(
            query, held[:low, key_at], CONTRACT, preferred_element_type=jnp.float32
        )
        keys = lax.broadcasted_iota(jnp.int32, (1, low), 1)
        rest = rest + jnp.where(keys < length, 0.0, -1e30)
        top = jnp.maximum(top, jnp.max(rest, axis=-1, keepdims=True))
    probs = jnp.exp2((last - top) * FACTOR)
    norm = jnp.sum(probs, axis=-1, keepdims=True)
    value = jnp.dot(
        probs.astype(jnp.bfloat16), held[low:high, value_at], preferred_element_type=jnp.float32
    )
    if low:
        probs = jnp.exp2((rest - top) * FACTOR)
        norm = norm + jnp.sum(probs, axis=-1, keepdims=True)
        value = value + jnp.dot(
            probs.astype(jnp.bfloat16), held[:low, value_at], preferred_element_type=jnp.float32
        )
    return top, norm, value


def attend_near_kernel(parts, block, scal, *refs):
    partial, stats, held, sems = refs[len(parts) :]
    fetch_blocks(refs, parts, lambda number: scal[2 + number], held, sems)
    heads = partial.shape[1] // HD
    for head in range(heads):
        out_at = head_columns(head)[3]
        for low in range(0, held.shape[0], block):
            top, norm, value = attend_rows(held, head, low, block, scal[0])
            partial[low : low + block, out_at] = value / norm
            stats[low : low + block, head : head + 1] = top * FACTOR + jnp.log(norm) * LOG2E


def attend_far_kernel(parts, block, scal, *refs):
    partial, stats, out, held, sems = refs[len(parts) :]
    fetch_blocks(refs, parts, lambda number: scal[2 + number], held, sems)
    heads = out.shape[1] // HD
    total = held.shape[0]
    length = scal[0]

    @pl.when(scal[1] == 0)
    def _():
        low = total - block
        for head in range(heads):
            out_at = head_columns(head)[3]
            _, norm, value = attend_rows(held, head, low, block, length)
            out[low:, out_at] = (value / norm).astype(out.dtype)
        out[:low, :] = partial[...].astype(out.dtype)

    @pl.when(scal[1] == 1)
    def _():
        for head in range(heads):
            query_at, key_at, value_at, out_at = head_columns(head)
            _, norm, value = attend_rows(held, head, 0, block, length)
            out[:block, out_at] = (value / norm).astype(out.dtype)
            scores = lax.dot_general(
                held[block:, query_at],
                held[:block, key_at],
                CONTRACT,
                preferred_element_type=jnp.float32,
            )
            keys = lax.broadcasted_iota(jnp.int32, (1, block), 1)
            scores = scores * FACTOR + jnp.where(keys < length, 0.0, -1e30)
            before = stats[:, head : head + 1]
            top = jnp.maximum(before, jnp.max(scores, axis=-1, keepdims=True))
            probs = jnp.exp2(scores - top)
            scale = jnp.exp2(before - top)
            norm = scale + jnp.sum(probs, axis=-1, keepdims=True)
            value = partial[:, out_at] * scale + jnp.dot(
                probs.astype(jnp.bfloat16),
                held[:block, value_at],
                preferred_element_type=jnp.float32,
            )
            out[block:, out_at] = (value / norm).astype(out.dtype)


def attend_blocks(arrays, parts, places, length, side, block, partial=None):
    rows = sum(a.shape[0] for a in arrays)
    columns = arrays[0].shape[1]
    wide = columns // (GQ + 2) * GQ
    scal = jnp.stack([length, side] + list(places)).astype(jnp.int32)
    hbm = pl.BlockSpec(memory_space=pltpu.HBM)
    vmem = pl.BlockSpec(memory_space=pltpu.VMEM)
    if partial is None:
        body, name = attend_near_kernel, "attend_near"
        out_shape = [
            jax.ShapeDtypeStruct((rows, wide), jnp.float32),
            jax.ShapeDtypeStruct((rows, HD), jnp.float32),
        ]
    else:
        body, name = attend_far_kernel, "attend_far"
        out_shape = [jax.ShapeDtypeStruct((rows, wide), jnp.bfloat16)]
    extra = [] if partial is None else list(partial)
    return pl.pallas_call(
        functools.partial(body, parts, block),
        out_shape=out_shape,
        in_specs=[pl.BlockSpec(memory_space=pltpu.SMEM)]
        + [hbm] * len(arrays)
        + [vmem] * len(extra),
        out_specs=[vmem] * len(out_shape),
        scratch_shapes=[
            pltpu.VMEM((rows, columns), jnp.bfloat16),
            pltpu.SemaphoreType.DMA((len(places),)),
        ],
        compiler_params=pltpu.CompilerParams(vmem_limit_bytes=SMALL_BYTES),
        cost_estimate=pl.CostEstimate(
            flops=2 * rows * rows * wide,
            bytes_accessed=2 * rows * (columns + wide),
            transcendentals=rows * rows * wide // HD // 2,
        ),
        name=name,
    )(scal, *arrays, *extra)


def after(x, *earlier):
    return lax.optimization_barrier((x,) + earlier)[0]


def four_planes(tokens, w_qkv, norm_gain, q_gain, k_gain, lengths):
    t = lax.axis_index("tensor")
    rows = tokens.shape[0]
    half = rows // 2
    columns = w_qkv.shape[1] // 4
    side = t // 2
    far_end = 3 * (1 - side)
    far_mid = 2 - side

    def slab(block):
        return lax.dynamic_slice(w_qkv, (0, block * columns), (w_qkv.shape[0], columns))

    def across(x, pairs):
        return lax.ppermute(x, "tensor", pairs)

    def exchange(x, bits):
        return across(x, [(i, i ^ bits) for i in range(4)])

    def spread(x):
        return lax.all_gather(x, "fsdp", axis=0, tiled=True)

    swap = [(1, 2), (2, 1)]
    far = [(0, 2), (3, 1)]
    outward = [(1, 0), (2, 3)]

    planes = [t] + [jnp.bitwise_xor(t, m) for m in (1, 2, 3)]
    own, out1, out2, out3 = [slab(p) for p in planes]
    normed = head_norm(tokens.astype(jnp.float32), norm_gain).astype(jnp.bfloat16)
    first, second = normed[:half], normed[half:]

    in2, in3, in1 = exchange(out2, 2), exchange(out3, 3), exchange(out1, 1)
    positions = jnp.arange(4 * rows, dtype=jnp.int32)
    angle = angles(positions)
    cos = jnp.concatenate([jnp.cos(angle)] * 2, axis=1)
    sin = jnp.concatenate([-jnp.sin(angle), jnp.sin(angle)], axis=1)
    quarter = rows // 4
    pair1 = exchange(normed[:quarter], 1)
    second_pair, third_pair = normed[quarter : quarter + half], normed[quarter + half :]
    in1, in2, in3, pair1, first, second, second_pair, third_pair, cos, sin = (
        lax.optimization_barrier(
            (in1, in2, in3, pair1, first, second, second_pair, third_pair, cos, sin)
        )
    )
    swap1 = across(first, swap)
    pair2 = exchange(second_pair, 1)
    swap2 = across(after(second, swap1, pair2), swap)
    pair3 = exchange(after(third_pair, pair2), 1)
    on1 = across(swap1, outward)
    far1 = across(after(first, swap2, pair3), far)
    on2 = across(swap2, outward)
    far2 = across(after(second, far1, on1), far)
    on3 = across(far1, outward)

    pieces = [spread(x) for x in (own, in1, in2, in3)]
    middle = jnp.where((t == 1) | (t == 2), 1, 0)
    scal = jnp.stack(planes + [jnp.int32(m) for m in range(4)] + [middle])

    gains = jnp.stack([q_gain, k_gain])

    made, parts, places = [], [], []

    tables = (cos, sin, gains)

    def run(call, vmem_bytes=VMEM_BYTES, space=pltpu.HBM):
        listed, first_row = [], 0
        for (block, _), place in call:
            listed.append((first_row, block.shape[0], len(places)))
            first_row += block.shape[0]
            places.append(place)
        parts.append(listed)
        made.append(
            project([b for b, _ in call], [p for _, p in call], pieces, scal, *tables, vmem_bytes, space)
        )

    pair_place = planes[1] * rows
    run(
        [
            ((normed, normed), t * rows),
            ((pair1, pair1), pair_place),
            ((pair2, pair2), pair_place + quarter),
            ((pair3, pair3), pair_place + quarter + half),
        ]
    )
    on4 = across(after(far2, on2, made[0]), outward)
    run([((swap1, on1), far_mid * rows), ((swap2, on2), far_mid * rows + half)])
    near_places = [place - side * rows for place in places]
    made[1] = after(made[1], on3)
    partial = attend_blocks(made, parts, near_places, lengths[0] - side * rows, side, rows)
    far1, on3, far2, on4 = [after(x, *partial) for x in (far1, on3, far2, on4)]
    run([((far1, on3), far_end * rows), ((far2, on4), far_end * rows + half)], SMALL_BYTES, pltpu.VMEM)
    return attend_blocks(made, parts, places, lengths[0], side, rows, partial)[0]


def solution(mesh):
    placed = (
        P(("groups", "fsdp", "tensor"), None),
        P(("groups", "fsdp", "tensor"), None),
        P(),
        P(),
        P(),
        P(("groups", "fsdp")),
    )
    sizes = dict(mesh.shape)
    body = four_planes if sizes["tensor"] == 4 and sizes["fsdp"] == 4 else any_mesh
    return jax.shard_map(
        body,
        mesh=mesh,
        in_specs=placed,
        out_specs=P(("groups", "fsdp"), "tensor"),
        check_vma=False,
    )
```

```python
import functools
import jax
import jax.numpy as jnp
from jax import lax
from jax.experimental import pallas as pl
from jax.experimental.pallas import tpu as pltpu
from jax.sharding import PartitionSpec as P

KV = 8
HD = 128
GQ = 4
LOG2E = 1.4426950408889634
VMEM_BYTES = 48 * 1024 * 1024
SMALL_BYTES = 20 * 1024 * 1024


def head_norm(vec, gain):
    scale = lax.rsqrt(jnp.mean(vec * vec, axis=-1, keepdims=True) + 1e-06)
    return vec * scale * gain


def angles(positions):
    half = HD // 2
    freqs = 1000000.0 ** (-2.0 * jnp.arange(half, dtype=jnp.float32) / HD)
    return positions.astype(jnp.float32)[:, None] * freqs[None, :]


def rotate(vec, positions):
    half = vec.shape[-1] // 2
    angle = angles(positions)
    cosine = jnp.cos(angle)[:, None, None, :]
    sine = jnp.sin(angle)[:, None, None, :]
    first = vec[..., :half]
    second = vec[..., half:]
    return jnp.concatenate(
        [first * cosine - second * sine, second * cosine + first * sine], axis=-1
    )


def attend(qkv, q_gain, k_gain, length):
    rows = qkv.shape[0]
    group = qkv.shape[2] - 2
    positions = jnp.arange(rows, dtype=jnp.int32)
    query = rotate(head_norm(qkv[:, :, :group], q_gain), positions).astype(jnp.bfloat16)
    keyed = rotate(head_norm(qkv[:, :, group : group + 1], k_gain), positions)[:, :, 0].astype(
        jnp.bfloat16
    )
    value = qkv[:, :, group + 1].astype(jnp.bfloat16)
    scores = jnp.einsum(
        "ikgd,jkd->kgij", query, keyed, preferred_element_type=jnp.float32
    ) / jnp.sqrt(jnp.float32(qkv.shape[3]))
    allowed = (positions[None, :] <= positions[:, None]) & (positions[None, :] < length)
    scores = jnp.where(allowed[None, None], scores, jnp.float32(-1e30))
    top = jnp.max(scores, axis=-1, keepdims=True)
    weights = jnp.exp(scores - top)
    probs = (weights / jnp.sum(weights, axis=-1, keepdims=True)).astype(jnp.bfloat16)
    out = jnp.einsum("kgij,jkd->ikgd", probs, value, preferred_element_type=jnp.float32)
    return out.reshape(rows, -1).astype(jnp.bfloat16)


def any_mesh(tokens, w_qkv, norm_gain, q_gain, k_gain, lengths):
    tensor_count = lax.axis_size("tensor")
    moved = lax.all_to_all(w_qkv, "tensor", split_axis=1, concat_axis=0, tiled=True)
    weight_cols = lax.all_gather(moved, "fsdp", axis=0, tiled=True)
    normed = head_norm(tokens.astype(jnp.float32), norm_gain).astype(jnp.bfloat16)
    qkv = jnp.dot(
        lax.all_gather(normed, "tensor", axis=0, tiled=True),
        weight_cols,
        preferred_element_type=jnp.float32,
    )
    qkv = qkv.reshape(qkv.shape[0], KV // tensor_count, GQ + 2, HD)
    return attend(qkv, q_gain, k_gain, lengths[0])


def project_kernel(counts, sources, tile, scal, *refs):
    blocks = len(counts)
    arrays = max(source[0] for source in sources) + 1
    middle_rows, end_rows = refs[:blocks], refs[blocks : 2 * blocks]
    refs = refs[2 * blocks :]
    pieces = refs[:arrays]
    cos_ref, sin_ref, gain_ref, out = refs[arrays : arrays + 4]
    taken, held, made, row_sems, sems, out_sems = refs[arrays + 4 :]
    depth = taken.shape[1] // 16
    columns = made.shape[1]
    steps = columns // tile

    def copies(step):
        listed = []
        for index, (array, first, group, slot) in enumerate(sources):
            start = pl.multiple_of((scal[group] * 4 + scal[slot]) * depth, 16)
            low = step * tile
            listed.append(
                pltpu.make_async_copy(
                    pieces[array].at[first : first + depth, low : low + tile],
                    held.at[step % 2, pl.ds(start, depth), :],
                    sems.at[step % 2, index],
                )
            )
        return listed

    starts = [sum(counts[:n]) for n in range(blocks)]
    row_copies = [
        [
            pltpu.make_async_copy(ref, taken.at[first : first + rows, :], row_sems.at[number])
            for ref in (middle_rows[number], end_rows[number])
        ]
        for number, (first, rows) in enumerate(zip(starts, counts))
    ]
    out_copies = []
    for copy in copies(0):
        copy.start()
    for in_middle, in_end in row_copies:
        pl.when(scal[8] == 1)(in_middle.start)
        pl.when(scal[8] == 0)(in_end.start)
    for step in range(steps):
        if step + 1 < steps:
            for copy in copies(step + 1):
                copy.start()
        if step == 0:
            for in_middle, _ in row_copies:
                in_middle.wait()
        for copy in copies(step):
            copy.wait()
        total = jnp.dot(taken[...], held[step % 2], preferred_element_type=jnp.float32)
        for number, (first, rows) in enumerate(zip(starts, counts)):
            place = pl.ds(pl.multiple_of(scal[9 + number], 16), rows)
            cosine = cos_ref[place, :]
            sine = sin_ref[place, :]
            for head in range(tile // HD):
                kind = (step * (tile // HD) + head) % (GQ + 2)
                vec = total[first : first + rows, head * HD : (head + 1) * HD]
                if kind <= GQ:
                    scale = lax.rsqrt(jnp.mean(vec * vec, axis=-1, keepdims=True) + 1e-06)
                    gain = gain_ref[0:1, :] if kind < GQ else gain_ref[1:2, :]
                    vec = vec * scale * gain
                    vec = vec * cosine + pltpu.roll(vec, HD // 2, 1) * sine
                at = step * tile + head * HD
                made[first : first + rows, at : at + HD] = vec.astype(made.dtype)
        at = slice(step * tile, (step + 1) * tile)
        out_copies.append(pltpu.make_async_copy(made.at[:, at], out.at[:, at], out_sems.at[step]))
        out_copies[-1].start()
    for copy in out_copies:
        copy.wait()


def project(rows_list, places, pieces, scal, cos, sin, gains, vmem_bytes, space):
    depth = rows_list[0][0].shape[1] // 16
    columns = pieces[0].shape[1]
    sources = [(n, m * depth, 4 + m, n) for n in range(4) for m in range(4)]
    counts = [r.shape[0] for r, _ in rows_list]
    steps = 3
    tile = columns // steps
    count = sum(counts)
    width = rows_list[0][0].shape[1]
    scal = jnp.concatenate([scal, jnp.stack(places)]).astype(jnp.int32)
    vmem = pl.BlockSpec(memory_space=pltpu.VMEM)
    hbm = pl.BlockSpec(memory_space=pltpu.HBM)
    return pl.pallas_call(
        functools.partial(project_kernel, counts, sources, tile),
        out_shape=space((count, columns), jnp.bfloat16),
        in_specs=[pl.BlockSpec(memory_space=pltpu.SMEM)]
        + [hbm] * (2 * len(counts) + len(pieces))
        + [vmem] * 3,
        out_specs=pl.BlockSpec(memory_space=space),
        scratch_shapes=[
            pltpu.VMEM((count, width), jnp.bfloat16),
            pltpu.VMEM((2, width, tile), jnp.bfloat16),
            pltpu.VMEM((count, columns), jnp.bfloat16),
            pltpu.SemaphoreType.DMA((len(counts),)),
            pltpu.SemaphoreType.DMA((2, 16)),
            pltpu.SemaphoreType.DMA((steps,)),
        ],
        compiler_params=pltpu.CompilerParams(vmem_limit_bytes=vmem_bytes),
        cost_estimate=pl.CostEstimate(
            flops=2 * count * width * columns,
            bytes_accessed=2 * (width * columns + count * (width + columns)),
            transcendentals=0,
        ),
        name="project",
    )(scal, *[r for r, _ in rows_list], *[r for _, r in rows_list], *pieces, cos, sin, gains)


FACTOR = LOG2E / float(HD) ** 0.5
CONTRACT = (((1,), (1,)), ((), ()))


def fetch_blocks(refs, parts, places, held, sems):
    copies = []
    for ref, blocks in zip(refs, parts):
        for first, rows, number in blocks:
            place = pl.ds(pl.multiple_of(places(number), 16), rows)
            copies.append(
                pltpu.make_async_copy(
                    ref.at[first : first + rows, :], held.at[place, :], sems.at[number]
                )
            )
    for copy in copies:
        copy.start()
    for copy in copies:
        copy.wait()


def head_columns(head):
    base = head // GQ * (GQ + 2) * HD
    query = base + head % GQ * HD
    key = base + GQ * HD
    return (
        slice(query, query + HD),
        slice(key, key + HD),
        slice(key + HD, key + 2 * HD),
        slice(head * HD, (head + 1) * HD),
    )


def attend_rows(own, at, rest, head, position, length):
    query_at, key_at, value_at, _ = head_columns(head)
    block = at.stop - at.start
    row = lax.broadcasted_iota(jnp.int32, (block, block), 0)
    col = lax.broadcasted_iota(jnp.int32, (block, block), 1)
    query = own[at, query_at]
    last = lax.dot_general(query, own[at, key_at], CONTRACT, preferred_element_type=jnp.float32)
    last = jnp.where((col <= row) & (col + position < length), last, -1e30)
    top = jnp.max(last, axis=-1, keepdims=True)
    if position:
        before = lax.dot_general(
            query, rest[:position, key_at], CONTRACT, preferred_element_type=jnp.float32
        )
        keys = lax.broadcasted_iota(jnp.int32, (1, position), 1)
        before = before + jnp.where(keys < length, 0.0, -1e30)
        top = jnp.maximum(top, jnp.max(before, axis=-1, keepdims=True))
    probs = jnp.exp2((last - top) * FACTOR)
    norm = jnp.sum(probs, axis=-1, keepdims=True)
    value = jnp.dot(
        probs.astype(jnp.bfloat16), own[at, value_at], preferred_element_type=jnp.float32
    )
    if position:
        probs = jnp.exp2((before - top) * FACTOR)
        norm = norm + jnp.sum(probs, axis=-1, keepdims=True)
        value = value + jnp.dot(
            probs.astype(jnp.bfloat16),
            rest[:position, value_at],
            preferred_element_type=jnp.float32,
        )
    return top, norm, value


def attend_near_kernel(parts, block, scal, *refs):
    partial, stats, held, sems = refs[len(parts) :]
    fetch_blocks(refs, parts, lambda number: scal[1 + number], held, sems)
    for head in range(partial.shape[1] // HD):
        out_at = head_columns(head)[3]
        for low in range(0, held.shape[0], block):
            at = slice(low, low + block)
            top, norm, value = attend_rows(held, at, held, head, low, scal[0])
            partial[at, out_at] = value / norm
            stats[at, head : head + 1] = top * FACTOR + jnp.log(norm) * LOG2E


def attend_far_kernel(scal, far, held, partial, stats, out):
    heads = out.shape[1] // HD
    block = far.shape[0]
    low = held.shape[0]
    whole = slice(0, block)
    length = scal[0]

    @pl.when(scal[1] == 0)
    def _():
        for head in range(heads):
            out_at = head_columns(head)[3]
            _, norm, value = attend_rows(far, whole, held, head, low, length)
            out[low:, out_at] = (value / norm).astype(out.dtype)
        out[:low, :] = partial[...].astype(out.dtype)

    @pl.when(scal[1] == 1)
    def _():
        for head in range(heads):
            query_at, key_at, value_at, out_at = head_columns(head)
            _, norm, value = attend_rows(far, whole, far, head, 0, length)
            out[:block, out_at] = (value / norm).astype(out.dtype)
            scores = lax.dot_general(
                held[:, query_at], far[:, key_at], CONTRACT, preferred_element_type=jnp.float32
            )
            keys = lax.broadcasted_iota(jnp.int32, (1, block), 1)
            scores = scores * FACTOR + jnp.where(keys < length, 0.0, -1e30)
            before = stats[:, head : head + 1]
            top = jnp.maximum(before, jnp.max(scores, axis=-1, keepdims=True))
            probs = jnp.exp2(scores - top)
            scale = jnp.exp2(before - top)
            norm = scale + jnp.sum(probs, axis=-1, keepdims=True)
            value = partial[:, out_at] * scale + jnp.dot(
                probs.astype(jnp.bfloat16), far[:, value_at], preferred_element_type=jnp.float32
            )
            out[block:, out_at] = (value / norm).astype(out.dtype)


def attend_cost(rows, wide):
    return pl.CostEstimate(
        flops=2 * rows * rows * wide,
        bytes_accessed=4 * rows * wide,
        transcendentals=rows * rows * wide // HD // 2,
    )


def attend_near(arrays, parts, places, length, block):
    rows = sum(a.shape[0] for a in arrays)
    columns = arrays[0].shape[1]
    wide = columns // (GQ + 2) * GQ
    scal = jnp.stack([length] + list(places)).astype(jnp.int32)
    vmem = pl.BlockSpec(memory_space=pltpu.VMEM)
    return pl.pallas_call(
        functools.partial(attend_near_kernel, parts, block),
        out_shape=[
            jax.ShapeDtypeStruct((rows, wide), jnp.float32),
            jax.ShapeDtypeStruct((rows, HD), jnp.float32),
            jax.ShapeDtypeStruct((rows, columns), jnp.bfloat16),
        ],
        in_specs=[pl.BlockSpec(memory_space=pltpu.SMEM)]
        + [pl.BlockSpec(memory_space=pltpu.HBM)] * len(arrays),
        out_specs=[vmem] * 3,
        scratch_shapes=[pltpu.SemaphoreType.DMA((len(places),))],
        compiler_params=pltpu.CompilerParams(vmem_limit_bytes=SMALL_BYTES),
        cost_estimate=attend_cost(rows, wide),
        name="attend_near",
    )(scal, *arrays)


def attend_far(far, near, length, side):
    partial, stats, held = near
    rows = far.shape[0] + held.shape[0]
    wide = partial.shape[1]
    vmem = pl.BlockSpec(memory_space=pltpu.VMEM)
    return pl.pallas_call(
        attend_far_kernel,
        out_shape=jax.ShapeDtypeStruct((rows, wide), jnp.bfloat16),
        in_specs=[pl.BlockSpec(memory_space=pltpu.SMEM)] + [vmem] * 4,
        out_specs=vmem,
        compiler_params=pltpu.CompilerParams(vmem_limit_bytes=SMALL_BYTES),
        cost_estimate=attend_cost(rows, wide),
        name="attend_far",
    )(jnp.stack([length, side]).astype(jnp.int32), far, held, partial, stats)


def after(x, *earlier):
    return lax.optimization_barrier((x,) + earlier)[0]


def four_planes(tokens, w_qkv, norm_gain, q_gain, k_gain, lengths):
    t = lax.axis_index("tensor")
    rows = tokens.shape[0]
    half = rows // 2
    columns = w_qkv.shape[1] // 4
    side = t // 2
    far_end = 3 * (1 - side)
    far_mid = 2 - side

    def slab(block):
        return lax.dynamic_slice(w_qkv, (0, block * columns), (w_qkv.shape[0], columns))

    def across(x, pairs):
        return lax.ppermute(x, "tensor", pairs)

    def exchange(x, bits):
        return across(x, [(i, i ^ bits) for i in range(4)])

    def spread(x):
        return lax.all_gather(x, "fsdp", axis=0, tiled=True)

    swap = [(1, 2), (2, 1)]
    far = [(0, 2), (3, 1)]
    outward = [(1, 0), (2, 3)]

    planes = [t] + [jnp.bitwise_xor(t, m) for m in (1, 2, 3)]
    own, out1, out2, out3 = [slab(p) for p in planes]
    normed = head_norm(tokens.astype(jnp.float32), norm_gain).astype(jnp.bfloat16)
    first, second = normed[:half], normed[half:]

    in2, in3, in1 = exchange(out2, 2), exchange(out3, 3), exchange(out1, 1)
    positions = jnp.arange(4 * rows, dtype=jnp.int32)
    angle = angles(positions)
    cos = jnp.concatenate([jnp.cos(angle)] * 2, axis=1)
    sin = jnp.concatenate([-jnp.sin(angle), jnp.sin(angle)], axis=1)
    quarter = rows // 4
    pair1 = exchange(normed[:quarter], 1)
    second_pair, third_pair = normed[quarter : quarter + half], normed[quarter + half :]
    in1, in2, in3, pair1, first, second, second_pair, third_pair, cos, sin = (
        lax.optimization_barrier(
            (in1, in2, in3, pair1, first, second, second_pair, third_pair, cos, sin)
        )
    )
    swap1 = across(first, swap)
    pair2 = exchange(second_pair, 1)
    swap2 = across(after(second, swap1, pair2), swap)
    pair3 = exchange(after(third_pair, pair2), 1)
    on1 = across(swap1, outward)
    far1 = across(after(first, swap2, pair3), far)
    on2 = across(swap2, outward)
    far2 = across(after(second, far1, on1), far)
    on3 = across(far1, outward)

    pieces = [spread(x) for x in (own, in1, in2, in3)]
    middle = jnp.where((t == 1) | (t == 2), 1, 0)
    scal = jnp.stack(planes + [jnp.int32(m) for m in range(4)] + [middle])

    gains = jnp.stack([q_gain, k_gain])

    made, parts, places = [], [], []

    tables = (cos, sin, gains)

    def run(call, vmem_bytes=VMEM_BYTES, space=pltpu.HBM):
        listed, first_row = [], 0
        for (block, _), place in call:
            listed.append((first_row, block.shape[0], len(places)))
            first_row += block.shape[0]
            places.append(place)
        parts.append(listed)
        made.append(
            project([b for b, _ in call], [p for _, p in call], pieces, scal, *tables, vmem_bytes, space)
        )

    pair_place = planes[1] * rows
    run(
        [
            ((normed, normed), t * rows),
            ((pair1, pair1), pair_place),
            ((pair2, pair2), pair_place + quarter),
            ((pair3, pair3), pair_place + quarter + half),
        ]
    )
    on4 = across(after(far2, on2, made[0]), outward)
    run([((swap1, on1), far_mid * rows), ((swap2, on2), far_mid * rows + half)])
    near_places = [place - side * rows for place in places]
    made[1] = after(made[1], on3)
    partial = attend_near(made, parts, near_places, lengths[0] - side * rows, rows)
    far1, on3, far2, on4 = [after(x, *partial) for x in (far1, on3, far2, on4)]
    run([((far1, on3), far_end * rows), ((far2, on4), far_end * rows + half)], SMALL_BYTES, pltpu.VMEM)
    return attend_far(made[-1], partial, lengths[0], side)


def solution(mesh):
    placed = (
        P(("groups", "fsdp", "tensor"), None),
        P(("groups", "fsdp", "tensor"), None),
        P(),
        P(),
        P(),
        P(("groups", "fsdp")),
    )
    sizes = dict(mesh.shape)
    body = four_planes if sizes["tensor"] == 4 and sizes["fsdp"] == 4 else any_mesh
    return jax.shard_map(
        body,
        mesh=mesh,
        in_specs=placed,
        out_specs=P(("groups", "fsdp"), "tensor"),
        check_vma=False,
    )
```

```python
import functools
import jax
import jax.numpy as jnp
from jax import lax
from jax.experimental import pallas as pl
from jax.experimental.pallas import tpu as pltpu
from jax.sharding import PartitionSpec as P

KV = 8
HD = 128
GQ = 4
LOG2E = 1.4426950408889634
VMEM_BYTES = 48 * 1024 * 1024
SMALL_BYTES = 20 * 1024 * 1024


def head_norm(vec, gain):
    scale = lax.rsqrt(jnp.mean(vec * vec, axis=-1, keepdims=True) + 1e-06)
    return vec * scale * gain


def angles(positions):
    half = HD // 2
    freqs = 1000000.0 ** (-2.0 * jnp.arange(half, dtype=jnp.float32) / HD)
    return positions.astype(jnp.float32)[:, None] * freqs[None, :]


def rotate(vec, positions):
    half = vec.shape[-1] // 2
    angle = angles(positions)
    cosine = jnp.cos(angle)[:, None, None, :]
    sine = jnp.sin(angle)[:, None, None, :]
    first = vec[..., :half]
    second = vec[..., half:]
    return jnp.concatenate(
        [first * cosine - second * sine, second * cosine + first * sine], axis=-1
    )


def attend(qkv, q_gain, k_gain, length):
    rows = qkv.shape[0]
    group = qkv.shape[2] - 2
    positions = jnp.arange(rows, dtype=jnp.int32)
    query = rotate(head_norm(qkv[:, :, :group], q_gain), positions).astype(jnp.bfloat16)
    keyed = rotate(head_norm(qkv[:, :, group : group + 1], k_gain), positions)[:, :, 0].astype(
        jnp.bfloat16
    )
    value = qkv[:, :, group + 1].astype(jnp.bfloat16)
    scores = jnp.einsum(
        "ikgd,jkd->kgij", query, keyed, preferred_element_type=jnp.float32
    ) / jnp.sqrt(jnp.float32(qkv.shape[3]))
    allowed = (positions[None, :] <= positions[:, None]) & (positions[None, :] < length)
    scores = jnp.where(allowed[None, None], scores, jnp.float32(-1e30))
    top = jnp.max(scores, axis=-1, keepdims=True)
    weights = jnp.exp(scores - top)
    probs = (weights / jnp.sum(weights, axis=-1, keepdims=True)).astype(jnp.bfloat16)
    out = jnp.einsum("kgij,jkd->ikgd", probs, value, preferred_element_type=jnp.float32)
    return out.reshape(rows, -1).astype(jnp.bfloat16)


def any_mesh(tokens, w_qkv, norm_gain, q_gain, k_gain, lengths):
    tensor_count = lax.axis_size("tensor")
    moved = lax.all_to_all(w_qkv, "tensor", split_axis=1, concat_axis=0, tiled=True)
    weight_cols = lax.all_gather(moved, "fsdp", axis=0, tiled=True)
    normed = head_norm(tokens.astype(jnp.float32), norm_gain).astype(jnp.bfloat16)
    qkv = jnp.dot(
        lax.all_gather(normed, "tensor", axis=0, tiled=True),
        weight_cols,
        preferred_element_type=jnp.float32,
    )
    qkv = qkv.reshape(qkv.shape[0], KV // tensor_count, GQ + 2, HD)
    return attend(qkv, q_gain, k_gain, lengths[0])


def project_kernel(counts, sources, tile, scal, *refs):
    blocks = len(counts)
    arrays = max(source[0] for source in sources) + 1
    middle_rows, end_rows = refs[:blocks], refs[blocks : 2 * blocks]
    refs = refs[2 * blocks :]
    pieces = refs[:arrays]
    cos_ref, sin_ref, gain_ref, out = refs[arrays : arrays + 4]
    taken, held, made, row_sems, sems, out_sems = refs[arrays + 4 :]
    depth = taken.shape[1] // 16
    columns = made.shape[1]
    steps = columns // tile

    def copies(step):
        listed = []
        for index, (array, first, group, slot) in enumerate(sources):
            start = pl.multiple_of((scal[group] * 4 + scal[slot]) * depth, 16)
            low = step * tile
            listed.append(
                pltpu.make_async_copy(
                    pieces[array].at[first : first + depth, low : low + tile],
                    held.at[step % 2, pl.ds(start, depth), :],
                    sems.at[step % 2, index],
                )
            )
        return listed

    starts = [sum(counts[:n]) for n in range(blocks)]
    row_copies = [
        [
            pltpu.make_async_copy(ref, taken.at[first : first + rows, :], row_sems.at[number])
            for ref in (middle_rows[number], end_rows[number])
        ]
        for number, (first, rows) in enumerate(zip(starts, counts))
    ]
    out_copies = []
    for copy in copies(0):
        copy.start()
    for in_middle, in_end in row_copies:
        pl.when(scal[8] == 1)(in_middle.start)
        pl.when(scal[8] == 0)(in_end.start)
    for step in range(steps):
        if step + 1 < steps:
            for copy in copies(step + 1):
                copy.start()
        if step == 0:
            for in_middle, _ in row_copies:
                in_middle.wait()
        for copy in copies(step):
            copy.wait()
        total = jnp.dot(taken[...], held[step % 2], preferred_element_type=jnp.float32)
        for number, (first, rows) in enumerate(zip(starts, counts)):
            place = pl.ds(pl.multiple_of(scal[9 + number], 16), rows)
            cosine = cos_ref[place, :]
            sine = sin_ref[place, :]
            for head in range(tile // HD):
                kind = (step * (tile // HD) + head) % (GQ + 2)
                vec = total[first : first + rows, head * HD : (head + 1) * HD]
                if kind <= GQ:
                    scale = lax.rsqrt(jnp.mean(vec * vec, axis=-1, keepdims=True) + 1e-06)
                    gain = gain_ref[0:1, :] if kind < GQ else gain_ref[1:2, :]
                    vec = vec * scale * gain
                    vec = vec * cosine + pltpu.roll(vec, HD // 2, 1) * sine
                at = step * tile + head * HD
                made[first : first + rows, at : at + HD] = vec.astype(made.dtype)
        at = slice(step * tile, (step + 1) * tile)
        out_copies.append(pltpu.make_async_copy(made.at[:, at], out.at[:, at], out_sems.at[step]))
        out_copies[-1].start()
    for copy in out_copies:
        copy.wait()


def project(rows_list, places, pieces, scal, cos, sin, gains, vmem_bytes, space):
    depth = rows_list[0][0].shape[1] // 16
    columns = pieces[0].shape[1]
    sources = [(n, m * depth, 4 + m, n) for n in range(4) for m in range(4)]
    counts = [r.shape[0] for r, _ in rows_list]
    steps = 3
    tile = columns // steps
    count = sum(counts)
    width = rows_list[0][0].shape[1]
    scal = jnp.concatenate([scal, jnp.stack(places)]).astype(jnp.int32)
    vmem = pl.BlockSpec(memory_space=pltpu.VMEM)
    hbm = pl.BlockSpec(memory_space=pltpu.HBM)
    return pl.pallas_call(
        functools.partial(project_kernel, counts, sources, tile),
        out_shape=space((count, columns), jnp.bfloat16),
        in_specs=[pl.BlockSpec(memory_space=pltpu.SMEM)]
        + [hbm] * (2 * len(counts) + len(pieces))
        + [vmem] * 3,
        out_specs=pl.BlockSpec(memory_space=space),
        scratch_shapes=[
            pltpu.VMEM((count, width), jnp.bfloat16),
            pltpu.VMEM((2, width, tile), jnp.bfloat16),
            pltpu.VMEM((count, columns), jnp.bfloat16),
            pltpu.SemaphoreType.DMA((len(counts),)),
            pltpu.SemaphoreType.DMA((2, 16)),
            pltpu.SemaphoreType.DMA((steps,)),
        ],
        compiler_params=pltpu.CompilerParams(vmem_limit_bytes=vmem_bytes),
        cost_estimate=pl.CostEstimate(
            flops=2 * count * width * columns,
            bytes_accessed=2 * (width * columns + count * (width + columns)),
            transcendentals=0,
        ),
        name="project",
    )(scal, *[r for r, _ in rows_list], *[r for _, r in rows_list], *pieces, cos, sin, gains)


FACTOR = LOG2E / float(HD) ** 0.5
CONTRACT = (((1,), (1,)), ((), ()))


def fetch_blocks(refs, parts, places, held, sems):
    copies = []
    for ref, blocks in zip(refs, parts):
        for first, rows, number in blocks:
            place = pl.ds(pl.multiple_of(places(number), 16), rows)
            copies.append(
                pltpu.make_async_copy(
                    ref.at[first : first + rows, :], held.at[place, :], sems.at[number]
                )
            )
    for copy in copies:
        copy.start()
    for copy in copies:
        copy.wait()


def head_columns(head):
    base = head // GQ * (GQ + 2) * HD
    query = base + head % GQ * HD
    key = base + GQ * HD
    return (
        slice(query, query + HD),
        slice(key, key + HD),
        slice(key + HD, key + 2 * HD),
        slice(head * HD, (head + 1) * HD),
    )


def attend_rows(own, at, rest, head, position, length):
    query_at, key_at, value_at, _ = head_columns(head)
    block = at.stop - at.start
    row = lax.broadcasted_iota(jnp.int32, (block, block), 0)
    col = lax.broadcasted_iota(jnp.int32, (block, block), 1)
    query = own[at, query_at]
    last = lax.dot_general(query, own[at, key_at], CONTRACT, preferred_element_type=jnp.float32)
    last = jnp.where((col <= row) & (col + position < length), last, -1e30)
    top = jnp.max(last, axis=-1, keepdims=True)
    if position:
        before = lax.dot_general(
            query, rest[:position, key_at], CONTRACT, preferred_element_type=jnp.float32
        )
        keys = lax.broadcasted_iota(jnp.int32, (1, position), 1)
        before = before + jnp.where(keys < length, 0.0, -1e30)
        top = jnp.maximum(top, jnp.max(before, axis=-1, keepdims=True))
    probs = jnp.exp2((last - top) * FACTOR)
    norm = jnp.sum(probs, axis=-1, keepdims=True)
    value = jnp.dot(
        probs.astype(jnp.bfloat16), own[at, value_at], preferred_element_type=jnp.float32
    )
    if position:
        probs = jnp.exp2((before - top) * FACTOR)
        norm = norm + jnp.sum(probs, axis=-1, keepdims=True)
        value = value + jnp.dot(
            probs.astype(jnp.bfloat16),
            rest[:position, value_at],
            preferred_element_type=jnp.float32,
        )
    return top, norm, value


def attend_near_kernel(parts, block, scal, *refs):
    partial, stats, held, sems = refs[len(parts) :]
    fetch_blocks(refs, parts, lambda number: scal[1 + number], held, sems)
    for head in range(partial.shape[1] // HD):
        out_at = head_columns(head)[3]
        for low in range(0, held.shape[0], block):
            at = slice(low, low + block)
            top, norm, value = attend_rows(held, at, held, head, low, scal[0])
            partial[at, out_at] = value / norm
            stats[at, head : head + 1] = top * FACTOR + jnp.log(norm) * LOG2E


def attend_far_kernel(scal, far, held, partial, stats, out):
    heads = out.shape[1] // HD
    block = far.shape[0]
    low = held.shape[0]
    whole = slice(0, block)
    length = scal[0]

    @pl.when(scal[1] == 0)
    def _():
        for head in range(heads):
            out_at = head_columns(head)[3]
            _, norm, value = attend_rows(far, whole, held, head, low, length)
            out[low:, out_at] = (value / norm).astype(out.dtype)
        out[:low, :] = partial[...].astype(out.dtype)

    @pl.when(scal[1] == 1)
    def _():
        for head in range(heads):
            query_at, key_at, value_at, out_at = head_columns(head)
            _, norm, value = attend_rows(far, whole, far, head, 0, length)
            out[:block, out_at] = (value / norm).astype(out.dtype)
            scores = lax.dot_general(
                held[:, query_at], far[:, key_at], CONTRACT, preferred_element_type=jnp.float32
            )
            keys = lax.broadcasted_iota(jnp.int32, (1, block), 1)
            scores = scores * FACTOR + jnp.where(keys < length, 0.0, -1e30)
            before = stats[:, head : head + 1]
            top = jnp.maximum(before, jnp.max(scores, axis=-1, keepdims=True))
            probs = jnp.exp2(scores - top)
            scale = jnp.exp2(before - top)
            norm = scale + jnp.sum(probs, axis=-1, keepdims=True)
            value = partial[:, out_at] * scale + jnp.dot(
                probs.astype(jnp.bfloat16), far[:, value_at], preferred_element_type=jnp.float32
            )
            out[block:, out_at] = (value / norm).astype(out.dtype)


def attend_cost(rows, wide):
    return pl.CostEstimate(
        flops=2 * rows * rows * wide,
        bytes_accessed=4 * rows * wide,
        transcendentals=rows * rows * wide // HD // 2,
    )


def attend_near(arrays, parts, places, length, block):
    rows = sum(a.shape[0] for a in arrays)
    columns = arrays[0].shape[1]
    wide = columns // (GQ + 2) * GQ
    scal = jnp.stack([length] + list(places)).astype(jnp.int32)
    vmem = pl.BlockSpec(memory_space=pltpu.VMEM)
    return pl.pallas_call(
        functools.partial(attend_near_kernel, parts, block),
        out_shape=[
            jax.ShapeDtypeStruct((rows, wide), jnp.float32),
            jax.ShapeDtypeStruct((rows, HD), jnp.float32),
            jax.ShapeDtypeStruct((rows, columns), jnp.bfloat16),
        ],
        in_specs=[pl.BlockSpec(memory_space=pltpu.SMEM)]
        + [pl.BlockSpec(memory_space=pltpu.HBM)] * len(arrays),
        out_specs=[vmem] * 3,
        scratch_shapes=[pltpu.SemaphoreType.DMA((len(places),))],
        compiler_params=pltpu.CompilerParams(vmem_limit_bytes=SMALL_BYTES),
        cost_estimate=attend_cost(rows, wide),
        name="attend_near",
    )(scal, *arrays)


def attend_far(far, near, length, side):
    partial, stats, held = near
    rows = far.shape[0] + held.shape[0]
    wide = partial.shape[1]
    vmem = pl.BlockSpec(memory_space=pltpu.VMEM)
    return pl.pallas_call(
        attend_far_kernel,
        out_shape=jax.ShapeDtypeStruct((rows, wide), jnp.bfloat16),
        in_specs=[pl.BlockSpec(memory_space=pltpu.SMEM)] + [vmem] * 4,
        out_specs=vmem,
        compiler_params=pltpu.CompilerParams(vmem_limit_bytes=SMALL_BYTES),
        cost_estimate=attend_cost(rows, wide),
        name="attend_far",
    )(jnp.stack([length, side]).astype(jnp.int32), far, held, partial, stats)


def after(x, *earlier):
    return lax.optimization_barrier((x,) + earlier)[0]


def four_planes(tokens, w_qkv, norm_gain, q_gain, k_gain, lengths):
    t = lax.axis_index("tensor")
    rows = tokens.shape[0]
    half = rows // 2
    columns = w_qkv.shape[1] // 4
    side = t // 2
    far_end = 3 * (1 - side)
    far_mid = 2 - side

    def slab(block):
        return lax.dynamic_slice(w_qkv, (0, block * columns), (w_qkv.shape[0], columns))

    def across(x, pairs):
        return lax.ppermute(x, "tensor", pairs)

    def exchange(x, bits):
        return across(x, [(i, i ^ bits) for i in range(4)])

    def spread(x):
        return lax.all_gather(x, "fsdp", axis=0, tiled=True)

    swap = [(1, 2), (2, 1)]
    far = [(0, 2), (3, 1)]
    outward = [(1, 0), (2, 3)]

    planes = [t] + [jnp.bitwise_xor(t, m) for m in (1, 2, 3)]
    out2 = slab(planes[2])
    w_qkv = after(w_qkv, out2)
    own, out1, out3 = [slab(p) for p in (planes[0], planes[1], planes[3])]
    tokens = after(tokens, out1)
    normed = head_norm(tokens.astype(jnp.float32), norm_gain).astype(jnp.bfloat16)
    first, second = normed[:half], normed[half:]

    in2, in3, in1 = exchange(out2, 2), exchange(out3, 3), exchange(out1, 1)
    positions = jnp.arange(4 * rows, dtype=jnp.int32)
    angle = angles(positions)
    cos = jnp.concatenate([jnp.cos(angle)] * 2, axis=1)
    sin = jnp.concatenate([-jnp.sin(angle), jnp.sin(angle)], axis=1)
    quarter = rows // 4
    pair1 = exchange(normed[:quarter], 1)
    second_pair, third_pair = normed[quarter : quarter + half], normed[quarter + half :]
    in1, in2, in3, pair1, first, second, second_pair, third_pair, cos, sin = (
        lax.optimization_barrier(
            (in1, in2, in3, pair1, first, second, second_pair, third_pair, cos, sin)
        )
    )
    swap1 = across(first, swap)
    pair2 = exchange(second_pair, 1)
    swap2 = across(after(second, swap1, pair2), swap)
    pair3 = exchange(after(third_pair, pair2), 1)
    on1 = across(swap1, outward)
    far1 = across(after(first, swap2, pair3), far)
    on2 = across(swap2, outward)
    far2 = across(after(second, far1, on1), far)
    on3 = across(far1, outward)

    pieces = [spread(x) for x in (own, in1, in2, in3)]
    middle = jnp.where((t == 1) | (t == 2), 1, 0)
    scal = jnp.stack(planes + [jnp.int32(m) for m in range(4)] + [middle])

    gains = jnp.stack([q_gain, k_gain])

    made, parts, places = [], [], []

    tables = (cos, sin, gains)

    def run(call, vmem_bytes=VMEM_BYTES, space=pltpu.HBM):
        listed, first_row = [], 0
        for (block, _), place in call:
            listed.append((first_row, block.shape[0], len(places)))
            first_row += block.shape[0]
            places.append(place)
        parts.append(listed)
        made.append(
            project([b for b, _ in call], [p for _, p in call], pieces, scal, *tables, vmem_bytes, space)
        )

    pair_place = planes[1] * rows
    run(
        [
            ((normed, normed), t * rows),
            ((pair1, pair1), pair_place),
            ((pair2, pair2), pair_place + quarter),
            ((pair3, pair3), pair_place + quarter + half),
        ]
    )
    on4 = across(after(far2, on2, made[0]), outward)
    run([((swap1, on1), far_mid * rows), ((swap2, on2), far_mid * rows + half)])
    near_places = [place - side * rows for place in places]
    made[1] = after(made[1], on3)
    partial = attend_near(made, parts, near_places, lengths[0] - side * rows, rows)
    far1, on3, far2, on4 = [after(x, *partial) for x in (far1, on3, far2, on4)]
    run([((far1, on3), far_end * rows), ((far2, on4), far_end * rows + half)], SMALL_BYTES, pltpu.VMEM)
    return attend_far(made[-1], partial, lengths[0], side)


def solution(mesh):
    placed = (
        P(("groups", "fsdp", "tensor"), None),
        P(("groups", "fsdp", "tensor"), None),
        P(),
        P(),
        P(),
        P(("groups", "fsdp")),
    )
    sizes = dict(mesh.shape)
    body = four_planes if sizes["tensor"] == 4 and sizes["fsdp"] == 4 else any_mesh
    return jax.shard_map(
        body,
        mesh=mesh,
        in_specs=placed,
        out_specs=P(("groups", "fsdp"), "tensor"),
        check_vma=False,
    )
```
